128 devices in a mesh: gx: 16 (over x, z), gy: 8 (over y, core).
Axes of the slice: x: 4, y: 4, z: 4, core: 2. Of those that a mesh axis runs over, the one named last changes fastest.
Arguments:
- values: float32 [16, 524288], P(None, ('gx', 'gy')), may hold values from -6 to 6
- coords: float32 [3, 524288], P(None, ('gx', 'gy')), may hold values from 0 to 1
- order: int32 [524288], P(('gx', 'gy')), may hold values from 0 to 4095, as said below
- leaf_basis: float32 [8192, 4096], P(('gx', 'gy')), may hold values from -0.75 to 0.75
- leaf_transfer: float32 [8192, 4096], P(('gx', 'gy')), may hold values from -0.5 to 0.5
- middle_transfer: float32 [1024, 4096], P(('gx', 'gy')), may hold values from -0.5 to 0.5
- root_transfer: float32 [128, 4096], P(('gx', 'gy')), may hold values from -0.5 to 0.5
- leaf_skeleton: float32 [8192, 192], P(('gx', 'gy')), may hold values from 0 to 1
- middle_skeleton: float32 [1024, 192], P(('gx', 'gy')), may hold values from 0 to 1
- root_skeleton: float32 [128, 192], P(('gx', 'gy')), may hold values from 0 to 1
- top_skeleton: float32 [16, 192], replicated, may hold values from 0 to 1
- leaf_far: int32 [8192, 64], P(('gx', 'gy')), may hold values from 0 to 1023
- middle_far: int32 [1024, 64], P(('gx', 'gy')), may hold values from 0 to 255
- root_far: int32 [128, 64], P(('gx', 'gy')), may hold values from 0 to 127
- leaf_near: int32 [8192, 26], P(('gx', 'gy')), may hold values from 0 to 79
- leaf_sends: int32 [131072], P(('gx', 'gy')), may hold values from 0 to 63
- middle_sends: int32 [32768], P(('gx', 'gy')), may hold values from 0 to 7
Outputs:
- product: float32 [16, 524288], P(None, ('gx', 'gy'))
The draws below stay inside these ranges and needn't reach their ends.
Inputs may be any that keep to these rules, and one draw needn't show every extreme that they name: `order`: each consecutive block of 4096 entries is a permutation of 0 to 4095.
All inputs are finite; a program needn't handle non-finite values.
Results may differ from the reference program's by a relative error of at most 0.00012.
Values sent between devices are 32-bit elements; how exact they have to be, the bound alone decides.
No kernel may reach another device: no remote copies, remote signals or barrier semaphores. Data moves between devices by JAX's collectives and lax.ppermute only.
A program may use at most 192 MiB of HBM per device.

```python
import math
import jax
import jax.numpy as jnp
from jax import lax

LEAF = 64
RANK = 64
RHS = 16
FAR = 64
NEAR = 26
ROOT_DEV = 1
LEAF_DEV = 64
PTS_DEV = 4096
HALO = 8
TOPS = 16
ROOTS = 128
MIDDLES = 1024
LEAVES = 8192
POINTS = 524288
SLOTS_LEAF = 1024
SLOTS_MID = 256
N_GX = 16
N_GY = 8


def draw_order(key, part):
    key = jax.random.fold_in(key, 11)
    blocks = POINTS // PTS_DEV
    keys = jax.random.split(key, blocks)
    shuffled = jax.vmap(lambda single: jax.random.permutation(single, PTS_DEV))(keys)
    return shuffled.astype(jnp.int32).reshape(POINTS).astype(jnp.int32)


def place_ends(drawn, stream_key, smallest, largest):
    spot = [jax.random.randint(jax.random.fold_in(stream_key, axis), (), 0, length) for axis, length in enumerate(drawn.shape)]
    longest = drawn.shape.index(max(drawn.shape))
    neighbour = spot[:longest] + [(spot[longest] + 1) % drawn.shape[longest]] + spot[longest + 1:]
    return drawn.at[tuple(spot)].set(smallest).at[tuple(neighbour)].set(largest)


def block_levels(key, dims, pieces, low, top_value):
    loudness = 1.0
    for dim, shards_of in pieces:
        steps = jax.random.uniform(jax.random.fold_in(jax.random.fold_in(key, 6), dim), (shards_of,), jnp.float32, low / len(pieces), top_value / len(pieces))
        loudness = loudness * jnp.repeat(jnp.exp(steps), dims[dim] // shards_of).reshape((-1,) + (1,) * (len(dims) - 1 - dim))
    return loudness


def normal_values(key, shape, deviation, reach, shards=(), kind=jnp.bfloat16):
    gain = block_levels(key, shape, shards, -0.22, 0.18) if shards else 1.0
    array = jax.random.normal(key, shape, jnp.float32) * deviation * gain
    return jnp.minimum(jnp.maximum(array, -reach), reach).astype(kind)


def setup_inputs(seed: int = 0) -> dict:
    key_list = jax.random.split(jax.random.key(seed), 18)
    values = normal_values(key_list[0], (RHS, POINTS), 1.0, 6.0, ((1, 128),), jnp.float32)
    coords = jnp.clip(1.0 * jax.random.uniform(key_list[1], (3, POINTS), jnp.float32) ** block_levels(key_list[1], (3, POINTS), ((1, 128),), -0.2, 0.2), 0.0, 1.0)
    order = draw_order(jax.random.fold_in(key_list[17], 71), 0)
    leaf_basis = normal_values(key_list[3], (LEAVES, LEAF * RANK), LEAF ** -0.5, 0.75, ((0, 128),), jnp.float32)
    leaf_transfer = normal_values(key_list[4], (LEAVES, RANK * RANK), (2 * RANK) ** -0.5, 0.5, ((0, 128),), jnp.float32)
    middle_transfer = normal_values(key_list[5], (MIDDLES, RANK * RANK), (2 * RANK) ** -0.5, 0.5, ((0, 128),), jnp.float32)
    root_transfer = normal_values(key_list[6], (ROOTS, RANK * RANK), (2 * RANK) ** -0.5, 0.5, ((0, 128),), jnp.float32)
    leaf_skeleton = jnp.clip(1.0 * jax.random.uniform(key_list[7], (LEAVES, 3 * RANK), jnp.float32) ** block_levels(key_list[7], (LEAVES, 3 * RANK), ((0, 128),), -0.2, 0.2), 0.0, 1.0)
    middle_skeleton = jnp.clip(1.0 * jax.random.uniform(key_list[8], (MIDDLES, 3 * RANK), jnp.float32) ** block_levels(key_list[8], (MIDDLES, 3 * RANK), ((0, 128),), -0.2, 0.2), 0.0, 1.0)
    root_skeleton = jnp.clip(1.0 * jax.random.uniform(key_list[9], (ROOTS, 3 * RANK), jnp.float32) ** block_levels(key_list[9], (ROOTS, 3 * RANK), ((0, 128),), -0.2, 0.2), 0.0, 1.0)
    top_skeleton = jnp.clip(jax.random.uniform(key_list[10], (TOPS, 3 * RANK), jnp.float32, 0.0, 1.0), 0.0, 1.0)
    leaf_far = place_ends(jax.random.randint(key_list[11], (LEAVES, FAR), 0, SLOTS_LEAF), jax.random.fold_in(key_list[11], 1), 0, SLOTS_LEAF - 1).astype(jnp.int32)
    middle_far = place_ends(jax.random.randint(key_list[12], (MIDDLES, FAR), 0, SLOTS_MID), jax.random.fold_in(key_list[12], 1), 0, SLOTS_MID - 1).astype(jnp.int32)
    root_far = place_ends(jax.random.randint(key_list[13], (ROOTS, FAR), 0, ROOTS), jax.random.fold_in(key_list[13], 1), 0, ROOTS - 1).astype(jnp.int32)
    leaf_near = place_ends(jax.random.randint(key_list[14], (LEAVES, NEAR), 0, LEAF_DEV + 2 * HALO), jax.random.fold_in(key_list[14], 1), 0, (LEAF_DEV + 2 * HALO) - 1).astype(jnp.int32)
    leaf_sends = place_ends(jax.random.randint(key_list[15], (SLOTS_LEAF * N_GX * N_GY,), 0, LEAF_DEV), jax.random.fold_in(key_list[15], 1), 0, LEAF_DEV - 1).astype(jnp.int32)
    middle_sends = place_ends(jax.random.randint(key_list[16], (SLOTS_MID * N_GX * N_GY,), 0, 8 * ROOT_DEV), jax.random.fold_in(key_list[16], 1), 0, (8 * ROOT_DEV) - 1).astype(jnp.int32)
    return {"values": values, "coords": coords, "order": order, "leaf_basis": leaf_basis, "leaf_transfer": leaf_transfer, "middle_transfer": middle_transfer, "root_transfer": root_transfer, "leaf_skeleton": leaf_skeleton, "middle_skeleton": middle_skeleton, "root_skeleton": root_skeleton, "top_skeleton": top_skeleton, "leaf_far": leaf_far, "middle_far": middle_far, "root_far": root_far, "leaf_near": leaf_near, "leaf_sends": leaf_sends, "middle_sends": middle_sends}


decay_rate = math.sqrt(3.0) / 0.3
highest = lax.Precision.HIGHEST

def matern(left, right):
    delta = left[..., :, :, None] - right[..., :, None, :]
    distance = jnp.sqrt(lax.optimization_barrier(jnp.sum(delta * delta, axis=-3)))
    scaled = decay_rate * distance
    return (1.0 + scaled) * jnp.exp(-scaled)

def interact(target_points, table_points, table_values, index):
    count = index.shape[0]
    listed = index.shape[1]
    block = math.gcd(count, 16)
    inner = target_points.shape[-1]

    def block_product(inputs):
        targets, chosen = inputs
        kernel = matern(targets[:, None], table_points[chosen])
        return jnp.einsum('nfks,nfsr->nkr', kernel, table_values[chosen], precision=highest)
    result = lax.map(block_product, (target_points.reshape(count // block, block, 3, inner), index.reshape(count // block, block, listed)))
    return result.reshape(count, inner, table_values.shape[-1])

def source_index(sends, far_list, per_block, blocks):
    capacity = sends.shape[0] // (blocks * blocks)
    table = sends.reshape(blocks, blocks, capacity) + (jnp.arange(blocks, dtype=jnp.int32) * per_block)[:, None, None]
    table = table.transpose(1, 0, 2).reshape(blocks, blocks * capacity)
    owner = jnp.arange(far_list.shape[0], dtype=jnp.int32) // (far_list.shape[0] // blocks)
    return table[owner[:, None], far_list]

def reference(values, coords, order, leaf_basis, leaf_transfer, middle_transfer, root_transfer, leaf_skeleton, middle_skeleton, root_skeleton, top_skeleton, leaf_far, middle_far, root_far, leaf_near, leaf_sends, middle_sends):
    blocks = N_GX * N_GY
    global_order = (order + jnp.arange(POINTS, dtype=jnp.int32) // PTS_DEV * PTS_DEV).astype(jnp.int32)
    x_tree = jnp.take(values, global_order, axis=1)
    points_tree = jnp.take(coords, global_order, axis=1)
    leaf_values = x_tree.reshape(RHS, LEAVES, LEAF).transpose(1, 2, 0)
    leaf_points = points_tree.reshape(3, LEAVES, LEAF).transpose(1, 0, 2)
    basis = leaf_basis.reshape(LEAVES, LEAF, RANK)
    leaf_maps = leaf_transfer.reshape(LEAVES, RANK, RANK)
    middle_maps = middle_transfer.reshape(MIDDLES, RANK, RANK)
    root_maps = root_transfer.reshape(ROOTS, RANK, RANK)
    up_leaf = jnp.einsum('lpr,lpk->lkr', leaf_values, basis, precision=highest)
    up_middle = jnp.einsum('nkm,nkr->nmr', leaf_maps, up_leaf, precision=highest).reshape(MIDDLES, 8, RANK, RHS).sum(axis=1)
    up_root = jnp.einsum('nkm,nkr->nmr', middle_maps, up_middle, precision=highest).reshape(ROOTS, 8, RANK, RHS).sum(axis=1)
    parent_sum = jnp.einsum('nkm,nkr->nmr', root_maps, up_root, precision=highest).reshape(TOPS, ROOTS // TOPS, RANK, RHS).sum(axis=1)
    top_points = top_skeleton.reshape(TOPS, 3, RANK)
    others = 1.0 - jnp.eye(TOPS, dtype=jnp.float32)
    top_kernel = matern(top_points[:, None], top_points[None, :]) * others[:, :, None, None]
    top_far = jnp.einsum('ghks,hsr->gkr', top_kernel, parent_sum, precision=highest)
    leaf_skel = leaf_skeleton.reshape(LEAVES, 3, RANK)
    middle_skel = middle_skeleton.reshape(MIDDLES, 3, RANK)
    root_skel = root_skeleton.reshape(ROOTS, 3, RANK)
    far_leaf = interact(leaf_skel, leaf_skel, up_leaf, source_index(leaf_sends, leaf_far, LEAF_DEV, blocks))
    far_middle = interact(middle_skel, middle_skel, up_middle, source_index(middle_sends, middle_far, MIDDLES // blocks, blocks))
    far_root = interact(root_skel, root_skel, up_root, root_far)
    down_root = far_root + jnp.einsum('nkm,nmr->nkr', root_maps, jnp.repeat(top_far, ROOTS // TOPS, axis=0), precision=highest)
    down_middle = far_middle + jnp.einsum('nkm,nmr->nkr', middle_maps, jnp.repeat(down_root, 8, axis=0), precision=highest)
    down_leaf = far_leaf + jnp.einsum('nkm,nmr->nkr', leaf_maps, jnp.repeat(down_middle, 8, axis=0), precision=highest)
    far_values = jnp.einsum('lpk,lkr->lpr', basis, down_leaf, precision=highest)
    leaf_ids = jnp.arange(LEAVES, dtype=jnp.int32)
    window_start = leaf_ids // LEAF_DEV * LEAF_DEV - HALO
    neighbours = window_start[:, None] + leaf_near
    inside = (neighbours >= 0) & (neighbours < LEAVES)
    neighbours = jnp.where(inside, neighbours, LEAVES).astype(jnp.int32)
    near_index = jnp.concatenate([leaf_ids[:, None], neighbours], axis=1)
    table_points = jnp.concatenate([leaf_points, jnp.zeros((1, 3, LEAF), jnp.float32)], axis=0)
    table_values = jnp.concatenate([leaf_values, jnp.zeros((1, LEAF, RHS), jnp.float32)], axis=0)
    near_values = interact(leaf_points, table_points, table_values, near_index)
    y_tree = (far_values + near_values).transpose(2, 0, 1).reshape(RHS, POINTS)
    return jnp.zeros_like(values).at[:, global_order].set(y_tree)
```

```python
import math

import jax
import jax.numpy as jnp
from jax import lax
from jax.experimental import pallas as pl
from jax.experimental.pallas import tpu as pltpu
from jax.sharding import PartitionSpec as P

LEAF = 64
RANK = 64
RHS = 16
FEATS = 32
COLS = 4

both = ("gx", "gy")
f32 = jnp.float32
bf16 = jnp.bfloat16
log2e = 1.0 / math.log(2.0)
scale = math.sqrt(3.0) / 0.3 * log2e

VM = pl.BlockSpec(memory_space=pltpu.VMEM)
SM = pl.BlockSpec(memory_space=pltpu.SMEM)


def lanes(shape):
    return lax.broadcasted_iota(jnp.int32, shape, len(shape) - 1)


def swap(x):
    return pltpu.roll(x, 64, axis=x.ndim - 1)


def halves(x):
    high = x.astype(bf16)
    return high, (x - high.astype(f32)).astype(bf16)


def thirds(x):
    first = x.astype(bf16).astype(f32)
    rest = x - first
    second = rest.astype(bf16).astype(f32)
    return first, second, (rest - second).astype(bf16).astype(f32)


NN = (((1,), (0,)), ((), ()))
NT = (((1,), (1,)), ((), ()))


def dot(a, b, dims=NN):
    return lax.dot_general(a, b, dims, preferred_element_type=f32)


def dot3(a, b, dims=NN):
    ah, al = halves(a)
    bh, bl = halves(b)
    rows = a.shape[0]
    first = dot(jnp.concatenate([ah, al], axis=0), bh, dims)
    return first[:rows] + first[rows:] + dot(ah, bl, dims)


def stacked(rows, norm_row, one_row, factor):
    x, y, z = [(jnp.broadcast_to(r, (8, 128)) - 0.5) * scale for r in rows]
    norm = x * x + y * y + z * z
    sub = lax.broadcasted_iota(jnp.int32, (8, 128), 0)
    out = jnp.where(sub < 2, x, jnp.where(sub < 4, y, z)) * factor
    out = jnp.where(sub == norm_row, norm, out)
    return jnp.where(sub == one_row, 1.0, out), sub


def target_features(rows):
    base, sub = stacked(rows, 6, 7, -2.0)
    first, second, third = thirds(base)
    even = sub % 2 == 0
    last = jnp.where(sub == 7, 1.0, jnp.where(even, third, second))
    return jnp.concatenate(
        [first, jnp.where(even, second, first), last, jnp.zeros_like(first)], axis=0
    ).astype(bf16)


def source_features(rows):
    base, sub = stacked(rows, 7, 6, 1.0)
    first, second, third = thirds(base)
    even = sub % 2 == 0
    norm = sub == 7
    return jnp.concatenate(
        [
            jnp.where(even | norm, first, second),
            jnp.where(even, first, jnp.where(norm, second, third)),
            jnp.where(even, first, jnp.where(norm, third, second)),
            jnp.zeros_like(first),
        ],
        axis=0,
    ).astype(bf16)


def source_pair(rows, s_ref, at):
    features = source_features(rows)
    tall = jnp.concatenate([features] * COLS, axis=0)
    eye = (lax.broadcasted_iota(jnp.int32, (128, 128), 0) == lanes((128, 128))).astype(f32).astype(bf16)
    turned = dot(eye, tall, NT).astype(bf16)
    s_ref[at] = turned[:64]
    s_ref[at + 1] = turned[64:]


def put_values(x_ref, at, wide):
    high, low = halves(wide)
    x_ref[at, 0] = high
    x_ref[at, 1] = low


def values_from_tile(tile):
    left = lanes(tile.shape) < 64
    other = swap(tile)
    return jnp.concatenate([jnp.where(left, tile, other), jnp.where(left, other, tile)], axis=0)


def twice(rows, upper):
    left = lanes(rows.shape) < 64
    return jnp.where(left, swap(rows), rows) if upper else jnp.where(left, rows, swap(rows))


def couple(ids, s_ref, x_ref, target):
    zero = jnp.zeros_like(target)
    left = lanes(target.shape) < 64
    lower = jnp.where(left, target, zero)
    upper = jnp.where(left, zero, target)
    spread = jnp.concatenate(
        [
            jnp.concatenate([lower, upper, zero, zero], axis=0),
            jnp.concatenate([zero, zero, lower, upper], axis=0),
        ],
        axis=1,
    )
    group = lanes((64, 128)) // FEATS
    highs, lows = [], []
    for quad in ids:
        s = s_ref[quad[3]]
        for c in (2, 1, 0):
            s = jnp.where(group <= c, s_ref[quad[c]], s)
        square = jnp.maximum(dot(s, spread), 1e-30)
        u = square * lax.rsqrt(square)
        kernel = (u + log2e) * jnp.exp2(-u)
        high, low = halves(kernel)
        highs.append(high)
        lows.append(low)
    k_high = jnp.concatenate(highs, axis=0)
    k_low = jnp.concatenate(lows, axis=0)
    near = lanes((16, 128)) < 64

    def joined(part):
        out = []
        for c in range(COLS):
            pieces = []
            for g in range(0, len(ids) - 1, 2):
                pieces.append(jnp.where(near, x_ref[ids[g][c], part], x_ref[ids[g + 1][c], part]))
            if len(ids) % 2:
                pieces.append(x_ref[ids[-1][c], part][:, :64])
            out.append(jnp.concatenate(pieces, axis=1))
        return jnp.concatenate(out, axis=0)

    x_high, x_low = joined(0), joined(1)
    rows = 16 * COLS
    first = dot(jnp.concatenate([x_high, x_low], axis=0), k_high)
    total = first[:rows] + first[rows:] + dot(x_high, k_low)
    even = total[:16, :128] + total[32:48, 128:]
    odd = total[16:32, :128] + total[48:, 128:]
    return even, odd


def two_targets(first, second):
    left = lanes(first[0].shape) < 64
    return (
        jnp.where(left, first[0], second[1]) + swap(jnp.where(left, second[0], first[1]))
    ) * (1.0 / log2e)


def one_target(pair):
    return (pair[0] + swap(pair[1])) * (1.0 / log2e)


def quads(index, row, count):
    return [[index[row, 4 * g + c] for c in range(4)] for g in range(count)]


def call(kernel, name, out, in_specs, scratch=(), flops=0, data=0, limit=48):
    return pl.pallas_call(
        kernel,
        name=name,
        out_shape=out,
        in_specs=in_specs,
        out_specs=jax.tree.map(lambda _: VM, out),
        scratch_shapes=list(scratch),
        cost_estimate=pl.CostEstimate(flops=flops, bytes_accessed=data, transcendentals=0),
        compiler_params=pltpu.CompilerParams(vmem_limit_bytes=limit * 2**20),
    )


def shape(*dims, kind=f32):
    return jax.ShapeDtypeStruct(dims, kind)


def pack_skeletons(sends, middle_sends, leaf_table, middle_table, out):
    left = lanes((3, 128)) < 64

    def body(b, _):
        rows = []
        for p in range(4):
            rows.append(
                jnp.where(left, leaf_table[sends[b * 8 + 2 * p]], leaf_table[sends[b * 8 + 2 * p + 1]])
            )
        rows.append(
            jnp.where(left, middle_table[middle_sends[2 * b]], middle_table[middle_sends[2 * b + 1]])
        )
        rows.append(jnp.zeros((1, 128), f32))
        out[b] = jnp.concatenate(rows, axis=0)
        return 0

    lax.fori_loop(0, 128, body, 0, unroll=4)


def permute_columns(source, index, out):
    height = source.shape[0] // 8

    def body(j, _):
        where = jnp.broadcast_to(index[pl.ds(j, 1), :], (8, 128))
        inside = where % 128
        tile = where // 128
        found = [jnp.zeros((8, 128), f32)] * height
        for i in range(32):
            match = tile == i
            for r in range(height):
                piece = source[8 * r : 8 * r + 8, 128 * i : 128 * i + 128]
                piece = jnp.take_along_axis(piece, inside, axis=1, mode="promise_in_bounds")
                found[r] = jnp.where(match, piece, found[r])
        for r in range(height):
            out[8 * r : 8 * r + 8, pl.ds(pl.multiple_of(j * 128, 128), 128)] = found[r]
        return 0

    lax.fori_loop(0, 32, body, 0)


def up_leaves(sends, source, order, basis, tree, up, out, tiles):
    permute_columns(source, order, tree)

    def leaf_pair(i, _):
        columns = pl.ds(pl.multiple_of(i * 128, 128), 128)
        x = tree[0:16, columns]
        a = dot3(x[:, :64], basis[2 * i])
        b = dot3(x[:, 64:], basis[2 * i + 1])
        up[:, columns] = jnp.concatenate([a, b], axis=1)
        tiles[2 * i] = jnp.concatenate([a[:8], a[8:]], axis=1)
        tiles[2 * i + 1] = jnp.concatenate([b[:8], b[8:]], axis=1)
        return 0

    lax.fori_loop(0, 32, leaf_pair, 0, unroll=4)

    def slot(s, _):
        out[s] = tiles[sends[s]]
        return 0

    lax.fori_loop(0, 1024, slot, 0, unroll=16)


def up_rest(sends, up, leaf_maps, middle_maps, root_maps, root_rows, middle_out, root_out, tiles):
    parts = []
    for j in range(8):
        part = dot3(up[:, 512 * j : 512 * j + 512], leaf_maps[512 * j : 512 * j + 512, :])
        tiles[j] = jnp.concatenate([part[:8], part[8:]], axis=1)
        parts.append(part)
    middle = jnp.concatenate(parts, axis=1)
    root = dot3(middle, middle_maps[...])
    top = dot3(root, root_maps[...])
    root_out[0:8] = jnp.concatenate([root[:8], root[8:]], axis=1)
    root_out[8:16] = jnp.concatenate([top[:8], top[8:]], axis=1)
    root_out[16:24] = root_rows[...]

    def slot(s, _):
        middle_out[s] = tiles[sends[s]]
        return 0

    lax.fori_loop(0, 256, slot, 0, unroll=16)


def invert(order, inverse):
    def body(i, _):
        inverse[order[i]] = i
        return 0

    lax.fori_loop(0, 4096, body, 0, unroll=32)


def near_field(index, window, out, s_ref, x_ref):
    s_ref[80] = jnp.zeros((64, 128), bf16)
    x_ref[80] = jnp.zeros((2, 16, 128), bf16)

    def prepare(i, _):
        block = window[:, pl.ds(pl.multiple_of(i * 128, 128), 128)]
        source_pair([block[16:17], block[17:18], block[18:19]], s_ref, 2 * i)
        put_values(x_ref, 2 * i, twice(block[:16], False))
        put_values(x_ref, 2 * i + 1, twice(block[:16], True))
        return 0

    lax.fori_loop(0, 40, prepare, 0, unroll=2)

    def pair(i, _):
        block = window[16:24, pl.ds(pl.multiple_of(i * 128 + 512, 128), 128)]
        results = []
        for half in range(2):
            points = twice(block, half == 1)
            target = target_features([points[0:1], points[1:2], points[2:3]])
            l = 2 * i + half
            sources = [l + 8] + [index[l, f] for f in range(26)] + [80]
            ids = [sources[4 * g : 4 * g + 4] for g in range(7)]
            results.append(couple(ids, s_ref, x_ref, target))
        out[:, pl.ds(pl.multiple_of(i * 128, 128), 128)] = two_targets(*results)
        return 0

    lax.fori_loop(0, 32, pair, 0)


def leaf_sources(received, s_ref):
    def prepare(q, _):
        block = received[q]
        for p in range(4):
            rows = [block[3 * p + j : 3 * p + j + 1] for j in range(3)]
            source_pair(rows, s_ref, q * 8 + 2 * p)
        return 0

    lax.fori_loop(0, 128, prepare, 0)


def far_leaves(index, tiles, s_ref, target_rows, out, x_ref):
    def prepare(s, _):
        put_values(x_ref, s, values_from_tile(tiles[s]))
        return 0

    lax.fori_loop(0, 1024, prepare, 0, unroll=8)
    far_pairs(index, s_ref, x_ref, target_rows, out, 32)


def far_pairs(index, s_ref, x_ref, target_rows, out, pairs):
    def pair(i, _):
        results = []
        for half in range(2):
            l = 2 * i + half
            rows = target_rows[l]
            target = target_features([rows[0:1], rows[1:2], rows[2:3]])
            results.append(couple(quads(index, l, 16), s_ref, x_ref, target))
        out[:, pl.ds(pl.multiple_of(i * 128, 128), 128)] = two_targets(*results)
        return 0

    lax.fori_loop(0, pairs, pair, 0)


def far_upper(
    middle_index, root_index, group, skeletons, middle_tiles, roots, middle_rows, top_rows,
    middle_out, root_out, top_out, s_ref, x_ref,
):
    left = lanes((1, 128)) < 64

    def middle_pair(q, _):
        block = skeletons[q]
        source_pair([block[12 + j : 13 + j] for j in range(3)], s_ref, 2 * q)
        put_values(x_ref, 2 * q, values_from_tile(middle_tiles[2 * q]))
        put_values(x_ref, 2 * q + 1, values_from_tile(middle_tiles[2 * q + 1]))
        return 0

    lax.fori_loop(0, 128, middle_pair, 0, unroll=2)
    far_pairs(middle_index, s_ref, x_ref, middle_rows, middle_out, 4)

    def root_pair(q, _):
        a, b = roots[2 * q], roots[2 * q + 1]
        source_pair([jnp.where(left, a[16 + j : 17 + j], b[16 + j : 17 + j]) for j in range(3)], s_ref, 2 * q)
        put_values(x_ref, 2 * q, values_from_tile(a[:8]))
        put_values(x_ref, 2 * q + 1, values_from_tile(b[:8]))
        return 0

    lax.fori_loop(0, 64, root_pair, 0, unroll=2)
    own = roots[group[1]]
    target = target_features([own[16:17], own[17:18], own[18:19]])
    root_out[...] = one_target(couple(quads(root_index, 0, 16), s_ref, x_ref, target))

    for q in range(8):
        a, b = top_rows[2 * q], top_rows[2 * q + 1]
        source_pair([jnp.where(left, a[j : j + 1], b[j : j + 1]) for j in range(3)], s_ref, 2 * q)

    def parent(h, _):
        total = roots[8 * h][8:16]
        for n in range(1, 8):
            total = total + roots[8 * h + n][8:16]
        total = jnp.where(h == group[0], jnp.zeros_like(total), total)
        put_values(x_ref, h, values_from_tile(total))
        return 0

    lax.fori_loop(0, 16, parent, 0)
    mine = top_rows[group[0]]
    target = target_features([mine[0:1], mine[1:2], mine[2:3]])
    ids = [[4 * g + c for c in range(4)] for g in range(4)]
    top_out[...] = one_target(couple(ids, s_ref, x_ref, target))


def down(near, far, far_middle, far_root, top_far, basis, leaf_maps, middle_maps, root_maps, inverse, out, tree):
    root = far_root[:, :64] + dot3(top_far[:, :64], root_maps[...], NT)
    middle = far_middle[...] + dot3(root, middle_maps[...], NT)
    for j in range(8):
        columns = slice(512 * j, 512 * j + 512)
        leaf = far[:, columns] + dot3(middle[:, 64 * j : 64 * j + 64], leaf_maps[columns, :], NT)
        for p in range(4):
            l = 8 * j + 2 * p
            a = dot3(leaf[:, 128 * p : 128 * p + 64], basis[l], NT)
            b = dot3(leaf[:, 128 * p + 64 : 128 * p + 128], basis[l + 1], NT)
            tree[:, 64 * l : 64 * l + 128] = jnp.concatenate([a, b], axis=1) + near[:, 64 * l : 64 * l + 128]
    permute_columns(tree, inverse, out)


def from_behind(block, distance):
    devices = range(lax.axis_size(both))
    return lax.ppermute(block, both, [(i - distance, i) for i in devices if i - distance in devices])


def paired(skeleton):
    rows = skeleton.reshape(-1, 3, RANK)
    return jnp.concatenate([rows, rows], axis=2)


def exchange(x):
    return lax.all_to_all(x, both, split_axis=0, concat_axis=0, tiled=True)


def shards(
    values,
    coords,
    order,
    leaf_basis,
    leaf_transfer,
    middle_transfer,
    root_transfer,
    leaf_skeleton,
    middle_skeleton,
    root_skeleton,
    top_skeleton,
    leaf_far,
    middle_far,
    root_far,
    leaf_near,
    leaf_sends,
    middle_sends,
):
    leaf_rows = paired(leaf_skeleton)
    middle_rows = paired(middle_skeleton)
    root_rows = paired(root_skeleton)[0]
    top_rows = paired(top_skeleton)
    packed = call(pack_skeletons, "pack_skeletons", shape(128, 16, 128), [SM, SM, VM, VM])(
        leaf_sends, middle_sends, leaf_rows, middle_rows
    )
    skeletons = exchange(packed)

    basis = leaf_basis.reshape(64, LEAF, RANK)
    source = jnp.concatenate([values, coords, jnp.zeros((5, values.shape[1]), f32)], axis=0)
    tree, up, outgoing = call(
        up_leaves,
        "up_leaves",
        (shape(24, 4096), shape(16, 4096), shape(1024, 8, 128)),
        [SM, VM, VM, VM],
        [pltpu.VMEM((64, 8, 128), f32)],
        data=8 * 2**20,
    )(leaf_sends, source, order.reshape(32, 128), basis)
    tiles = exchange(outgoing.reshape(128, 64, 128)).reshape(1024, 8, 128)

    before = from_behind(tree[:, 4096 - 512 :], 1)
    after = from_behind(tree[:, :512], -1)

    leaf_maps = leaf_transfer.reshape(64 * RANK, RANK)
    middle_maps = middle_transfer.reshape(8 * RANK, RANK)
    root_maps = root_transfer.reshape(RANK, RANK)
    middle_out, root_out = call(
        up_rest,
        "up_rest",
        (shape(256, 8, 128), shape(24, 128)),
        [SM, VM, VM, VM, VM, VM],
        [pltpu.VMEM((8, 8, 128), f32)],
        data=4 * 2**20,
    )(
        middle_sends, up, leaf_maps, middle_maps, root_maps,
        jnp.concatenate([root_rows, jnp.zeros((5, 128), f32)], axis=0),
    )
    middle_tiles = exchange(middle_out.reshape(128, 16, 128)).reshape(256, 8, 128)
    roots = lax.all_gather(root_out[None], both, axis=0, tiled=True)

    window = jnp.concatenate([before, tree, after], axis=1)
    near = call(
        near_field,
        "near_field",
        shape(16, 4096),
        [SM, VM],
        [pltpu.VMEM((81, 64, 128), bf16), pltpu.VMEM((81, 2, 16, 128), bf16)],
        flops=22 * 10**9,
    )(leaf_near, window)
    inverse = pl.pallas_call(
        invert,
        name="invert",
        out_shape=shape(4096, kind=jnp.int32),
        in_specs=[SM],
        out_specs=SM,
        cost_estimate=pl.CostEstimate(flops=6 * 10**9, bytes_accessed=0, transcendentals=0),
    )(order).reshape(32, 128)
    leaf_table = call(
        leaf_sources, "leaf_sources", shape(1024, 64, 128, kind=bf16), [VM], flops=12 * 10**9
    )(skeletons)
    far = call(
        far_leaves,
        "far_leaves",
        shape(16, 4096),
        [SM, VM, VM, VM],
        [pltpu.VMEM((1024, 2, 16, 128), bf16)],
        flops=50 * 10**9,
    )(leaf_far, tiles, leaf_table, leaf_rows)
    group = jnp.stack([lax.axis_index("gx"), lax.axis_index(both)]).astype(jnp.int32)
    far_middle, far_root, top_far = call(
        far_upper,
        "far_upper",
        (shape(16, 512), shape(16, 128), shape(16, 128)),
        [SM, SM, SM, VM, VM, VM, VM, VM],
        [pltpu.VMEM((256, 64, 128), bf16), pltpu.VMEM((256, 2, 16, 128), bf16)],
        flops=10 * 10**9,
    )(middle_far, root_far, group, skeletons, middle_tiles, roots, middle_rows, top_rows)
    return call(
        down,
        "down",
        shape(16, 4096),
        [VM] * 10,
        [pltpu.VMEM((16, 4096), f32)],
        data=8 * 2**20,
    )(near, far, far_middle, far_root, top_far, basis, leaf_maps, middle_maps, root_maps, inverse)


def solution(mesh):
    split = P(both, None)
    placed = (
        P(None, both),
        P(None, both),
        P(both),
        split,
        split,
        split,
        split,
        split,
        split,
        split,
        P(),
        split,
        split,
        split,
        split,
        P(both),
        P(both),
    )
    return jax.shard_map(
        shards, mesh=mesh, in_specs=placed, out_specs=P(None, both), check_vma=False
    )
```

```python
import math

import jax
import jax.numpy as jnp
from jax import lax
from jax.experimental import pallas as pl
from jax.experimental.pallas import tpu as pltpu
from jax.sharding import PartitionSpec as P

LEAF = 64
RANK = 64
RHS = 16
FEATS = 32
COLS = 4

both = ("gx", "gy")
f32 = jnp.float32
bf16 = jnp.bfloat16
log2e = 1.0 / math.log(2.0)
scale = math.sqrt(3.0) / 0.3 * log2e

VM = pl.BlockSpec(memory_space=pltpu.VMEM)
SM = pl.BlockSpec(memory_space=pltpu.SMEM)


def lanes(shape):
    return lax.broadcasted_iota(jnp.int32, shape, len(shape) - 1)


def swap(x):
    return pltpu.roll(x, 64, axis=x.ndim - 1)


def halves(x):
    high = x.astype(bf16)
    return high, (x - high.astype(f32)).astype(bf16)


def thirds(x):
    first = x.astype(bf16).astype(f32)
    rest = x - first
    second = rest.astype(bf16).astype(f32)
    return first, second, (rest - second).astype(bf16).astype(f32)


NN = (((1,), (0,)), ((), ()))
NT = (((1,), (1,)), ((), ()))


def dot(a, b, dims=NN):
    return lax.dot_general(a, b, dims, preferred_element_type=f32)


def dot3(a, b, dims=NN):
    ah, al = halves(a)
    bh, bl = halves(b)
    rows = a.shape[0]
    first = dot(jnp.concatenate([ah, al], axis=0), bh, dims)
    return first[:rows] + first[rows:] + dot(ah, bl, dims)


def stacked(rows, norm_row, one_row, factor):
    x, y, z = [(jnp.broadcast_to(r, (8, 128)) - 0.5) * scale for r in rows]
    norm = x * x + y * y + z * z
    sub = lax.broadcasted_iota(jnp.int32, (8, 128), 0)
    out = jnp.where(sub < 2, x, jnp.where(sub < 4, y, z)) * factor
    out = jnp.where(sub == norm_row, norm, out)
    return jnp.where(sub == one_row, 1.0, out), sub


def target_features(rows):
    base, sub = stacked(rows, 6, 7, -2.0)
    first, second, third = thirds(base)
    even = sub % 2 == 0
    last = jnp.where(sub == 7, 1.0, jnp.where(even, third, second))
    return jnp.concatenate(
        [first, jnp.where(even, second, first), last, jnp.zeros_like(first)], axis=0
    ).astype(bf16)


def source_features(rows):
    base, sub = stacked(rows, 7, 6, 1.0)
    first, second, third = thirds(base)
    even = sub % 2 == 0
    norm = sub == 7
    return jnp.concatenate(
        [
            jnp.where(even | norm, first, second),
            jnp.where(even, first, jnp.where(norm, second, third)),
            jnp.where(even, first, jnp.where(norm, third, second)),
            jnp.zeros_like(first),
        ],
        axis=0,
    ).astype(bf16)


def source_row(v, column):
    return (v & -8) + ((v & 1) << 2) + ((column - (v >> 1)) & 3)


def source_eight(pairs, s_ref, at):
    tall = jnp.concatenate([source_features(rows) for rows in pairs], axis=0)
    eye = (lax.broadcasted_iota(jnp.int32, (128, 128), 0) == lanes((128, 128))).astype(f32).astype(bf16)
    turned = dot(eye, tall, NT)
    for k in range(COLS):
        moved = (turned if k == 0 else pltpu.roll(turned, FEATS * k, axis=1)).astype(bf16)
        s_ref[at + k] = moved[:64]
        s_ref[at + COLS + k] = moved[64:]


def put_values(x_ref, at, wide):
    high, low = halves(wide)
    x_ref[at, 0] = high
    x_ref[at, 1] = low


def values_from_tile(tile):
    left = lanes(tile.shape) < 64
    other = swap(tile)
    return jnp.concatenate([jnp.where(left, tile, other), jnp.where(left, other, tile)], axis=0)


def twice(rows, upper):
    left = lanes(rows.shape) < 64
    return jnp.where(left, swap(rows), rows) if upper else jnp.where(left, rows, swap(rows))


def make_kernel(ids, start, s_ref, spread, k_ref):
    stop = min(start + 4, len(ids) // COLS)
    group = lanes((64, 128)) // FEATS
    stack = []
    for g in range(start, stop):
        quad = ids[4 * g : 4 * g + 4]
        s = s_ref[source_row(quad[3], 3)]
        for c in (2, 1, 0):
            s = jnp.where(group <= c, s_ref[source_row(quad[c], c)], s)
        stack.append(s)
    square = jnp.maximum(dot(jnp.concatenate(stack, axis=0), spread), 1e-30)
    u = square * lax.rsqrt(square)
    high, low = halves((u + log2e) * jnp.exp2(-u))
    k_ref[0, 64 * start : 64 * stop] = high
    k_ref[1, 64 * start : 64 * stop] = low


def apply_kernel(ids, start, x_ref, k_ref, total):
    count = len(ids) // COLS
    stop = min(start + 4, count)
    near = lanes((16, 128)) < 64

    def joined(part):
        out = []
        for c in range(COLS):
            pieces = []
            for g in range(start, stop, 2):
                first = x_ref[ids[4 * g + c], part]
                if g + 1 < count:
                    pieces.append(jnp.where(near, first, x_ref[ids[4 * g + 4 + c], part]))
                else:
                    pieces.append(first[:, :64])
            out.append(jnp.concatenate(pieces, axis=1))
        return jnp.concatenate(out, axis=0)

    x_high, x_low = joined(0), joined(1)
    rows = slice(64 * start, 64 * stop)
    first = dot(jnp.concatenate([x_high, x_low], axis=0), k_ref[0, rows])
    second = dot(x_high, k_ref[1, rows])
    return (first, second) if total is None else (total[0] + first, total[1] + second)


def summed(total):
    rows = 16 * COLS
    whole = total[0][:rows] + total[0][rows:] + total[1]
    return whole[:16, :128] + whole[32:48, 128:], whole[16:32, :128] + whole[48:, 128:]


def spread_target(target):
    zero = jnp.zeros_like(target)
    left = lanes(target.shape) < 64
    lower = jnp.where(left, target, zero)
    upper = jnp.where(left, zero, target)
    return jnp.concatenate(
        [
            jnp.concatenate([lower, upper, zero, zero], axis=0),
            jnp.concatenate([zero, zero, lower, upper], axis=0),
        ],
        axis=1,
    )


def couple(ids, s_ref, x_ref, target, k_ref):
    spread = spread_target(target)
    total = None
    for q in range(0, len(ids) // COLS, 4):
        make_kernel(ids, q, s_ref, spread, k_ref)
        total = apply_kernel(ids, q, x_ref, k_ref, total)
    return summed(total)


def couple_all(count, ids, target, s_ref, x_ref, out, ka, kb, unroll=1):
    def advance(new, k_new, old, k_old):
        made, used = ids(new), ids(old)
        spread = spread_target(target(new))
        total = None
        for q in range(0, len(made) // COLS, 4):
            make_kernel(made, q, s_ref, spread, k_new)
            total = apply_kernel(used, q, x_ref, k_old, total)
        return summed(total)

    first = ids(0)
    spread = spread_target(target(0))
    for q in range(0, len(first) // COLS, 4):
        make_kernel(first, q, s_ref, spread, ka)

    def pair(i, _):
        lower = advance(2 * i + 1, kb, 2 * i, ka)
        upper = advance(jnp.minimum(2 * i + 2, count - 1), ka, 2 * i + 1, kb)
        out[:, pl.ds(pl.multiple_of(i * 128, 128), 128)] = two_targets(lower, upper)
        return 0

    lax.fori_loop(0, count // 2, pair, 0, unroll=unroll)


def two_targets(first, second):
    left = lanes(first[0].shape) < 64
    return (
        jnp.where(left, first[0], second[1]) + swap(jnp.where(left, second[0], first[1]))
    ) * (1.0 / log2e)


def one_target(pair):
    return (pair[0] + swap(pair[1])) * (1.0 / log2e)


HBM = pl.BlockSpec(memory_space=pl.ANY)


def call(kernel, name, out, in_specs, scratch=(), flops=0, data=0, limit=60):
    return pl.pallas_call(
        kernel,
        name=name,
        out_shape=out,
        in_specs=in_specs,
        out_specs=jax.tree.map(lambda _: VM, out),
        scratch_shapes=list(scratch),
        cost_estimate=pl.CostEstimate(flops=flops, bytes_accessed=data, transcendentals=0),
        compiler_params=pltpu.CompilerParams(vmem_limit_bytes=limit * 2**20),
    )


def shape(*dims, kind=f32):
    return jax.ShapeDtypeStruct(dims, kind)


def put_rows(skeleton, table):
    first = skeleton[:, :128]
    table[0] = twice(first, False)
    table[1] = twice(first, True)
    last = skeleton[:, 128:]
    table[2] = jnp.concatenate([last, last], axis=1)


def rows_of(table, at):
    return [table[j, pl.ds(at, 1), :] for j in range(3)]


def pair_rows(table, a, b):
    left = lanes((1, 128)) < 64
    return [jnp.where(left, x, y) for x, y in zip(rows_of(table, a), rows_of(table, b))]


def pack_skeletons(sends, middle_sends, leaf_skeleton, middle_skeleton, out, leaf_table, middle_table):
    put_rows(leaf_skeleton, leaf_table)
    put_rows(middle_skeleton, middle_table)

    def body(b, _):
        rows = []
        for p in range(4):
            rows += pair_rows(leaf_table, sends[b * 8 + 2 * p], sends[b * 8 + 2 * p + 1])
        rows += pair_rows(middle_table, middle_sends[2 * b], middle_sends[2 * b + 1])
        rows.append(jnp.zeros((1, 128), f32))
        out[b] = jnp.concatenate(rows, axis=0)
        return 0

    lax.fori_loop(0, 128, body, 0, unroll=4)


def take(x, index):
    pieces = [
        jnp.take_along_axis(x[r : r + 8], index, axis=1, mode="promise_in_bounds")
        for r in range(0, x.shape[0], 8)
    ]
    return pieces[0] if len(pieces) == 1 else jnp.concatenate(pieces, axis=0)


def even_first():
    i = lanes((8, 128))
    return (i & 64) + 2 * (i & 31) + ((i >> 5) & 1)


def evens_odds():
    i = lanes((8, 128))
    return ((i & 32) << 1) + 2 * (i & 31) + (i >> 6)


def evens_odds_back():
    i = lanes((8, 128))
    return ((i & 1) << 6) + ((i >> 6) << 5) + ((i & 63) >> 1)


def permute_columns(source, index, out, halved):
    height = source.shape[0] // 8

    def body(j, _):
        where = jnp.broadcast_to(index[pl.ds(j, 1), :], (8, 128))
        if halved:
            where = take(where, even_first())
        inside = where & 127
        tile = where >> 7
        found = [jnp.zeros((8, 128), f32)] * height
        for i in range(32):
            match = tile == i
            for r in range(height):
                piece = source[8 * r : 8 * r + 8, 128 * i : 128 * i + 128]
                found[r] = jnp.where(match, take(piece, inside), found[r])
        for r in range(height):
            out[8 * r : 8 * r + 8, pl.ds(pl.multiple_of(j * 128, 128), 128)] = found[r]
        return 0

    lax.fori_loop(0, 32, body, 0, unroll=2)


def pair_halves(result):
    return result[:16] + swap(result[16:])


def as_tile(x):
    left = lanes((8, 128)) < 64
    return jnp.where(left, x[:8], swap(x[8:]))


def side_by_side(a, b):
    return jnp.where(lanes(a.shape) < 64, a, swap(b))


def even_odd_rows(blocks):
    left = lanes((16, 128)) < 64
    even, odd = [], []
    for v, w in zip(blocks[::2], blocks[1::2]):
        even.append(jnp.where(left, v, swap(w)))
        odd.append(jnp.where(left, swap(v), w))
    return jnp.concatenate([jnp.concatenate(even, axis=1), jnp.concatenate(odd, axis=1)], axis=0)


def tree_order(values, coords, order, tree, first_leaves, last_leaves, source):
    source[0:16] = values[...]
    source[16:19] = coords[...]
    source[19:24] = jnp.zeros((5, 4096), f32)
    permute_columns(source, order, tree, True)
    first_leaves[...] = tree[:, :512]
    last_leaves[...] = tree[:, 3584:]


def up_pass(
    sends, middle_sends, tree, root_skeleton, basis, leaf_maps, middle_maps, root_maps,
    out, root_out, basis_rows, leaf_rows, middle_rows, root_rows,
    split, tiles, middle_tiles, root_table, sems,
):
    copies = []
    for m, (whole, rows) in enumerate(
        ((basis, basis_rows), (leaf_maps, leaf_rows), (middle_maps, middle_rows), (root_maps, root_rows))
    ):
        copies.append(
            [
                pltpu.make_async_copy(whole.at[:, pl.ds(128 * t, 128)], rows.at[:, t, :], sems.at[m, t])
                for t in range(32)
            ]
        )
    for group in copies:
        for copy in group:
            copy.start()
    for copy in copies[0]:
        copy.wait()

    def leaf_pair(i, _):
        columns = pl.ds(pl.multiple_of(i * 128, 128), 128)
        x = tree[0:16, columns]
        a = pair_halves(dot3(jnp.concatenate([x[:, :32], x[:, 32:64]], axis=0), basis_rows[2 * i]))
        b = pair_halves(dot3(jnp.concatenate([x[:, 64:96], x[:, 96:]], axis=0), basis_rows[2 * i + 1]))
        split[:, columns] = take(side_by_side(a, b), evens_odds())
        tiles[2 * i] = as_tile(a)
        tiles[2 * i + 1] = as_tile(b)
        return 0

    lax.fori_loop(0, 32, leaf_pair, 0, unroll=4)

    def slots(b, _):
        for c in range(8):
            out[b, 8 * c : 8 * c + 8] = tiles[sends[8 * b + c]]
        return 0

    lax.fori_loop(0, 128, slots, 0, unroll=2)
    for group in copies[1:]:
        for copy in group:
            copy.wait()
    middles = []
    for j in range(8):
        blocks = [split[:, 512 * j + 128 * p : 512 * j + 128 * p + 128] for p in range(4)]
        part = pair_halves(dot3(even_odd_rows(blocks), leaf_rows[8 * j : 8 * j + 8].reshape(256, 128)))
        middle_tiles[j] = as_tile(part)
        middles.append(part)
    blocks = [take(side_by_side(middles[2 * p], middles[2 * p + 1]), evens_odds()) for p in range(4)]
    root = pair_halves(dot3(even_odd_rows(blocks), middle_rows[...].reshape(256, 128)))
    turned = take(root, evens_odds())
    top = pair_halves(dot3(jnp.concatenate([turned[:, :32], turned[:, 64:96]], axis=0), root_rows[0]))
    put_rows(root_skeleton, root_table)
    root_out[0:8] = as_tile(root)
    root_out[8:16] = as_tile(top)
    root_out[16:24] = jnp.concatenate(rows_of(root_table, 0) + [jnp.zeros((5, 128), f32)], axis=0)

    def middle_slots(b, _):
        for c in range(2):
            out[b, 64 + 8 * c : 72 + 8 * c] = middle_tiles[middle_sends[2 * b + c]]
        return 0

    lax.fori_loop(0, 128, middle_slots, 0, unroll=4)


def invert(order, inverse):
    def body(b, _):
        for p in range(64):
            inverse[order[b * 64 + p]] = b * 64 + (p % 2) * 32 + p // 2
        return 0

    lax.fori_loop(0, 64, body, 0)


def near_field(index, before, tree, after, out, window, s_ref, x_ref, ka, kb):
    window[:, :512] = before[...]
    window[:, 512:4608] = tree[...]
    window[:, 4608:] = after[...]
    for k in range(8):
        s_ref[80 + k] = jnp.zeros((64, 128), bf16)
    x_ref[80] = jnp.zeros((2, 16, 128), bf16)

    def prepare(i, _):
        pairs = []
        for p in range(4):
            block = window[:, pl.ds(pl.multiple_of(i * 512 + p * 128, 128), 128)]
            pairs.append([block[16:17], block[17:18], block[18:19]])
            put_values(x_ref, 8 * i + 2 * p, twice(block[:16], False))
            put_values(x_ref, 8 * i + 2 * p + 1, twice(block[:16], True))
        source_eight(pairs, s_ref, 8 * i)
        return 0

    lax.fori_loop(0, 10, prepare, 0, unroll=2)

    def ids(l):
        return [l + 8] + [index[f, l] for f in range(26)] + [80]

    def target(l):
        block = window[16:24, pl.ds(pl.multiple_of((l >> 1) * 128 + 512, 128), 128)]
        left = lanes(block.shape) < 64
        points = jnp.where(left == (l % 2 == 0), block, swap(block))
        return target_features([points[0:1], points[1:2], points[2:3]])

    couple_all(64, ids, target, s_ref, x_ref, out, ka, kb, unroll=2)


def sources(received, s_ref, middle_ref):
    def prepare(q, _):
        block = received[q]
        source_eight([[block[3 * p + j : 3 * p + j + 1] for j in range(3)] for p in range(4)], s_ref, q * 8)
        return 0

    lax.fori_loop(0, 128, prepare, 0, unroll=4)

    def middle(q, _):
        source_eight(
            [[received[4 * q + p, 12 + j : 13 + j] for j in range(3)] for p in range(4)], middle_ref, q * 8
        )
        return 0

    lax.fori_loop(0, 32, middle, 0, unroll=4)


def far_ids(index):
    return lambda l: [index[l, f] for f in range(64)]


def far_leaves(index, skeleton, received, table, out, s_ref, tiles, x_ref, rows, ka, kb, sems):
    parts = [
        pltpu.make_async_copy(
            received.at[pl.ds(32 * p, 32), pl.ds(0, 64), :], tiles.at[pl.ds(32 * p, 32)], sems.at[p]
        )
        for p in range(4)
    ]
    for part in parts:
        part.start()
    loaded = pltpu.make_async_copy(table, s_ref, sems.at[4])
    loaded.start()
    put_rows(skeleton, rows)
    for p in range(4):
        parts[p].wait()

        def prepare(q, _):
            for c in range(8):
                put_values(x_ref, 8 * q + c, values_from_tile(tiles[q, 8 * c : 8 * c + 8]))
            return 0

        lax.fori_loop(32 * p, 32 * p + 32, prepare, 0)
    loaded.wait()
    couple_all(
        64, far_ids(index), lambda l: target_features(rows_of(rows, l)), s_ref, x_ref, out, ka, kb
    )


def lifted(x, rows):
    left = lanes(x.shape) < 64
    zero = jnp.zeros_like(x)
    wide = jnp.concatenate([jnp.where(left, x, zero), jnp.where(left, zero, swap(x))], axis=0)
    return dot3(wide, rows, NT)


def natural(result, p):
    part = slice(64 * p, 64 * p + 64)
    return take(jnp.concatenate([result[:16, part], result[16:, part]], axis=1), evens_odds_back())


def finish(
    middle_index, root_index, received, middle_table, roots, middle_skeleton, top_skeleton,
    near, far, basis_rows, leaf_rows, middle_rows, root_rows, inverse,
    out, far_middle, x_ref, s_ref, ka, kb, middle_points, top_points, tree,
):
    left = lanes((1, 128)) < 64
    put_rows(middle_skeleton, middle_points)
    put_rows(top_skeleton, top_points)
    group = lax.axis_index("gx")

    def middle_values(q, _):
        for c in range(2):
            put_values(x_ref, 2 * q + c, values_from_tile(received[q, 8 * c : 8 * c + 8]))
        return 0

    lax.fori_loop(0, 128, middle_values, 0, unroll=4)
    couple_all(
        8, far_ids(middle_index), lambda l: target_features(rows_of(middle_points, l)),
        middle_table, x_ref, far_middle, ka, kb,
    )

    def root_sources(q, _):
        pairs = []
        for p in range(4):
            a, b = roots[8 * q + 2 * p], roots[8 * q + 2 * p + 1]
            pairs.append([jnp.where(left, a[16 + j : 17 + j], b[16 + j : 17 + j]) for j in range(3)])
            put_values(x_ref, 8 * q + 2 * p, values_from_tile(a[:8]))
            put_values(x_ref, 8 * q + 2 * p + 1, values_from_tile(b[:8]))
        source_eight(pairs, s_ref, 8 * q)
        return 0

    lax.fori_loop(0, 16, root_sources, 0, unroll=2)
    own = roots[lax.axis_index(both)]
    target = target_features([own[16:17], own[17:18], own[18:19]])
    far_root = one_target(couple(far_ids(root_index)(0), s_ref, x_ref, target, ka))

    for q in range(2):
        source_eight([pair_rows(top_points, 8 * q + 2 * p, 8 * q + 2 * p + 1) for p in range(4)], s_ref, 8 * q)

    def parent(h, _):
        total = roots[8 * h][8:16]
        for n in range(1, 8):
            total = total + roots[8 * h + n][8:16]
        total = jnp.where(h == group, jnp.zeros_like(total), total)
        put_values(x_ref, h, values_from_tile(total))
        return 0

    lax.fori_loop(0, 16, parent, 0, unroll=2)
    target = target_features(rows_of(top_points, group))
    top_far = one_target(couple(list(range(16)), s_ref, x_ref, target, ka))

    raised = lifted(top_far, root_rows[0])
    gap = jnp.zeros((16, 32), f32)
    root = far_root + take(
        jnp.concatenate([raised[:16], gap, raised[16:], gap], axis=1), evens_odds_back()
    )
    raised = lifted(root, middle_rows[...].reshape(256, 128))
    for p in range(4):
        columns = slice(128 * p, 128 * p + 128)
        far_middle[:, columns] = far_middle[:, columns] + natural(raised, p)

    def one_middle(i, _):
        pair = far_middle[:, pl.ds(pl.multiple_of(i * 128, 128), 128)]
        for half in range(2):
            at = 16 * i + 8 * half
            raised = lifted(swap(pair) if half else pair, leaf_rows[pl.ds(at, 8)].reshape(256, 128))
            for p in range(4):
                columns = pl.ds(pl.multiple_of(i * 1024 + half * 512 + 128 * p, 128), 128)
                leaf = far[:, columns] + natural(raised, p)
                a = lifted(leaf, basis_rows[at + 2 * p])
                b = lifted(swap(leaf), basis_rows[at + 2 * p + 1])
                tree[:, columns] = near[:, columns] + jnp.concatenate([a[:16], a[16:], b[:16], b[16:]], axis=1)
        return 0

    lax.fori_loop(0, 4, one_middle, 0)
    permute_columns(tree, inverse, out, False)


def from_behind(block, distance):
    devices = range(lax.axis_size(both))
    return lax.ppermute(block, both, [(i - distance, i) for i in devices if i - distance in devices])


def exchange(x):
    return lax.all_to_all(x, both, split_axis=0, concat_axis=0, tiled=True)


def shards(
    values,
    coords,
    order,
    leaf_basis,
    leaf_transfer,
    middle_transfer,
    root_transfer,
    leaf_skeleton,
    middle_skeleton,
    root_skeleton,
    top_skeleton,
    leaf_far,
    middle_far,
    root_far,
    leaf_near,
    leaf_sends,
    middle_sends,
):
    tree, first_leaves, last_leaves = call(
        tree_order,
        "tree_order",
        (shape(24, 4096), shape(24, 512), shape(24, 512)),
        [VM, VM, VM],
        [pltpu.VMEM((24, 4096), f32)],
    )(values, coords, order.reshape(32, 128))
    before = from_behind(last_leaves, 1)
    after = from_behind(first_leaves, -1)
    packed = call(
        pack_skeletons,
        "pack_skeletons",
        shape(128, 16, 128),
        [SM, SM, VM, VM],
        [pltpu.VMEM((3, 64, 128), f32), pltpu.VMEM((3, 8, 128), f32)],
    )(leaf_sends, middle_sends, leaf_skeleton, middle_skeleton)
    skeletons = exchange(packed)

    outgoing, root_out, basis_rows, leaf_rows, middle_rows, root_rows = call(
        up_pass,
        "up_pass",
        (
            shape(128, 80, 128), shape(24, 128),
            shape(64, 32, 128), shape(64, 32, 128), shape(8, 32, 128), shape(1, 32, 128),
        ),
        [SM, SM, VM, VM, HBM, HBM, HBM, HBM],
        [
            pltpu.VMEM((16, 4096), f32),
            pltpu.VMEM((64, 8, 128), f32),
            pltpu.VMEM((8, 8, 128), f32),
            pltpu.VMEM((3, 1, 128), f32),
            pltpu.SemaphoreType.DMA((4, 32)),
        ],
        flops=8 * 10**9,
    )(
        leaf_sends, middle_sends, tree, root_skeleton,
        leaf_basis, leaf_transfer, middle_transfer, root_transfer,
    )
    outgoing, before, after = lax.optimization_barrier((outgoing, before, after))
    received = exchange(outgoing)
    roots = lax.all_gather(root_out[None], both, axis=0, tiled=True)

    kernels = [pltpu.VMEM((2, 1024, 256), bf16)] * 2
    near = call(
        near_field,
        "near_field",
        shape(16, 4096),
        [SM, VM, VM, VM],
        [
            pltpu.VMEM((24, 5120), f32),
            pltpu.VMEM((88, 64, 128), bf16),
            pltpu.VMEM((81, 2, 16, 128), bf16),
            pltpu.VMEM((2, 448, 256), bf16),
            pltpu.VMEM((2, 448, 256), bf16),
        ],
        flops=22 * 10**9,
    )(leaf_near.T, before, tree, after)
    inverse = pl.pallas_call(
        invert,
        name="invert",
        out_shape=shape(4096, kind=jnp.int32),
        in_specs=[SM],
        out_specs=SM,
        cost_estimate=pl.CostEstimate(flops=6 * 10**9, bytes_accessed=0, transcendentals=0),
    )(order).reshape(32, 128)
    leaf_table, middle_table = call(
        sources,
        "sources",
        (shape(1024, 64, 128, kind=bf16), shape(256, 64, 128, kind=bf16)),
        [VM],
        flops=16 * 10**9,
    )(skeletons)
    far = call(
        far_leaves,
        "far_leaves",
        shape(16, 4096),
        [SM, VM, HBM, HBM],
        [
            pltpu.VMEM((1024, 64, 128), bf16),
            pltpu.VMEM((128, 64, 128), f32),
            pltpu.VMEM((1024, 2, 16, 128), bf16),
            pltpu.VMEM((3, 64, 128), f32),
            *kernels,
            pltpu.SemaphoreType.DMA((5,)),
        ],
        flops=50 * 10**9,
    )(leaf_far, leaf_skeleton, received, leaf_table)
    return call(
        finish,
        "finish",
        shape(16, 4096),
        [SM, SM, VM, VM, VM, VM, VM, VM, VM, VM, VM, VM, VM, VM],
        [
            pltpu.VMEM((16, 512), f32),
            pltpu.VMEM((256, 2, 16, 128), bf16),
            pltpu.VMEM((128, 64, 128), bf16),
            *kernels,
            pltpu.VMEM((3, 8, 128), f32),
            pltpu.VMEM((3, 16, 128), f32),
            pltpu.VMEM((16, 4096), f32),
        ],
        flops=10 * 10**9,
    )(
        middle_far, root_far, received[:, 64:], middle_table, roots, middle_skeleton, top_skeleton,
        near, far, basis_rows, leaf_rows, middle_rows, root_rows, inverse,
    )


def solution(mesh):
    split = P(both, None)
    placed = (
        P(None, both),
        P(None, both),
        P(both),
        split,
        split,
        split,
        split,
        split,
        split,
        split,
        P(),
        split,
        split,
        split,
        split,
        P(both),
        P(both),
    )
    return jax.shard_map(
        shards, mesh=mesh, in_specs=placed, out_specs=P(None, both), check_vma=False
    )
```

```python
import math

import jax
import jax.numpy as jnp
from jax import lax
from jax.experimental import pallas as pl
from jax.experimental.pallas import tpu as pltpu
from jax.sharding import PartitionSpec as P

LEAF = 64
RANK = 64
RHS = 16
FEATS = 32
COLS = 4

both = ("gx", "gy")
f32 = jnp.float32
bf16 = jnp.bfloat16
log2e = 1.0 / math.log(2.0)
scale = math.sqrt(3.0) / 0.3 * log2e

VM = pl.BlockSpec(memory_space=pltpu.VMEM)
SM = pl.BlockSpec(memory_space=pltpu.SMEM)


def lanes(shape):
    return lax.broadcasted_iota(jnp.int32, shape, len(shape) - 1)


def swap(x):
    return pltpu.roll(x, 64, axis=x.ndim - 1)


def halves(x):
    high = x.astype(bf16)
    return high, (x - high.astype(f32)).astype(bf16)


def thirds(x):
    first = x.astype(bf16).astype(f32)
    rest = x - first
    second = rest.astype(bf16).astype(f32)
    return first, second, (rest - second).astype(bf16).astype(f32)


NN = (((1,), (0,)), ((), ()))
NT = (((1,), (1,)), ((), ()))


def dot(a, b, dims=NN):
    return lax.dot_general(a, b, dims, preferred_element_type=f32)


def dot3(a, b, dims=NN):
    ah, al = halves(a)
    bh, bl = halves(b)
    rows = a.shape[0]
    first = dot(jnp.concatenate([ah, al], axis=0), bh, dims)
    return first[:rows] + first[rows:] + dot(ah, bl, dims)


def stacked(rows, norm_row, one_row, factor):
    x, y, z = [(jnp.broadcast_to(r, (8, 128)) - 0.5) * scale for r in rows]
    norm = x * x + y * y + z * z
    sub = lax.broadcasted_iota(jnp.int32, (8, 128), 0)
    out = jnp.where(sub < 2, x, jnp.where(sub < 4, y, z)) * factor
    out = jnp.where(sub == norm_row, norm, out)
    return jnp.where(sub == one_row, 1.0, out), sub


def target_features(rows):
    base, sub = stacked(rows, 6, 7, -2.0)
    first, second, third = thirds(base)
    even = sub % 2 == 0
    last = jnp.where(sub == 7, 1.0, jnp.where(even, third, second))
    return jnp.concatenate(
        [first, jnp.where(even, second, first), last, jnp.zeros_like(first)], axis=0
    ).astype(bf16)


def source_features(rows):
    base, sub = stacked(rows, 7, 6, 1.0)
    first, second, third = thirds(base)
    even = sub % 2 == 0
    norm = sub == 7
    return jnp.concatenate(
        [
            jnp.where(even | norm, first, second),
            jnp.where(even, first, jnp.where(norm, second, third)),
            jnp.where(even, first, jnp.where(norm, third, second)),
            jnp.zeros_like(first),
        ],
        axis=0,
    ).astype(bf16)


def source_row(v, column):
    return (v & -8) + ((v & 1) << 2) + ((column - (v >> 1)) & 3)


def source_eight(pairs, s_ref, at):
    tall = jnp.concatenate([source_features(rows) for rows in pairs], axis=0)
    eye = (lax.broadcasted_iota(jnp.int32, (128, 128), 0) == lanes((128, 128))).astype(f32).astype(bf16)
    turned = dot(eye, tall, NT)
    for k in range(COLS):
        moved = (turned if k == 0 else pltpu.roll(turned, FEATS * k, axis=1)).astype(bf16)
        s_ref[at + k] = moved[:64]
        s_ref[at + COLS + k] = moved[64:]


def put_values(x_ref, at, wide):
    high, low = halves(wide)
    x_ref[at, 0] = high
    x_ref[at, 1] = low


def values_from_tile(tile):
    left = lanes(tile.shape) < 64
    other = swap(tile)
    return jnp.concatenate([jnp.where(left, tile, other), jnp.where(left, other, tile)], axis=0)


def twice(rows, upper):
    left = lanes(rows.shape) < 64
    return jnp.where(left, swap(rows), rows) if upper else jnp.where(left, rows, swap(rows))


def make_kernel(ids, start, s_ref, spread, k_ref):
    stop = min(start + 4, len(ids) // COLS)
    group = lanes((64, 128)) // FEATS
    stack = []
    for g in range(start, stop):
        quad = ids[4 * g : 4 * g + 4]
        s = s_ref[source_row(quad[3], 3)]
        for c in (2, 1, 0):
            s = jnp.where(group <= c, s_ref[source_row(quad[c], c)], s)
        stack.append(s)
    square = jnp.maximum(dot(jnp.concatenate(stack, axis=0), spread), 1e-30)
    u = square * lax.rsqrt(square)
    high, low = halves((u + log2e) * jnp.exp2(-u))
    k_ref[0, 64 * start : 64 * stop] = high
    k_ref[1, 64 * start : 64 * stop] = low


def apply_kernel(ids, start, x_ref, k_ref, total):
    count = len(ids) // COLS
    stop = min(start + 4, count)
    near = lanes((16, 128)) < 64

    def joined(part):
        out = []
        for c in range(COLS):
            pieces = []
            for g in range(start, stop, 2):
                first = x_ref[ids[4 * g + c], part]
                if g + 1 < count:
                    pieces.append(jnp.where(near, first, x_ref[ids[4 * g + 4 + c], part]))
                else:
                    pieces.append(first[:, :64])
            out.append(jnp.concatenate(pieces, axis=1))
        return jnp.concatenate(out, axis=0)

    x_high, x_low = joined(0), joined(1)
    rows = slice(64 * start, 64 * stop)
    first = dot(jnp.concatenate([x_high, x_low], axis=0), k_ref[0, rows])
    second = dot(x_high, k_ref[1, rows])
    return (first, second) if total is None else (total[0] + first, total[1] + second)


def summed(total):
    rows = 16 * COLS
    whole = total[0][:rows] + total[0][rows:] + total[1]
    return whole[:16, :128] + whole[32:48, 128:], whole[16:32, :128] + whole[48:, 128:]


def spread_target(target):
    zero = jnp.zeros_like(target)
    left = lanes(target.shape) < 64
    lower = jnp.where(left, target, zero)
    upper = jnp.where(left, zero, target)
    return jnp.concatenate(
        [
            jnp.concatenate([lower, upper, zero, zero], axis=0),
            jnp.concatenate([zero, zero, lower, upper], axis=0),
        ],
        axis=1,
    )


def couple(parts, s_ref, x_ref, k_refs):
    for (ids, target), k_ref in zip(parts, k_refs):
        spread = spread_target(target)
        for q in range(0, len(ids) // COLS, 4):
            make_kernel(ids, q, s_ref, spread, k_ref)
    sums = []
    for (ids, _), k_ref in zip(parts, k_refs):
        total = None
        for q in range(0, len(ids) // COLS, 4):
            total = apply_kernel(ids, q, x_ref, k_ref, total)
        sums.append(one_target(summed(total)))
    return sums


def couple_all(count, ids, target, s_ref, x_ref, out, ka, kb, unroll=1):
    def advance(new, k_new, old, k_old):
        made, used = ids(new), ids(old)
        spread = spread_target(target(new))
        total = None
        for q in range(0, len(made) // COLS, 4):
            make_kernel(made, q, s_ref, spread, k_new)
            total = apply_kernel(used, q, x_ref, k_old, total)
        return summed(total)

    first = ids(0)
    spread = spread_target(target(0))
    for q in range(0, len(first) // COLS, 4):
        make_kernel(first, q, s_ref, spread, ka)

    def pair(i, _):
        lower = advance(2 * i + 1, kb, 2 * i, ka)
        upper = advance(jnp.minimum(2 * i + 2, count - 1), ka, 2 * i + 1, kb)
        out[:, pl.ds(pl.multiple_of(i * 128, 128), 128)] = two_targets(lower, upper)
        return 0

    lax.fori_loop(0, count // 2, pair, 0, unroll=unroll)


def two_targets(first, second):
    left = lanes(first[0].shape) < 64
    return (
        jnp.where(left, first[0], second[1]) + swap(jnp.where(left, second[0], first[1]))
    ) * (1.0 / log2e)


def one_target(pair):
    return (pair[0] + swap(pair[1])) * (1.0 / log2e)


HBM = pl.BlockSpec(memory_space=pl.ANY)


def call(kernel, name, out, in_specs, scratch=(), flops=0, data=0, limit=60, outs=None):
    return pl.pallas_call(
        kernel,
        name=name,
        out_shape=out,
        in_specs=in_specs,
        out_specs=jax.tree.map(lambda _: VM, out) if outs is None else outs,
        scratch_shapes=list(scratch),
        cost_estimate=pl.CostEstimate(flops=flops, bytes_accessed=data, transcendentals=0),
        compiler_params=pltpu.CompilerParams(vmem_limit_bytes=limit * 2**20),
    )


def shape(*dims, kind=f32):
    return jax.ShapeDtypeStruct(dims, kind)


def put_rows(skeleton, table):
    first = skeleton[:, :128]
    table[0] = twice(first, False)
    table[1] = twice(first, True)
    last = skeleton[:, 128:]
    table[2] = jnp.concatenate([last, last], axis=1)


def rows_of(table, at):
    return [table[j, pl.ds(at, 1), :] for j in range(3)]


def pair_rows(table, a, b):
    left = lanes((1, 128)) < 64
    return [jnp.where(left, x, y) for x, y in zip(rows_of(table, a), rows_of(table, b))]


PAIR_ROWS = (0, 3, 8, 11)
MIDDLE_ROWS = (6, 7, 14)


def pack_skeletons(
    sends, middle_sends, leaf_skeleton, middle_skeleton,
    out, leaf_table, middle_table, early, late, middles, lasts,
):
    put_rows(leaf_skeleton, leaf_table)
    put_rows(middle_skeleton, middle_table)

    def spot(l, _):
        tile = jnp.concatenate(rows_of(leaf_table, l) + [jnp.zeros((5, 128), f32)], axis=0)
        early[l] = tile
        late[l] = pltpu.roll(tile, 3, axis=0)
        return 0

    lax.fori_loop(0, 64, spot, 0, unroll=4)
    for m in range(8):
        x, y, z = rows_of(middle_table, m)
        middles[m] = jnp.concatenate([jnp.zeros((6, 128), f32), x, y], axis=0)
        lasts[m] = jnp.concatenate([jnp.zeros((6, 128), f32), z, jnp.zeros((1, 128), f32)], axis=0)
    left = lanes((8, 128)) < 64

    def body(b, _):
        slot = [sends[b * 8 + c] for c in range(8)]
        m, n = middle_sends[2 * b], middle_sends[2 * b + 1]
        for half, third in ((0, middles), (1, lasts)):
            c = 4 * half
            first = early[slot[c]] + late[slot[c + 2]] + third[m]
            second = early[slot[c + 1]] + late[slot[c + 3]] + third[n]
            out[b, 8 * half : 8 * half + 8] = jnp.where(left, first, second)
        return 0

    lax.fori_loop(0, 128, body, 0, unroll=4)


def take(x, index):
    pieces = [
        jnp.take_along_axis(x[r : r + 8], index, axis=1, mode="promise_in_bounds")
        for r in range(0, x.shape[0], 8)
    ]
    return pieces[0] if len(pieces) == 1 else jnp.concatenate(pieces, axis=0)


def even_first():
    i = lanes((8, 128))
    return (i & 64) + 2 * (i & 31) + ((i >> 5) & 1)


def evens_odds():
    i = lanes((8, 128))
    return ((i & 32) << 1) + 2 * (i & 31) + (i >> 6)


def evens_odds_back():
    i = lanes((8, 128))
    return ((i & 1) << 6) + ((i >> 6) << 5) + ((i & 63) >> 1)


def permute_columns(source, index, out, halved, tiles=(0, 32), shift=0):
    height = source.shape[0] // 8

    def body(j, _):
        where = jnp.broadcast_to(index[pl.ds(j, 1), :], (8, 128))
        if halved:
            where = take(where, even_first())
        inside = where & 127
        tile = where >> 7
        found = [jnp.zeros((8, 128), f32)] * height
        for i in range(32):
            match = tile == i
            for r in range(height):
                piece = source[8 * r : 8 * r + 8, 128 * i : 128 * i + 128]
                found[r] = jnp.where(match, take(piece, inside), found[r])
        for r in range(height):
            out[8 * r : 8 * r + 8, pl.ds(pl.multiple_of((j + shift) * 128, 128), 128)] = found[r]
        return 0

    lax.fori_loop(*tiles, body, 0, unroll=2)


def pair_halves(result):
    return result[:16] + swap(result[16:])


def as_tile(x):
    left = lanes((8, 128)) < 64
    return jnp.where(left, x[:8], swap(x[8:]))


def side_by_side(a, b):
    return jnp.where(lanes(a.shape) < 64, a, swap(b))


def even_odd_rows(blocks):
    left = lanes((16, 128)) < 64
    even, odd = [], []
    for v, w in zip(blocks[::2], blocks[1::2]):
        even.append(jnp.where(left, v, swap(w)))
        odd.append(jnp.where(left, swap(v), w))
    return jnp.concatenate([jnp.concatenate(even, axis=1), jnp.concatenate(odd, axis=1)], axis=0)


def pad_points(coords, source):
    source[0:3] = coords[...]
    source[3:8] = jnp.zeros((5, 4096), f32)


def tree_order(values, coords, order, tree, first_leaves, last_leaves, source):
    pad_points(coords, source)
    permute_columns(values, order, tree, True)
    permute_columns(source, order, first_leaves.at[16:24], True, (0, 4))
    permute_columns(source, order, last_leaves.at[16:24], True, (28, 32), -28)
    first_leaves[0:16] = tree[:, :512]
    last_leaves[0:16] = tree[:, 3584:]


def up_pass(
    sends, middle_sends, tree, root_skeleton, basis, leaf_maps, middle_maps, root_maps,
    out, root_out, basis_rows, leaf_rows, middle_rows, root_rows,
    message, split, tiles, middle_tiles, root_table, sems, out_sems,
):
    copies = []
    for m, (whole, rows) in enumerate(
        ((basis, basis_rows), (leaf_maps, leaf_rows), (middle_maps, middle_rows), (root_maps, root_rows))
    ):
        copies.append(
            [
                pltpu.make_async_copy(whole.at[:, pl.ds(128 * t, 128)], rows.at[:, t, :], sems.at[m, t])
                for t in range(32)
            ]
        )
    for group in copies:
        for copy in group:
            copy.start()
    for copy in copies[0]:
        copy.wait()

    def leaf_pair(i, _):
        columns = pl.ds(pl.multiple_of(i * 128, 128), 128)
        x = tree[:, columns]
        a = pair_halves(dot3(jnp.concatenate([x[:, :32], x[:, 32:64]], axis=0), basis_rows[2 * i]))
        b = pair_halves(dot3(jnp.concatenate([x[:, 64:96], x[:, 96:]], axis=0), basis_rows[2 * i + 1]))
        split[:, columns] = take(side_by_side(a, b), evens_odds())
        tiles[2 * i] = as_tile(a)
        tiles[2 * i + 1] = as_tile(b)
        return 0

    lax.fori_loop(0, 32, leaf_pair, 0, unroll=4)

    def slots(b, _):
        for c in range(8):
            message[b, 8 * c : 8 * c + 8] = tiles[sends[8 * b + c]]
        return 0

    sent = []
    for p in range(4):
        lax.fori_loop(32 * p, 32 * p + 32, slots, 0, unroll=2)
        part = (pl.ds(32 * p, 32), pl.ds(0, 64))
        sent.append(pltpu.make_async_copy(message.at[part], out.at[part], out_sems.at[p]))
        sent[-1].start()
    for group in copies[1:]:
        for copy in group:
            copy.wait()
    middles = []
    for j in range(8):
        blocks = [split[:, 512 * j + 128 * p : 512 * j + 128 * p + 128] for p in range(4)]
        part = pair_halves(dot3(even_odd_rows(blocks), leaf_rows[8 * j : 8 * j + 8].reshape(256, 128)))
        middle_tiles[j] = as_tile(part)
        middles.append(part)
    blocks = [take(side_by_side(middles[2 * p], middles[2 * p + 1]), evens_odds()) for p in range(4)]
    root = pair_halves(dot3(even_odd_rows(blocks), middle_rows[...].reshape(256, 128)))
    turned = take(root, evens_odds())
    top = pair_halves(dot3(jnp.concatenate([turned[:, :32], turned[:, 64:96]], axis=0), root_rows[0]))
    put_rows(root_skeleton, root_table)
    root_out[0:8] = as_tile(root)
    root_out[8:16] = as_tile(top)
    root_out[16:24] = jnp.concatenate(rows_of(root_table, 0) + [jnp.zeros((5, 128), f32)], axis=0)

    def middle_slots(b, _):
        for c in range(2):
            message[b, 64 + 8 * c : 72 + 8 * c] = middle_tiles[middle_sends[2 * b + c]]
        return 0

    lax.fori_loop(0, 128, middle_slots, 0, unroll=4)
    part = (pl.ds(0, 128), pl.ds(64, 16))
    sent.append(pltpu.make_async_copy(message.at[part], out.at[part], out_sems.at[4]))
    sent[-1].start()
    for copy in sent:
        copy.wait()


def invert(order, inverse):
    def body(b, _):
        for p in range(64):
            inverse[order[b * 64 + p]] = b * 64 + (p % 2) * 32 + p // 2
        return 0

    lax.fori_loop(0, 64, body, 0)


def near_field(index, before, tree, after, coords, order, out, window, source, s_ref, x_ref, ka, kb):
    window[:, :512] = before[...]
    window[0:16, 512:4608] = tree[...]
    window[:, 4608:] = after[...]
    pad_points(coords, source)
    permute_columns(source, order, window.at[16:24], True, (0, 32), 4)
    for k in range(8):
        s_ref[80 + k] = jnp.zeros((64, 128), bf16)
    x_ref[80] = jnp.zeros((2, 16, 128), bf16)

    def prepare(i, _):
        pairs = []
        for p in range(4):
            block = window[:, pl.ds(pl.multiple_of(i * 512 + p * 128, 128), 128)]
            pairs.append([block[16:17], block[17:18], block[18:19]])
            put_values(x_ref, 8 * i + 2 * p, twice(block[:16], False))
            put_values(x_ref, 8 * i + 2 * p + 1, twice(block[:16], True))
        source_eight(pairs, s_ref, 8 * i)
        return 0

    lax.fori_loop(0, 10, prepare, 0, unroll=2)

    def ids(l):
        return [l + 8] + [index[f, l] for f in range(26)] + [80]

    def target(l):
        block = window[16:24, pl.ds(pl.multiple_of((l >> 1) * 128 + 512, 128), 128)]
        left = lanes(block.shape) < 64
        points = jnp.where(left == (l % 2 == 0), block, swap(block))
        return target_features([points[0:1], points[1:2], points[2:3]])

    couple_all(64, ids, target, s_ref, x_ref, out, ka, kb, unroll=2)


def sources(received, s_ref, middle_ref):
    def prepare(q, _):
        block = received[q]
        source_eight([[block[r + j : r + j + 1] for j in range(3)] for r in PAIR_ROWS], s_ref, q * 8)
        return 0

    lax.fori_loop(0, 128, prepare, 0, unroll=4)

    def middle(q, _):
        source_eight(
            [[received[4 * q + p, r : r + 1] for r in MIDDLE_ROWS] for p in range(4)], middle_ref, q * 8
        )
        return 0

    lax.fori_loop(0, 32, middle, 0, unroll=4)


def far_ids(index):
    return lambda l: [index[l, f] for f in range(64)]


def far_leaves(index, skeleton, received, table, out, s_ref, tiles, x_ref, rows, ka, kb, sems):
    parts = [
        pltpu.make_async_copy(
            received.at[pl.ds(32 * p, 32), pl.ds(0, 64), :], tiles.at[pl.ds(32 * p, 32)], sems.at[p]
        )
        for p in range(4)
    ]
    for part in parts:
        part.start()
    loaded = pltpu.make_async_copy(table, s_ref, sems.at[4])
    loaded.start()
    put_rows(skeleton, rows)
    for p in range(4):
        parts[p].wait()

        def prepare(q, _):
            for c in range(8):
                put_values(x_ref, 8 * q + c, values_from_tile(tiles[q, 8 * c : 8 * c + 8]))
            return 0

        lax.fori_loop(32 * p, 32 * p + 32, prepare, 0, unroll=2)
    loaded.wait()
    couple_all(
        64, far_ids(index), lambda l: target_features(rows_of(rows, l)), s_ref, x_ref, out, ka, kb, 2
    )


def lifted(x, rows):
    left = lanes(x.shape) < 64
    zero = jnp.zeros_like(x)
    wide = jnp.concatenate([jnp.where(left, x, zero), jnp.where(left, zero, swap(x))], axis=0)
    return dot3(wide, rows, NT)


def natural(result, p):
    part = slice(64 * p, 64 * p + 64)
    return take(jnp.concatenate([result[:16, part], result[16:, part]], axis=1), evens_odds_back())


def finish(
    middle_index, root_index, received, middle_table_far, roots_far, middle_skeleton, top_skeleton,
    near, far, basis_far, leaf_far, middle_rows, root_rows, inverse,
    out, far_middle, values, middle_table, roots, basis_rows, leaf_rows,
    x_ref, s_ref, ka, kb, middle_points, top_points, tree, sems,
):
    loads = [
        pltpu.make_async_copy(source, target, sems.at[i])
        for i, (source, target) in enumerate(
            (
                (received.at[pl.ds(0, 128), pl.ds(64, 16)], values),
                (middle_table_far, middle_table),
                (roots_far, roots),
                (leaf_far, leaf_rows),
                (basis_far, basis_rows),
            )
        )
    ]
    for load in loads:
        load.start()
    left = lanes((1, 128)) < 64
    put_rows(middle_skeleton, middle_points)
    put_rows(top_skeleton, top_points)
    group = lax.axis_index("gx")
    loads[0].wait()

    def middle_values(q, _):
        for c in range(2):
            put_values(x_ref, 2 * q + c, values_from_tile(values[q, 8 * c : 8 * c + 8]))
        return 0

    lax.fori_loop(0, 128, middle_values, 0, unroll=4)
    loads[1].wait()
    couple_all(
        8, far_ids(middle_index), lambda l: target_features(rows_of(middle_points, l)),
        middle_table, x_ref, far_middle, ka, kb,
    )
    loads[2].wait()

    def root_sources(q, _):
        pairs = []
        for p in range(4):
            a, b = roots[8 * q + 2 * p], roots[8 * q + 2 * p + 1]
            pairs.append([jnp.where(left, a[16 + j : 17 + j], b[16 + j : 17 + j]) for j in range(3)])
            put_values(x_ref, 8 * q + 2 * p, values_from_tile(a[:8]))
            put_values(x_ref, 8 * q + 2 * p + 1, values_from_tile(b[:8]))
        source_eight(pairs, s_ref, 8 * q)
        return 0

    lax.fori_loop(0, 16, root_sources, 0, unroll=4)
    for q in range(2):
        source_eight(
            [pair_rows(top_points, 8 * q + 2 * p, 8 * q + 2 * p + 1) for p in range(4)], s_ref, 128 + 8 * q
        )

    def parent(h, _):
        total = roots[8 * h][8:16]
        for n in range(1, 8):
            total = total + roots[8 * h + n][8:16]
        total = jnp.where(h == group, jnp.zeros_like(total), total)
        put_values(x_ref, 128 + h, values_from_tile(total))
        return 0

    lax.fori_loop(0, 16, parent, 0, unroll=4)
    own = roots[lax.axis_index(both)]
    far_root, top_far = couple(
        [
            (far_ids(root_index)(0), target_features([own[16:17], own[17:18], own[18:19]])),
            (list(range(128, 144)), target_features(rows_of(top_points, group))),
        ],
        s_ref,
        x_ref,
        (ka, kb),
    )
    loads[3].wait()
    loads[4].wait()

    raised = lifted(top_far, root_rows[0])
    gap = jnp.zeros((16, 32), f32)
    root = far_root + take(
        jnp.concatenate([raised[:16], gap, raised[16:], gap], axis=1), evens_odds_back()
    )
    raised = lifted(root, middle_rows[...].reshape(256, 128))
    for p in range(4):
        columns = slice(128 * p, 128 * p + 128)
        far_middle[:, columns] = far_middle[:, columns] + natural(raised, p)

    def one_middle(i, _):
        pair = far_middle[:, pl.ds(pl.multiple_of(i * 128, 128), 128)]
        for half in range(2):
            at = 16 * i + 8 * half
            raised = lifted(swap(pair) if half else pair, leaf_rows[pl.ds(at, 8)].reshape(256, 128))
            for p in range(4):
                columns = pl.ds(pl.multiple_of(i * 1024 + half * 512 + 128 * p, 128), 128)
                leaf = far[:, columns] + natural(raised, p)
                a = lifted(leaf, basis_rows[at + 2 * p])
                b = lifted(swap(leaf), basis_rows[at + 2 * p + 1])
                tree[:, columns] = near[:, columns] + jnp.concatenate([a[:16], a[16:], b[:16], b[16:]], axis=1)
        return 0

    lax.fori_loop(0, 4, one_middle, 0, unroll=2)
    permute_columns(tree, inverse, out, False)


def from_behind(block, distance):
    devices = range(lax.axis_size(both))
    return lax.ppermute(block, both, [(i - distance, i) for i in devices if i - distance in devices])


def exchange(x):
    return lax.all_to_all(x, both, split_axis=0, concat_axis=0, tiled=True)


def shards(
    values,
    coords,
    order,
    leaf_basis,
    leaf_transfer,
    middle_transfer,
    root_transfer,
    leaf_skeleton,
    middle_skeleton,
    root_skeleton,
    top_skeleton,
    leaf_far,
    middle_far,
    root_far,
    leaf_near,
    leaf_sends,
    middle_sends,
):
    order_rows = order.reshape(32, 128)
    tree, first_leaves, last_leaves = call(
        tree_order,
        "tree_order",
        (shape(16, 4096), shape(24, 512), shape(24, 512)),
        [VM, VM, VM],
        [pltpu.VMEM((8, 4096), f32)],
    )(values, coords, order_rows)
    before = from_behind(last_leaves, 1)
    after = from_behind(first_leaves, -1)
    packed = call(
        pack_skeletons,
        "pack_skeletons",
        shape(128, 16, 128),
        [SM, SM, VM, VM],
        [
            pltpu.VMEM((3, 64, 128), f32),
            pltpu.VMEM((3, 8, 128), f32),
            pltpu.VMEM((64, 8, 128), f32),
            pltpu.VMEM((64, 8, 128), f32),
            pltpu.VMEM((8, 8, 128), f32),
            pltpu.VMEM((8, 8, 128), f32),
        ],
    )(leaf_sends, middle_sends, leaf_skeleton, middle_skeleton)
    skeletons = exchange(packed)

    outgoing, root_out, basis_rows, leaf_rows, middle_rows, root_rows = call(
        up_pass,
        "up_pass",
        (
            shape(128, 80, 128), shape(24, 128),
            shape(64, 32, 128), shape(64, 32, 128), shape(8, 32, 128), shape(1, 32, 128),
        ),
        [SM, SM, VM, VM, HBM, HBM, HBM, HBM],
        [
            pltpu.VMEM((128, 80, 128), f32),
            pltpu.VMEM((16, 4096), f32),
            pltpu.VMEM((64, 8, 128), f32),
            pltpu.VMEM((8, 8, 128), f32),
            pltpu.VMEM((3, 1, 128), f32),
            pltpu.SemaphoreType.DMA((4, 32)),
            pltpu.SemaphoreType.DMA((5,)),
        ],
        flops=8 * 10**9,
        outs=(HBM, VM, VM, VM, VM, VM),
    )(
        leaf_sends, middle_sends, tree, root_skeleton,
        leaf_basis, leaf_transfer, middle_transfer, root_transfer,
    )
    outgoing, before, after = lax.optimization_barrier((outgoing, before, after))
    received = exchange(outgoing)
    roots = lax.all_gather(root_out[None], both, axis=0, tiled=True)

    kernels = [pltpu.VMEM((2, 1024, 256), bf16)] * 2
    near = call(
        near_field,
        "near_field",
        shape(16, 4096),
        [SM, VM, VM, VM, VM, VM],
        [
            pltpu.VMEM((24, 5120), f32),
            pltpu.VMEM((8, 4096), f32),
            pltpu.VMEM((88, 64, 128), bf16),
            pltpu.VMEM((81, 2, 16, 128), bf16),
            pltpu.VMEM((2, 448, 256), bf16),
            pltpu.VMEM((2, 448, 256), bf16),
        ],
        flops=22 * 10**9,
    )(leaf_near.T, before, tree, after, coords, order_rows)
    inverse = pl.pallas_call(
        invert,
        name="invert",
        out_shape=shape(4096, kind=jnp.int32),
        in_specs=[SM],
        out_specs=SM,
        cost_estimate=pl.CostEstimate(flops=6 * 10**9, bytes_accessed=0, transcendentals=0),
    )(order).reshape(32, 128)
    leaf_table, middle_table = call(
        sources,
        "sources",
        (shape(1024, 64, 128, kind=bf16), shape(256, 64, 128, kind=bf16)),
        [VM],
        flops=16 * 10**9,
    )(skeletons)
    far = call(
        far_leaves,
        "far_leaves",
        shape(16, 4096),
        [SM, VM, HBM, HBM],
        [
            pltpu.VMEM((1024, 64, 128), bf16),
            pltpu.VMEM((128, 64, 128), f32),
            pltpu.VMEM((1024, 2, 16, 128), bf16),
            pltpu.VMEM((3, 64, 128), f32),
            *kernels,
            pltpu.SemaphoreType.DMA((5,)),
        ],
        flops=50 * 10**9,
    )(leaf_far, leaf_skeleton, received, leaf_table)
    return call(
        finish,
        "finish",
        shape(16, 4096),
        [SM, SM, HBM, HBM, HBM, VM, VM, VM, VM, HBM, HBM, VM, VM, VM],
        [
            pltpu.VMEM((16, 512), f32),
            pltpu.VMEM((128, 16, 128), f32),
            pltpu.VMEM((256, 64, 128), bf16),
            pltpu.VMEM((128, 24, 128), f32),
            pltpu.VMEM((64, 32, 128), f32),
            pltpu.VMEM((64, 32, 128), f32),
            pltpu.VMEM((256, 2, 16, 128), bf16),
            pltpu.VMEM((144, 64, 128), bf16),
            *kernels,
            pltpu.VMEM((3, 8, 128), f32),
            pltpu.VMEM((3, 16, 128), f32),
            pltpu.VMEM((16, 4096), f32),
            pltpu.SemaphoreType.DMA((5,)),
        ],
        flops=10 * 10**9,
    )(
        middle_far, root_far, received, middle_table, roots, middle_skeleton, top_skeleton,
        near, far, basis_rows, leaf_rows, middle_rows, root_rows, inverse,
    )


def solution(mesh):
    split = P(both, None)
    placed = (
        P(None, both),
        P(None, both),
        P(both),
        split,
        split,
        split,
        split,
        split,
        split,
        split,
        P(),
        split,
        split,
        split,
        split,
        P(both),
        P(both),
    )
    return jax.shard_map(
        shards, mesh=mesh, in_specs=placed, out_specs=P(None, both), check_vma=False
    )
```

```python
import math

import jax
import jax.numpy as jnp
from jax import lax
from jax.experimental import pallas as pl
from jax.experimental.pallas import tpu as pltpu
from jax.sharding import PartitionSpec as P

LEAF = 64
RANK = 64
RHS = 16
FEATS = 32
COLS = 4

both = ("gx", "gy")
f32 = jnp.float32
bf16 = jnp.bfloat16
log2e = 1.0 / math.log(2.0)
scale = math.sqrt(3.0) / 0.3 * log2e

VM = pl.BlockSpec(memory_space=pltpu.VMEM)
SM = pl.BlockSpec(memory_space=pltpu.SMEM)


def lanes(shape):
    return lax.broadcasted_iota(jnp.int32, shape, len(shape) - 1)


def swap(x):
    return pltpu.roll(x, 64, axis=x.ndim - 1)


def halves(x):
    high = x.astype(bf16)
    return high, (x - high.astype(f32)).astype(bf16)


def thirds(x):
    first = x.astype(bf16).astype(f32)
    rest = x - first
    second = rest.astype(bf16).astype(f32)
    return first, second, (rest - second).astype(bf16).astype(f32)


NN = (((1,), (0,)), ((), ()))
NT = (((1,), (1,)), ((), ()))


def dot(a, b, dims=NN):
    return lax.dot_general(a, b, dims, preferred_element_type=f32)


def dot3(a, b, dims=NN):
    ah, al = halves(a)
    bh, bl = halves(b)
    rows = a.shape[0]
    first = dot(jnp.concatenate([ah, al], axis=0), bh, dims)
    return first[:rows] + first[rows:] + dot(ah, bl, dims)


def stacked(rows, norm_row, one_row, factor):
    x, y, z = [(jnp.broadcast_to(r, (8, 128)) - 0.5) * scale for r in rows]
    norm = x * x + y * y + z * z
    sub = lax.broadcasted_iota(jnp.int32, (8, 128), 0)
    out = jnp.where(sub < 2, x, jnp.where(sub < 4, y, z)) * factor
    out = jnp.where(sub == norm_row, norm, out)
    return jnp.where(sub == one_row, 1.0, out), sub


def target_features(rows):
    base, sub = stacked(rows, 6, 7, -2.0)
    first, second, third = thirds(base)
    even = sub % 2 == 0
    last = jnp.where(sub == 7, 1.0, jnp.where(even, third, second))
    return jnp.concatenate(
        [first, jnp.where(even, second, first), last, jnp.zeros_like(first)], axis=0
    ).astype(bf16)


def source_features(rows):
    base, sub = stacked(rows, 7, 6, 1.0)
    first, second, third = thirds(base)
    even = sub % 2 == 0
    norm = sub == 7
    return jnp.concatenate(
        [
            jnp.where(even | norm, first, second),
            jnp.where(even, first, jnp.where(norm, second, third)),
            jnp.where(even, first, jnp.where(norm, third, second)),
            jnp.zeros_like(first),
        ],
        axis=0,
    ).astype(bf16)


def source_row(v, column):
    return (v & -8) + ((v & 1) << 2) + ((column - (v >> 1)) & 3)


def source_eight(pairs, s_ref, at):
    tall = jnp.concatenate([source_features(rows) for rows in pairs], axis=0)
    eye = (lax.broadcasted_iota(jnp.int32, (128, 128), 0) == lanes((128, 128))).astype(f32).astype(bf16)
    turned = dot(eye, tall, NT)
    for k in range(COLS):
        moved = (turned if k == 0 else pltpu.roll(turned, FEATS * k, axis=1)).astype(bf16)
        s_ref[at + k] = moved[:64]
        s_ref[at + COLS + k] = moved[64:]


def put_values(x_ref, at, wide):
    high, low = halves(wide)
    x_ref[at, 0] = high
    x_ref[at, 1] = low


def values_from_tile(tile):
    left = lanes(tile.shape) < 64
    other = swap(tile)
    return jnp.concatenate([jnp.where(left, tile, other), jnp.where(left, other, tile)], axis=0)


def twice(rows, upper):
    left = lanes(rows.shape) < 64
    return jnp.where(left, swap(rows), rows) if upper else jnp.where(left, rows, swap(rows))


def make_kernel(ids, start, s_ref, spread, k_ref):
    stop = min(start + 4, len(ids) // COLS)
    group = lanes((64, 128)) // FEATS
    stack = []
    for g in range(start, stop):
        quad = ids[4 * g : 4 * g + 4]
        s = s_ref[source_row(quad[3], 3)]
        for c in (2, 1, 0):
            s = jnp.where(group <= c, s_ref[source_row(quad[c], c)], s)
        stack.append(s)
    square = jnp.maximum(dot(jnp.concatenate(stack, axis=0), spread), 1e-30)
    u = square * lax.rsqrt(square)
    high, low = halves((u + log2e) * jnp.exp2(-u))
    k_ref[0, 64 * start : 64 * stop] = high
    k_ref[1, 64 * start : 64 * stop] = low


def apply_kernel(ids, start, x_ref, k_ref, total):
    count = len(ids) // COLS
    stop = min(start + 4, count)
    near = lanes((16, 128)) < 64

    def joined(part):
        out = []
        for c in range(COLS):
            pieces = []
            for g in range(start, stop, 2):
                first = x_ref[ids[4 * g + c], part]
                if g + 1 < count:
                    pieces.append(jnp.where(near, first, x_ref[ids[4 * g + 4 + c], part]))
                else:
                    pieces.append(first[:, :64])
            out.append(jnp.concatenate(pieces, axis=1))
        return jnp.concatenate(out, axis=0)

    x_high, x_low = joined(0), joined(1)
    rows = slice(64 * start, 64 * stop)
    first = dot(jnp.concatenate([x_high, x_low], axis=0), k_ref[0, rows])
    second = dot(x_high, k_ref[1, rows])
    return (first, second) if total is None else (total[0] + first, total[1] + second)


def summed(total):
    rows = 16 * COLS
    whole = total[0][:rows] + total[0][rows:] + total[1]
    return whole[:16, :128] + whole[32:48, 128:], whole[16:32, :128] + whole[48:, 128:]


def spread_target(target):
    zero = jnp.zeros_like(target)
    left = lanes(target.shape) < 64
    lower = jnp.where(left, target, zero)
    upper = jnp.where(left, zero, target)
    return jnp.concatenate(
        [
            jnp.concatenate([lower, upper, zero, zero], axis=0),
            jnp.concatenate([zero, zero, lower, upper], axis=0),
        ],
        axis=1,
    )


def couple(parts, s_ref, x_ref, k_refs):
    for (ids, target), k_ref in zip(parts, k_refs):
        spread = spread_target(target)
        for q in range(0, len(ids) // COLS, 4):
            make_kernel(ids, q, s_ref, spread, k_ref)
    sums = []
    for (ids, _), k_ref in zip(parts, k_refs):
        total = None
        for q in range(0, len(ids) // COLS, 4):
            total = apply_kernel(ids, q, x_ref, k_ref, total)
        sums.append(one_target(summed(total)))
    return sums


def couple_all(count, ids, target, s_ref, x_ref, out, ka, kb, unroll=1, beside=None):
    def advance(new, k_new, old, k_old):
        made, used = ids(new), ids(old)
        spread = spread_target(target(new))
        total = None
        for q in range(0, len(made) // COLS, 4):
            make_kernel(made, q, s_ref, spread, k_new)
            total = apply_kernel(used, q, x_ref, k_old, total)
        return summed(total)

    first = ids(0)
    spread = spread_target(target(0))
    for q in range(0, len(first) // COLS, 4):
        make_kernel(first, q, s_ref, spread, ka)

    def pair(i, _):
        if beside is not None:
            beside(i)
        lower = advance(2 * i + 1, kb, 2 * i, ka)
        upper = advance(jnp.minimum(2 * i + 2, count - 1), ka, 2 * i + 1, kb)
        out[:, pl.ds(pl.multiple_of(i * 128, 128), 128)] = two_targets(lower, upper)
        return 0

    lax.fori_loop(0, count // 2, pair, 0, unroll=unroll)


def two_targets(first, second):
    left = lanes(first[0].shape) < 64
    return (
        jnp.where(left, first[0], second[1]) + swap(jnp.where(left, second[0], first[1]))
    ) * (1.0 / log2e)


def one_target(pair):
    return (pair[0] + swap(pair[1])) * (1.0 / log2e)


HBM = pl.BlockSpec(memory_space=pl.ANY)


def call(kernel, name, out, in_specs, scratch=(), flops=0, data=0, limit=60, outs=None):
    return pl.pallas_call(
        kernel,
        name=name,
        out_shape=out,
        in_specs=in_specs,
        out_specs=jax.tree.map(lambda _: VM, out) if outs is None else outs,
        scratch_shapes=list(scratch),
        cost_estimate=pl.CostEstimate(flops=flops, bytes_accessed=data, transcendentals=0),
        compiler_params=pltpu.CompilerParams(vmem_limit_bytes=limit * 2**20),
    )


def shape(*dims, kind=f32):
    return jax.ShapeDtypeStruct(dims, kind)


def put_rows(skeleton, table):
    first = skeleton[:, :128]
    table[0] = twice(first, False)
    table[1] = twice(first, True)
    last = skeleton[:, 128:]
    table[2] = jnp.concatenate([last, last], axis=1)


def rows_of(table, at):
    return [table[j, pl.ds(at, 1), :] for j in range(3)]


def pair_rows(table, a, b):
    left = lanes((1, 128)) < 64
    return [jnp.where(left, x, y) for x, y in zip(rows_of(table, a), rows_of(table, b))]


PAIR_ROWS = (0, 3, 8, 11)
MIDDLE_ROWS = (6, 7, 14)


def pack_skeletons(
    sends, middle_sends, leaf_skeleton, middle_skeleton,
    out, leaf_table, middle_table, early, late, middles, lasts,
):
    put_rows(leaf_skeleton, leaf_table)
    put_rows(middle_skeleton, middle_table)

    def spot(l, _):
        tile = jnp.concatenate(rows_of(leaf_table, l) + [jnp.zeros((5, 128), f32)], axis=0)
        early[l] = tile
        late[l] = pltpu.roll(tile, 3, axis=0)
        return 0

    lax.fori_loop(0, 64, spot, 0, unroll=4)
    for m in range(8):
        x, y, z = rows_of(middle_table, m)
        middles[m] = jnp.concatenate([jnp.zeros((6, 128), f32), x, y], axis=0)
        lasts[m] = jnp.concatenate([jnp.zeros((6, 128), f32), z, jnp.zeros((1, 128), f32)], axis=0)
    left = lanes((8, 128)) < 64

    def body(b, _):
        slot = [sends[b * 8 + c] for c in range(8)]
        m, n = middle_sends[2 * b], middle_sends[2 * b + 1]
        for half, third in ((0, middles), (1, lasts)):
            c = 4 * half
            first = early[slot[c]] + late[slot[c + 2]] + third[m]
            second = early[slot[c + 1]] + late[slot[c + 3]] + third[n]
            out[b, 8 * half : 8 * half + 8] = jnp.where(left, first, second)
        return 0

    lax.fori_loop(0, 128, body, 0, unroll=4)


def take(x, index):
    pieces = [
        jnp.take_along_axis(x[r : r + 8], index, axis=1, mode="promise_in_bounds")
        for r in range(0, x.shape[0], 8)
    ]
    return pieces[0] if len(pieces) == 1 else jnp.concatenate(pieces, axis=0)


def even_first():
    i = lanes((8, 128))
    return (i & 64) + 2 * (i & 31) + ((i >> 5) & 1)


def evens_odds():
    i = lanes((8, 128))
    return ((i & 32) << 1) + 2 * (i & 31) + (i >> 6)


def evens_odds_back():
    i = lanes((8, 128))
    return ((i & 1) << 6) + ((i >> 6) << 5) + ((i & 63) >> 1)


def permute_columns(source, index, out, halved, tiles=(0, 32), shift=0):
    height = source.shape[0] // 8

    def body(j, _):
        where = jnp.broadcast_to(index[pl.ds(j, 1), :], (8, 128))
        if halved:
            where = take(where, even_first())
        inside = where & 127
        tile = where >> 7
        found = [jnp.zeros((8, 128), f32)] * height
        for i in range(32):
            match = tile == i
            for r in range(height):
                piece = source[8 * r : 8 * r + 8, 128 * i : 128 * i + 128]
                found[r] = jnp.where(match, take(piece, inside), found[r])
        for r in range(height):
            out[8 * r : 8 * r + 8, pl.ds(pl.multiple_of((j + shift) * 128, 128), 128)] = found[r]
        return 0

    lax.fori_loop(*tiles, body, 0, unroll=2)


def pair_halves(result):
    return result[:16] + swap(result[16:])


def as_tile(x):
    left = lanes((8, 128)) < 64
    return jnp.where(left, x[:8], swap(x[8:]))


def side_by_side(a, b):
    return jnp.where(lanes(a.shape) < 64, a, swap(b))


def even_odd_rows(blocks):
    left = lanes((16, 128)) < 64
    even, odd = [], []
    for v, w in zip(blocks[::2], blocks[1::2]):
        even.append(jnp.where(left, v, swap(w)))
        odd.append(jnp.where(left, swap(v), w))
    return jnp.concatenate([jnp.concatenate(even, axis=1), jnp.concatenate(odd, axis=1)], axis=0)


def pad_points(coords, source):
    source[0:3] = coords[...]
    source[3:8] = jnp.zeros((5, 4096), f32)


def tree_order(
    values, coords, order, basis, leaf_maps, middle_maps, root_maps,
    tree, first_leaves, last_leaves, basis_rows, leaf_rows, middle_rows, root_rows, source, sems,
):
    copies = []
    for m, (whole, rows) in enumerate(
        ((basis, basis_rows), (leaf_maps, leaf_rows), (middle_maps, middle_rows), (root_maps, root_rows))
    ):
        copies += [
            pltpu.make_async_copy(whole.at[:, pl.ds(128 * t, 128)], rows.at[:, t, :], sems.at[m, t])
            for t in range(32)
        ]
    for copy in copies:
        copy.start()
    pad_points(coords, source)
    permute_columns(values, order, tree, True)
    permute_columns(source, order, first_leaves.at[16:24], True, (0, 4))
    permute_columns(source, order, last_leaves.at[16:24], True, (28, 32), -28)
    first_leaves[0:16] = tree[:, :512]
    last_leaves[0:16] = tree[:, 3584:]
    for copy in copies:
        copy.wait()


def up_pass(
    sends, middle_sends, tree, root_skeleton, basis_rows, leaf_far, middle_rows, root_rows,
    out, upper_out, message, upper, split, tiles, middle_tiles, root_table, leaf_rows, sems,
):
    load = pltpu.make_async_copy(leaf_far, leaf_rows, sems.at[4])
    load.start()

    def leaf_pair(i, _):
        columns = pl.ds(pl.multiple_of(i * 128, 128), 128)
        x = tree[:, columns]
        a = pair_halves(dot3(jnp.concatenate([x[:, :32], x[:, 32:64]], axis=0), basis_rows[2 * i]))
        b = pair_halves(dot3(jnp.concatenate([x[:, 64:96], x[:, 96:]], axis=0), basis_rows[2 * i + 1]))
        split[:, columns] = take(side_by_side(a, b), evens_odds())
        tiles[2 * i] = as_tile(a)
        tiles[2 * i + 1] = as_tile(b)
        return 0

    lax.fori_loop(0, 32, leaf_pair, 0, unroll=4)

    def slots(b, _):
        for c in range(8):
            message[b, 8 * c : 8 * c + 8] = tiles[sends[8 * b + c]]
        return 0

    sent = []
    for p in range(4):
        lax.fori_loop(32 * p, 32 * p + 32, slots, 0, unroll=2)
        part = pl.ds(32 * p, 32)
        sent.append(pltpu.make_async_copy(message.at[part], out.at[part], sems.at[p]))
        sent[-1].start()
    load.wait()
    middles = []
    for j in range(8):
        blocks = [split[:, 512 * j + 128 * p : 512 * j + 128 * p + 128] for p in range(4)]
        part = pair_halves(dot3(even_odd_rows(blocks), leaf_rows[8 * j : 8 * j + 8].reshape(256, 128)))
        middle_tiles[j] = as_tile(part)
        middles.append(part)
    blocks = [take(side_by_side(middles[2 * p], middles[2 * p + 1]), evens_odds()) for p in range(4)]
    root = pair_halves(dot3(even_odd_rows(blocks), middle_rows[...].reshape(256, 128)))
    turned = take(root, evens_odds())
    top = pair_halves(dot3(jnp.concatenate([turned[:, :32], turned[:, 64:96]], axis=0), root_rows[0]))
    put_rows(root_skeleton, root_table)
    block = jnp.concatenate(
        [as_tile(root), as_tile(top)] + rows_of(root_table, 0) + [jnp.zeros((5, 128), f32)], axis=0
    )

    def middle_slots(b, _):
        for c in range(2):
            upper[b, 8 * c : 8 * c + 8] = middle_tiles[middle_sends[2 * b + c]]
        upper[b, 16:40] = block
        return 0

    lax.fori_loop(0, 128, middle_slots, 0, unroll=4)
    sent.append(pltpu.make_async_copy(upper, upper_out, sems.at[5]))
    sent[-1].start()
    for copy in sent:
        copy.wait()


def near_field(
    index, order_list, before, tree, after, coords, order, out, inverse, window, source, s_ref, x_ref, ka, kb
):
    window[:, :512] = before[...]
    window[0:16, 512:4608] = tree[...]
    window[:, 4608:] = after[...]
    pad_points(coords, source)
    permute_columns(source, order, window.at[16:24], True, (0, 32), 4)
    for k in range(8):
        s_ref[80 + k] = jnp.zeros((64, 128), bf16)
    x_ref[80] = jnp.zeros((2, 16, 128), bf16)

    def prepare(i, _):
        pairs = []
        for p in range(4):
            block = window[:, pl.ds(pl.multiple_of(i * 512 + p * 128, 128), 128)]
            pairs.append([block[16:17], block[17:18], block[18:19]])
            put_values(x_ref, 8 * i + 2 * p, twice(block[:16], False))
            put_values(x_ref, 8 * i + 2 * p + 1, twice(block[:16], True))
        source_eight(pairs, s_ref, 8 * i)
        return 0

    lax.fori_loop(0, 10, prepare, 0, unroll=2)

    def ids(l):
        return [l + 8] + [index[f, l] for f in range(26)] + [80]

    def target(l):
        block = window[16:24, pl.ds(pl.multiple_of((l >> 1) * 128 + 512, 128), 128)]
        left = lanes(block.shape) < 64
        points = jnp.where(left == (l % 2 == 0), block, swap(block))
        return target_features([points[0:1], points[1:2], points[2:3]])

    def invert(i):
        for l in (2 * i, 2 * i + 1):
            for p in range(64):
                inverse[order_list[l * 64 + p]] = l * 64 + (p % 2) * 32 + p // 2

    couple_all(64, ids, target, s_ref, x_ref, out, ka, kb, unroll=2, beside=invert)


def sources(received, s_ref, middle_ref):
    def prepare(q, _):
        block = received[q]
        source_eight([[block[r + j : r + j + 1] for j in range(3)] for r in PAIR_ROWS], s_ref, q * 8)
        return 0

    lax.fori_loop(0, 128, prepare, 0, unroll=4)

    def middle(q, _):
        source_eight(
            [[received[4 * q + p, r : r + 1] for r in MIDDLE_ROWS] for p in range(4)], middle_ref, q * 8
        )
        return 0

    lax.fori_loop(0, 32, middle, 0, unroll=4)


def far_ids(index):
    return lambda l: [index[l, f] for f in range(64)]


def far_leaves(index, skeleton, received, table, out, s_ref, tiles, x_ref, rows, ka, kb, sems):
    parts = [
        pltpu.make_async_copy(
            received.at[pl.ds(32 * p, 32)], tiles.at[pl.ds(32 * p, 32)], sems.at[p]
        )
        for p in range(4)
    ]
    for part in parts:
        part.start()
    loaded = pltpu.make_async_copy(table, s_ref, sems.at[4])
    loaded.start()
    put_rows(skeleton, rows)
    for p in range(4):
        parts[p].wait()

        def prepare(q, _):
            for c in range(8):
                put_values(x_ref, 8 * q + c, values_from_tile(tiles[q, 8 * c : 8 * c + 8]))
            return 0

        lax.fori_loop(32 * p, 32 * p + 32, prepare, 0, unroll=2)
    loaded.wait()
    couple_all(
        64, far_ids(index), lambda l: target_features(rows_of(rows, l)), s_ref, x_ref, out, ka, kb, 2
    )


def lifted(x, rows):
    left = lanes(x.shape) < 64
    zero = jnp.zeros_like(x)
    wide = jnp.concatenate([jnp.where(left, x, zero), jnp.where(left, zero, swap(x))], axis=0)
    return dot3(wide, rows, NT)


def natural(result, p):
    part = slice(64 * p, 64 * p + 64)
    return take(jnp.concatenate([result[:16, part], result[16:, part]], axis=1), evens_odds_back())


def finish(
    middle_index, root_index, received, middle_table_far, middle_skeleton, top_skeleton,
    near, far, basis_far, leaf_far, middle_rows, root_rows, inverse,
    out, far_middle, values, middle_table, roots, basis_rows, leaf_rows,
    x_ref, s_ref, ka, kb, middle_points, top_points, tree, sems,
):
    loads = [
        pltpu.make_async_copy(source, target, sems.at[i])
        for i, (source, target) in enumerate(
            (
                (received.at[pl.ds(0, 128), pl.ds(0, 16)], values),
                (middle_table_far, middle_table),
                (received.at[pl.ds(0, 128), pl.ds(16, 24)], roots),
                (leaf_far, leaf_rows),
                (basis_far, basis_rows),
            )
        )
    ]
    for load in loads:
        load.start()
    left = lanes((1, 128)) < 64
    put_rows(middle_skeleton, middle_points)
    put_rows(top_skeleton, top_points)
    group = lax.axis_index("gx")
    loads[0].wait()

    def middle_values(q, _):
        for c in range(2):
            put_values(x_ref, 2 * q + c, values_from_tile(values[q, 8 * c : 8 * c + 8]))
        return 0

    lax.fori_loop(0, 128, middle_values, 0, unroll=4)
    loads[1].wait()
    couple_all(
        8, far_ids(middle_index), lambda l: target_features(rows_of(middle_points, l)),
        middle_table, x_ref, far_middle, ka, kb,
    )
    loads[2].wait()

    def root_sources(q, _):
        pairs = []
        for p in range(4):
            a, b = roots[8 * q + 2 * p], roots[8 * q + 2 * p + 1]
            pairs.append([jnp.where(left, a[16 + j : 17 + j], b[16 + j : 17 + j]) for j in range(3)])
            put_values(x_ref, 8 * q + 2 * p, values_from_tile(a[:8]))
            put_values(x_ref, 8 * q + 2 * p + 1, values_from_tile(b[:8]))
        source_eight(pairs, s_ref, 8 * q)
        return 0

    lax.fori_loop(0, 16, root_sources, 0, unroll=4)
    for q in range(2):
        source_eight(
            [pair_rows(top_points, 8 * q + 2 * p, 8 * q + 2 * p + 1) for p in range(4)], s_ref, 128 + 8 * q
        )

    def parent(h, _):
        total = roots[8 * h][8:16]
        for n in range(1, 8):
            total = total + roots[8 * h + n][8:16]
        total = jnp.where(h == group, jnp.zeros_like(total), total)
        put_values(x_ref, 128 + h, values_from_tile(total))
        return 0

    lax.fori_loop(0, 16, parent, 0, unroll=4)
    own = roots[lax.axis_index(both)]
    far_root, top_far = couple(
        [
            (far_ids(root_index)(0), target_features([own[16:17], own[17:18], own[18:19]])),
            (list(range(128, 144)), target_features(rows_of(top_points, group))),
        ],
        s_ref,
        x_ref,
        (ka, kb),
    )
    loads[3].wait()
    loads[4].wait()

    raised = lifted(top_far, root_rows[0])
    gap = jnp.zeros((16, 32), f32)
    root = far_root + take(
        jnp.concatenate([raised[:16], gap, raised[16:], gap], axis=1), evens_odds_back()
    )
    raised = lifted(root, middle_rows[...].reshape(256, 128))
    for p in range(4):
        columns = slice(128 * p, 128 * p + 128)
        far_middle[:, columns] = far_middle[:, columns] + natural(raised, p)

    def one_middle(i, _):
        pair = far_middle[:, pl.ds(pl.multiple_of(i * 128, 128), 128)]
        for half in range(2):
            at = 16 * i + 8 * half
            raised = lifted(swap(pair) if half else pair, leaf_rows[pl.ds(at, 8)].reshape(256, 128))
            for p in range(4):
                columns = pl.ds(pl.multiple_of(i * 1024 + half * 512 + 128 * p, 128), 128)
                leaf = far[:, columns] + natural(raised, p)
                a = lifted(leaf, basis_rows[at + 2 * p])
                b = lifted(swap(leaf), basis_rows[at + 2 * p + 1])
                tree[:, columns] = near[:, columns] + jnp.concatenate([a[:16], a[16:], b[:16], b[16:]], axis=1)
        return 0

    lax.fori_loop(0, 4, one_middle, 0, unroll=2)
    permute_columns(tree, inverse, out, False)


def from_behind(block, distance):
    devices = range(lax.axis_size(both))
    return lax.ppermute(block, both, [(i - distance, i) for i in devices if i - distance in devices])


def exchange(x):
    return lax.all_to_all(x, both, split_axis=0, concat_axis=0, tiled=True)


def shards(
    values,
    coords,
    order,
    leaf_basis,
    leaf_transfer,
    middle_transfer,
    root_transfer,
    leaf_skeleton,
    middle_skeleton,
    root_skeleton,
    top_skeleton,
    leaf_far,
    middle_far,
    root_far,
    leaf_near,
    leaf_sends,
    middle_sends,
):
    order_rows = order.reshape(32, 128)
    tree, first_leaves, last_leaves, basis_rows, leaf_rows, middle_rows, root_rows = call(
        tree_order,
        "tree_order",
        (
            shape(16, 4096), shape(24, 512), shape(24, 512),
            shape(64, 32, 128), shape(64, 32, 128), shape(8, 32, 128), shape(1, 32, 128),
        ),
        [VM, VM, VM, HBM, HBM, HBM, HBM],
        [pltpu.VMEM((8, 4096), f32), pltpu.SemaphoreType.DMA((4, 32))],
        flops=4 * 10**9,
    )(values, coords, order_rows, leaf_basis, leaf_transfer, middle_transfer, root_transfer)
    before = from_behind(last_leaves, 1)
    after = from_behind(first_leaves, -1)
    packed = call(
        pack_skeletons,
        "pack_skeletons",
        shape(128, 16, 128),
        [SM, SM, VM, VM],
        [
            pltpu.VMEM((3, 64, 128), f32),
            pltpu.VMEM((3, 8, 128), f32),
            pltpu.VMEM((64, 8, 128), f32),
            pltpu.VMEM((64, 8, 128), f32),
            pltpu.VMEM((8, 8, 128), f32),
            pltpu.VMEM((8, 8, 128), f32),
        ],
    )(leaf_sends, middle_sends, leaf_skeleton, middle_skeleton)
    skeletons = exchange(packed)

    outgoing, upper = call(
        up_pass,
        "up_pass",
        (shape(128, 64, 128), shape(128, 40, 128)),
        [SM, SM, VM, VM, VM, HBM, VM, VM],
        [
            pltpu.VMEM((128, 64, 128), f32),
            pltpu.VMEM((128, 40, 128), f32),
            pltpu.VMEM((16, 4096), f32),
            pltpu.VMEM((64, 8, 128), f32),
            pltpu.VMEM((8, 8, 128), f32),
            pltpu.VMEM((3, 1, 128), f32),
            pltpu.VMEM((64, 32, 128), f32),
            pltpu.SemaphoreType.DMA((6,)),
        ],
        flops=8 * 10**9,
        outs=(HBM, HBM),
    )(leaf_sends, middle_sends, tree, root_skeleton, basis_rows, leaf_rows, middle_rows, root_rows)
    outgoing, before, after = lax.optimization_barrier((outgoing, before, after))
    received = exchange(outgoing)

    kernels = [pltpu.VMEM((2, 1024, 256), bf16)] * 2
    near, inverse = call(
        near_field,
        "near_field",
        (shape(16, 4096), shape(4096, kind=jnp.int32)),
        [SM, SM, VM, VM, VM, VM, VM],
        [
            pltpu.VMEM((24, 5120), f32),
            pltpu.VMEM((8, 4096), f32),
            pltpu.VMEM((88, 64, 128), bf16),
            pltpu.VMEM((81, 2, 16, 128), bf16),
            pltpu.VMEM((2, 448, 256), bf16),
            pltpu.VMEM((2, 448, 256), bf16),
        ],
        flops=22 * 10**9,
        outs=(VM, SM),
    )(leaf_near.T, order, before, tree, after, coords, order_rows)
    inverse = inverse.reshape(32, 128)
    upper, near = lax.optimization_barrier((upper, near))
    upper_received = exchange(upper)
    leaf_table, middle_table = call(
        sources,
        "sources",
        (shape(1024, 64, 128, kind=bf16), shape(256, 64, 128, kind=bf16)),
        [VM],
        flops=16 * 10**9,
    )(skeletons)
    far = call(
        far_leaves,
        "far_leaves",
        shape(16, 4096),
        [SM, VM, HBM, HBM],
        [
            pltpu.VMEM((1024, 64, 128), bf16),
            pltpu.VMEM((128, 64, 128), f32),
            pltpu.VMEM((1024, 2, 16, 128), bf16),
            pltpu.VMEM((3, 64, 128), f32),
            *kernels,
            pltpu.SemaphoreType.DMA((5,)),
        ],
        flops=50 * 10**9,
    )(leaf_far, leaf_skeleton, received, leaf_table)
    return call(
        finish,
        "finish",
        shape(16, 4096),
        [SM, SM, HBM, HBM, VM, VM, VM, VM, HBM, HBM, VM, VM, VM],
        [
            pltpu.VMEM((16, 512), f32),
            pltpu.VMEM((128, 16, 128), f32),
            pltpu.VMEM((256, 64, 128), bf16),
            pltpu.VMEM((128, 24, 128), f32),
            pltpu.VMEM((64, 32, 128), f32),
            pltpu.VMEM((64, 32, 128), f32),
            pltpu.VMEM((256, 2, 16, 128), bf16),
            pltpu.VMEM((144, 64, 128), bf16),
            *kernels,
            pltpu.VMEM((3, 8, 128), f32),
            pltpu.VMEM((3, 16, 128), f32),
            pltpu.VMEM((16, 4096), f32),
            pltpu.SemaphoreType.DMA((5,)),
        ],
        flops=10 * 10**9,
    )(
        middle_far, root_far, upper_received, middle_table, middle_skeleton, top_skeleton,
        near, far, basis_rows, leaf_rows, middle_rows, root_rows, inverse,
    )


def solution(mesh):
    split = P(both, None)
    placed = (
        P(None, both),
        P(None, both),
        P(both),
        split,
        split,
        split,
        split,
        split,
        split,
        split,
        P(),
        split,
        split,
        split,
        split,
        P(both),
        P(both),
    )
    return jax.shard_map(
        shards, mesh=mesh, in_specs=placed, out_specs=P(None, both), check_vma=False
    )
```

```python
import math

import jax
import jax.numpy as jnp
from jax import lax
from jax.experimental import pallas as pl
from jax.experimental.pallas import tpu as pltpu
from jax.sharding import PartitionSpec as P

LEAF = 64
RANK = 64
RHS = 16
FEATS = 32
COLS = 4

both = ("gx", "gy")
f32 = jnp.float32
bf16 = jnp.bfloat16
log2e = 1.0 / math.log(2.0)
scale = math.sqrt(3.0) / 0.3 * log2e

VM = pl.BlockSpec(memory_space=pltpu.VMEM)
SM = pl.BlockSpec(memory_space=pltpu.SMEM)


def lanes(shape):
    return lax.broadcasted_iota(jnp.int32, shape, len(shape) - 1)


def swap(x):
    return pltpu.roll(x, 64, axis=x.ndim - 1)


def halves(x):
    high = x.astype(bf16)
    return high, (x - high.astype(f32)).astype(bf16)


def thirds(x):
    first = x.astype(bf16).astype(f32)
    rest = x - first
    second = rest.astype(bf16).astype(f32)
    return first, second, (rest - second).astype(bf16).astype(f32)


NN = (((1,), (0,)), ((), ()))
NT = (((1,), (1,)), ((), ()))


def dot(a, b, dims=NN):
    return lax.dot_general(a, b, dims, preferred_element_type=f32)


def dot3(a, b, dims=NN):
    ah, al = halves(a)
    bh, bl = halves(b)
    rows = a.shape[0]
    first = dot(jnp.concatenate([ah, al], axis=0), bh, dims)
    return first[:rows] + first[rows:] + dot(ah, bl, dims)


def stacked(rows, norm_row, one_row, factor):
    x, y, z = [(jnp.broadcast_to(r, (8, 128)) - 0.5) * scale for r in rows]
    norm = x * x + y * y + z * z
    sub = lax.broadcasted_iota(jnp.int32, (8, 128), 0)
    out = jnp.where(sub < 2, x, jnp.where(sub < 4, y, z)) * factor
    out = jnp.where(sub == norm_row, norm, out)
    return jnp.where(sub == one_row, 1.0, out), sub


def target_features(rows):
    base, sub = stacked(rows, 6, 7, -2.0)
    first, second, third = thirds(base)
    even = sub % 2 == 0
    last = jnp.where(sub == 7, 1.0, jnp.where(even, third, second))
    return jnp.concatenate(
        [first, jnp.where(even, second, first), last, jnp.zeros_like(first)], axis=0
    ).astype(bf16)


def source_features(rows):
    base, sub = stacked(rows, 7, 6, 1.0)
    first, second, third = thirds(base)
    even = sub % 2 == 0
    norm = sub == 7
    return jnp.concatenate(
        [
            jnp.where(even | norm, first, second),
            jnp.where(even, first, jnp.where(norm, second, third)),
            jnp.where(even, first, jnp.where(norm, third, second)),
            jnp.zeros_like(first),
        ],
        axis=0,
    ).astype(bf16)


def source_row(v, column):
    return (v & -8) + ((v & 1) << 2) + ((column - (v >> 1)) & 3)


def source_eight(pairs, s_ref, at):
    tall = jnp.concatenate([source_features(rows) for rows in pairs], axis=0)
    eye = (lax.broadcasted_iota(jnp.int32, (128, 128), 0) == lanes((128, 128))).astype(f32).astype(bf16)
    turned = dot(eye, tall, NT)
    for k in range(COLS):
        moved = (turned if k == 0 else pltpu.roll(turned, FEATS * k, axis=1)).astype(bf16)
        s_ref[at + k] = moved[:64]
        s_ref[at + COLS + k] = moved[64:]


def put_values(x_ref, at, wide):
    high, low = halves(wide)
    x_ref[at, 0] = high
    x_ref[at, 1] = low


def values_from_tile(tile):
    left = lanes(tile.shape) < 64
    other = swap(tile)
    return jnp.concatenate([jnp.where(left, tile, other), jnp.where(left, other, tile)], axis=0)


def twice(rows, upper):
    left = lanes(rows.shape) < 64
    return jnp.where(left, swap(rows), rows) if upper else jnp.where(left, rows, swap(rows))


def make_kernel(ids, start, s_ref, spread, k_ref):
    stop = min(start + 4, len(ids) // COLS)
    group = lanes((64, 128)) // FEATS
    stack = []
    for g in range(start, stop):
        quad = ids[4 * g : 4 * g + 4]
        s = s_ref[source_row(quad[3], 3)]
        for c in (2, 1, 0):
            s = jnp.where(group <= c, s_ref[source_row(quad[c], c)], s)
        stack.append(s)
    square = jnp.maximum(dot(jnp.concatenate(stack, axis=0), spread), 1e-30)
    u = square * lax.rsqrt(square)
    high, low = halves((u + log2e) * jnp.exp2(-u))
    k_ref[0, 64 * start : 64 * stop] = high
    k_ref[1, 64 * start : 64 * stop] = low


def apply_kernel(ids, start, x_ref, k_ref, total):
    count = len(ids) // COLS
    stop = min(start + 4, count)
    near = lanes((16, 128)) < 64

    def joined(part):
        out = []
        for c in range(COLS):
            pieces = []
            for g in range(start, stop, 2):
                first = x_ref[ids[4 * g + c], part]
                if g + 1 < count:
                    pieces.append(jnp.where(near, first, x_ref[ids[4 * g + 4 + c], part]))
                else:
                    pieces.append(first[:, :64])
            out.append(jnp.concatenate(pieces, axis=1))
        return jnp.concatenate(out, axis=0)

    x_high, x_low = joined(0), joined(1)
    rows = slice(64 * start, 64 * stop)
    first = dot(jnp.concatenate([x_high, x_low], axis=0), k_ref[0, rows])
    second = dot(x_high, k_ref[1, rows])
    return (first, second) if total is None else (total[0] + first, total[1] + second)


def summed(total):
    rows = 16 * COLS
    whole = total[0][:rows] + total[0][rows:] + total[1]
    return whole[:16, :128] + whole[32:48, 128:], whole[16:32, :128] + whole[48:, 128:]


def spread_target(target):
    zero = jnp.zeros_like(target)
    left = lanes(target.shape) < 64
    lower = jnp.where(left, target, zero)
    upper = jnp.where(left, zero, target)
    return jnp.concatenate(
        [
            jnp.concatenate([lower, upper, zero, zero], axis=0),
            jnp.concatenate([zero, zero, lower, upper], axis=0),
        ],
        axis=1,
    )


def couple(parts, s_ref, x_ref, k_refs):
    for (ids, target), k_ref in zip(parts, k_refs):
        spread = spread_target(target)
        for q in range(0, len(ids) // COLS, 4):
            make_kernel(ids, q, s_ref, spread, k_ref)
    sums = []
    for (ids, _), k_ref in zip(parts, k_refs):
        total = None
        for q in range(0, len(ids) // COLS, 4):
            total = apply_kernel(ids, q, x_ref, k_ref, total)
        sums.append(one_target(summed(total)))
    return sums


def couple_all(count, ids, target, s_ref, x_ref, out, ka, kb, unroll=1, beside=None):
    def advance(new, k_new, old, k_old):
        made, used = ids(new), ids(old)
        spread = spread_target(target(new))
        total = None
        for q in range(0, len(made) // COLS, 4):
            make_kernel(made, q, s_ref, spread, k_new)
            total = apply_kernel(used, q, x_ref, k_old, total)
        return summed(total)

    first = ids(0)
    spread = spread_target(target(0))
    for q in range(0, len(first) // COLS, 4):
        make_kernel(first, q, s_ref, spread, ka)

    def pair(i, _):
        if beside is not None:
            beside(i)
        lower = advance(2 * i + 1, kb, 2 * i, ka)
        upper = advance(jnp.minimum(2 * i + 2, count - 1), ka, 2 * i + 1, kb)
        out[:, pl.ds(pl.multiple_of(i * 128, 128), 128)] = two_targets(lower, upper)
        return 0

    lax.fori_loop(0, count // 2, pair, 0, unroll=unroll)


def two_targets(first, second):
    left = lanes(first[0].shape) < 64
    return (
        jnp.where(left, first[0], second[1]) + swap(jnp.where(left, second[0], first[1]))
    ) * (1.0 / log2e)


def one_target(pair):
    return (pair[0] + swap(pair[1])) * (1.0 / log2e)


HBM = pl.BlockSpec(memory_space=pl.ANY)


def call(kernel, name, out, in_specs, scratch=(), flops=0, data=0, limit=60, outs=None):
    return pl.pallas_call(
        kernel,
        name=name,
        out_shape=out,
        in_specs=in_specs,
        out_specs=jax.tree.map(lambda _: VM, out) if outs is None else outs,
        scratch_shapes=list(scratch),
        cost_estimate=pl.CostEstimate(flops=flops, bytes_accessed=data, transcendentals=0),
        compiler_params=pltpu.CompilerParams(vmem_limit_bytes=limit * 2**20),
    )


def shape(*dims, kind=f32):
    return jax.ShapeDtypeStruct(dims, kind)


def put_rows(skeleton, table):
    first = skeleton[:, :128]
    table[0] = twice(first, False)
    table[1] = twice(first, True)
    last = skeleton[:, 128:]
    table[2] = jnp.concatenate([last, last], axis=1)


def rows_of(table, at):
    return [table[j, pl.ds(at, 1), :] for j in range(3)]


def pair_rows(table, a, b):
    left = lanes((1, 128)) < 64
    return [jnp.where(left, x, y) for x, y in zip(rows_of(table, a), rows_of(table, b))]


PAIR_ROWS = (0, 3, 8, 11)
MIDDLE_ROWS = (6, 7, 14)


def pack_skeletons(
    sends, middle_sends, leaf_skeleton, middle_skeleton,
    out, leaf_table, middle_table, early, late, middles, lasts,
):
    put_rows(leaf_skeleton, leaf_table)
    put_rows(middle_skeleton, middle_table)

    def spot(l, _):
        tile = jnp.concatenate(rows_of(leaf_table, l) + [jnp.zeros((5, 128), f32)], axis=0)
        early[l] = tile
        late[l] = pltpu.roll(tile, 3, axis=0)
        return 0

    lax.fori_loop(0, 64, spot, 0, unroll=4)
    for m in range(8):
        x, y, z = rows_of(middle_table, m)
        middles[m] = jnp.concatenate([jnp.zeros((6, 128), f32), x, y], axis=0)
        lasts[m] = jnp.concatenate([jnp.zeros((6, 128), f32), z, jnp.zeros((1, 128), f32)], axis=0)
    left = lanes((8, 128)) < 64

    def body(b, _):
        slot = [sends[b * 8 + c] for c in range(8)]
        m, n = middle_sends[2 * b], middle_sends[2 * b + 1]
        for half, third in ((0, middles), (1, lasts)):
            c = 4 * half
            first = early[slot[c]] + late[slot[c + 2]] + third[m]
            second = early[slot[c + 1]] + late[slot[c + 3]] + third[n]
            out[b, 8 * half : 8 * half + 8] = jnp.where(left, first, second)
        return 0

    lax.fori_loop(0, 128, body, 0, unroll=4)


def take(x, index):
    pieces = [
        jnp.take_along_axis(x[r : r + 8], index, axis=1, mode="promise_in_bounds")
        for r in range(0, x.shape[0], 8)
    ]
    return pieces[0] if len(pieces) == 1 else jnp.concatenate(pieces, axis=0)


def even_first():
    i = lanes((8, 128))
    return (i & 64) + 2 * (i & 31) + ((i >> 5) & 1)


def evens_odds():
    i = lanes((8, 128))
    return ((i & 32) << 1) + 2 * (i & 31) + (i >> 6)


def evens_odds_back():
    i = lanes((8, 128))
    return ((i & 1) << 6) + ((i >> 6) << 5) + ((i & 63) >> 1)


def permute_columns(source, index, out, halved, tiles=(0, 32), shift=0):
    height = source.shape[0] // 8

    def body(j, _):
        where = jnp.broadcast_to(index[pl.ds(j, 1), :], (8, 128))
        if halved:
            where = take(where, even_first())
        inside = where & 127
        tile = where >> 7
        found = [jnp.zeros((8, 128), f32)] * height
        for i in range(32):
            match = tile == i
            for r in range(height):
                piece = source[8 * r : 8 * r + 8, 128 * i : 128 * i + 128]
                found[r] = jnp.where(match, take(piece, inside), found[r])
        for r in range(height):
            out[8 * r : 8 * r + 8, pl.ds(pl.multiple_of((j + shift) * 128, 128), 128)] = found[r]
        return 0

    lax.fori_loop(*tiles, body, 0, unroll=2)


def pair_halves(result):
    return result[:16] + swap(result[16:])


def as_tile(x):
    left = lanes((8, 128)) < 64
    return jnp.where(left, x[:8], swap(x[8:]))


def side_by_side(a, b):
    return jnp.where(lanes(a.shape) < 64, a, swap(b))


def even_odd_rows(blocks):
    left = lanes((16, 128)) < 64
    even, odd = [], []
    for v, w in zip(blocks[::2], blocks[1::2]):
        even.append(jnp.where(left, v, swap(w)))
        odd.append(jnp.where(left, swap(v), w))
    return jnp.concatenate([jnp.concatenate(even, axis=1), jnp.concatenate(odd, axis=1)], axis=0)


def pad_points(coords, source):
    source[0:3] = coords[...]
    source[3:8] = jnp.zeros((5, 4096), f32)


def tree_order(
    values, coords, order, basis, leaf_maps, middle_maps, root_maps,
    tree, first_leaves, last_leaves, basis_rows, leaf_rows, middle_rows, root_rows, source, sems,
):
    copies = []
    for m, (whole, rows) in enumerate(
        ((basis, basis_rows), (leaf_maps, leaf_rows), (middle_maps, middle_rows), (root_maps, root_rows))
    ):
        copies += [
            pltpu.make_async_copy(whole.at[:, pl.ds(128 * t, 128)], rows.at[:, t, :], sems.at[m, t])
            for t in range(32)
        ]
    for copy in copies:
        copy.start()
    pad_points(coords, source)
    permute_columns(values, order, tree, True)
    permute_columns(source, order, first_leaves.at[16:24], True, (0, 4))
    permute_columns(source, order, last_leaves.at[16:24], True, (28, 32), -28)
    first_leaves[0:16] = tree[:, :512]
    last_leaves[0:16] = tree[:, 3584:]
    for copy in copies:
        copy.wait()


def up_pass(
    sends, middle_sends, tree, root_skeleton, basis_rows, leaf_far, middle_rows, root_rows,
    out, upper_out, message, upper, split, tiles, middle_tiles, root_table, leaf_rows, sems,
):
    load = pltpu.make_async_copy(leaf_far, leaf_rows, sems.at[4])
    load.start()

    def leaf_pair(i, _):
        columns = pl.ds(pl.multiple_of(i * 128, 128), 128)
        x = tree[:, columns]
        a = pair_halves(dot3(jnp.concatenate([x[:, :32], x[:, 32:64]], axis=0), basis_rows[2 * i]))
        b = pair_halves(dot3(jnp.concatenate([x[:, 64:96], x[:, 96:]], axis=0), basis_rows[2 * i + 1]))
        split[:, columns] = take(side_by_side(a, b), evens_odds())
        tiles[2 * i] = as_tile(a)
        tiles[2 * i + 1] = as_tile(b)
        return 0

    lax.fori_loop(0, 32, leaf_pair, 0, unroll=4)

    def slots(b, _):
        for c in range(8):
            message[b, 8 * c : 8 * c + 8] = tiles[sends[8 * b + c]]
        return 0

    sent = []
    for p in range(4):
        lax.fori_loop(32 * p, 32 * p + 32, slots, 0, unroll=2)
        part = pl.ds(32 * p, 32)
        sent.append(pltpu.make_async_copy(message.at[part], out.at[part], sems.at[p]))
        sent[-1].start()
    load.wait()
    middles = []
    for j in range(8):
        blocks = [split[:, 512 * j + 128 * p : 512 * j + 128 * p + 128] for p in range(4)]
        part = pair_halves(dot3(even_odd_rows(blocks), leaf_rows[8 * j : 8 * j + 8].reshape(256, 128)))
        middle_tiles[j] = as_tile(part)
        middles.append(part)
    blocks = [take(side_by_side(middles[2 * p], middles[2 * p + 1]), evens_odds()) for p in range(4)]
    root = pair_halves(dot3(even_odd_rows(blocks), middle_rows[...].reshape(256, 128)))
    turned = take(root, evens_odds())
    top = pair_halves(dot3(jnp.concatenate([turned[:, :32], turned[:, 64:96]], axis=0), root_rows[0]))
    put_rows(root_skeleton, root_table)
    block = jnp.concatenate(
        [as_tile(root), as_tile(top)] + rows_of(root_table, 0) + [jnp.zeros((5, 128), f32)], axis=0
    )

    def middle_slots(b, _):
        for c in range(2):
            upper[b, 8 * c : 8 * c + 8] = middle_tiles[middle_sends[2 * b + c]]
        upper[b, 16:40] = block
        return 0

    lax.fori_loop(0, 128, middle_slots, 0, unroll=4)
    sent.append(pltpu.make_async_copy(upper, upper_out, sems.at[5]))
    sent[-1].start()
    for copy in sent:
        copy.wait()


def near_field(
    index, before, tree, after, coords, order, out, window, source, s_ref, x_ref, ka, kb
):
    window[:, :512] = before[...]
    window[0:16, 512:4608] = tree[...]
    window[:, 4608:] = after[...]
    pad_points(coords, source)
    permute_columns(source, order, window.at[16:24], True, (0, 32), 4)
    for k in range(8):
        s_ref[80 + k] = jnp.zeros((64, 128), bf16)
    x_ref[80] = jnp.zeros((2, 16, 128), bf16)

    def prepare(i, _):
        pairs = []
        for p in range(4):
            block = window[:, pl.ds(pl.multiple_of(i * 512 + p * 128, 128), 128)]
            pairs.append([block[16:17], block[17:18], block[18:19]])
            put_values(x_ref, 8 * i + 2 * p, twice(block[:16], False))
            put_values(x_ref, 8 * i + 2 * p + 1, twice(block[:16], True))
        source_eight(pairs, s_ref, 8 * i)
        return 0

    lax.fori_loop(0, 10, prepare, 0, unroll=2)

    def ids(l):
        return [l + 8] + [index[f, l] for f in range(26)] + [80]

    def target(l):
        block = window[16:24, pl.ds(pl.multiple_of((l >> 1) * 128 + 512, 128), 128)]
        left = lanes(block.shape) < 64
        points = jnp.where(left == (l % 2 == 0), block, swap(block))
        return target_features([points[0:1], points[1:2], points[2:3]])

    couple_all(64, ids, target, s_ref, x_ref, out, ka, kb, unroll=2)


def sources(received, out, middle_out, s_ref, middle_ref, sems):
    def prepare(q, _):
        block = received[q]
        source_eight([[block[r + j : r + j + 1] for j in range(3)] for r in PAIR_ROWS], s_ref, q * 8)
        return 0

    def middle(q, _):
        source_eight(
            [[received[4 * q + p, r : r + 1] for r in MIDDLE_ROWS] for p in range(4)], middle_ref, q * 8
        )
        return 0

    sent = []
    for table, whole, body, count in ((s_ref, out, prepare, 8), (middle_ref, middle_out, middle, 2)):
        for p in range(count):
            lax.fori_loop(16 * p, 16 * p + 16, body, 0, unroll=4)
            part = pl.ds(128 * p, 128)
            sent.append(pltpu.make_async_copy(table.at[part], whole.at[part], sems.at[len(sent)]))
            sent[-1].start()
    for copy in sent:
        copy.wait()


def far_ids(index):
    return lambda l: [index[l, f] for f in range(64)]


def far_leaves(
    index, order_list, skeleton, received, table, out, inverse, s_ref, tiles, x_ref, rows, ka, kb, sems
):
    parts = [
        pltpu.make_async_copy(
            received.at[pl.ds(32 * p, 32)], tiles.at[pl.ds(32 * p, 32)], sems.at[p]
        )
        for p in range(4)
    ]
    for part in parts:
        part.start()
    loaded = pltpu.make_async_copy(table, s_ref, sems.at[4])
    loaded.start()
    put_rows(skeleton, rows)
    for p in range(4):
        parts[p].wait()

        def prepare(q, _):
            for c in range(8):
                put_values(x_ref, 8 * q + c, values_from_tile(tiles[q, 8 * c : 8 * c + 8]))
            return 0

        lax.fori_loop(32 * p, 32 * p + 32, prepare, 0, unroll=2)
    loaded.wait()

    def invert(i):
        for l in (2 * i, 2 * i + 1):
            for p in range(64):
                inverse[order_list[l * 64 + p]] = l * 64 + (p % 2) * 32 + p // 2

    couple_all(
        64, far_ids(index), lambda l: target_features(rows_of(rows, l)), s_ref, x_ref, out, ka, kb, 2, invert
    )


def lifted(x, rows):
    left = lanes(x.shape) < 64
    zero = jnp.zeros_like(x)
    wide = jnp.concatenate([jnp.where(left, x, zero), jnp.where(left, zero, swap(x))], axis=0)
    return dot3(wide, rows, NT)


def natural(result, p):
    part = slice(64 * p, 64 * p + 64)
    return take(jnp.concatenate([result[:16, part], result[16:, part]], axis=1), evens_odds_back())


def finish(
    middle_index, root_index, received, middle_table_far, middle_skeleton, top_skeleton,
    near, far, basis_far, leaf_far, middle_rows, root_rows, inverse,
    out, far_middle, values, middle_table, roots, basis_rows, leaf_rows,
    x_ref, s_ref, ka, kb, middle_points, top_points, tree, sems,
):
    loads = [
        pltpu.make_async_copy(source, target, sems.at[i])
        for i, (source, target) in enumerate(
            (
                (received.at[pl.ds(0, 128), pl.ds(0, 16)], values),
                (middle_table_far, middle_table),
                (received.at[pl.ds(0, 128), pl.ds(16, 24)], roots),
                (leaf_far, leaf_rows),
                (basis_far, basis_rows),
            )
        )
    ]
    for load in loads:
        load.start()
    left = lanes((1, 128)) < 64
    put_rows(middle_skeleton, middle_points)
    put_rows(top_skeleton, top_points)
    group = lax.axis_index("gx")
    loads[0].wait()

    def middle_values(q, _):
        for c in range(2):
            put_values(x_ref, 2 * q + c, values_from_tile(values[q, 8 * c : 8 * c + 8]))
        return 0

    lax.fori_loop(0, 128, middle_values, 0, unroll=4)
    loads[1].wait()
    couple_all(
        8, far_ids(middle_index), lambda l: target_features(rows_of(middle_points, l)),
        middle_table, x_ref, far_middle, ka, kb,
    )
    loads[2].wait()

    def root_sources(q, _):
        pairs = []
        for p in range(4):
            a, b = roots[8 * q + 2 * p], roots[8 * q + 2 * p + 1]
            pairs.append([jnp.where(left, a[16 + j : 17 + j], b[16 + j : 17 + j]) for j in range(3)])
            put_values(x_ref, 8 * q + 2 * p, values_from_tile(a[:8]))
            put_values(x_ref, 8 * q + 2 * p + 1, values_from_tile(b[:8]))
        source_eight(pairs, s_ref, 8 * q)
        return 0

    lax.fori_loop(0, 16, root_sources, 0, unroll=4)
    for q in range(2):
        source_eight(
            [pair_rows(top_points, 8 * q + 2 * p, 8 * q + 2 * p + 1) for p in range(4)], s_ref, 128 + 8 * q
        )

    def parent(h, _):
        total = roots[8 * h][8:16]
        for n in range(1, 8):
            total = total + roots[8 * h + n][8:16]
        total = jnp.where(h == group, jnp.zeros_like(total), total)
        put_values(x_ref, 128 + h, values_from_tile(total))
        return 0

    lax.fori_loop(0, 16, parent, 0, unroll=4)
    own = roots[lax.axis_index(both)]
    far_root, top_far = couple(
        [
            (far_ids(root_index)(0), target_features([own[16:17], own[17:18], own[18:19]])),
            (list(range(128, 144)), target_features(rows_of(top_points, group))),
        ],
        s_ref,
        x_ref,
        (ka, kb),
    )
    loads[3].wait()
    loads[4].wait()

    raised = lifted(top_far, root_rows[0])
    gap = jnp.zeros((16, 32), f32)
    root = far_root + take(
        jnp.concatenate([raised[:16], gap, raised[16:], gap], axis=1), evens_odds_back()
    )
    raised = lifted(root, middle_rows[...].reshape(256, 128))
    for p in range(4):
        columns = slice(128 * p, 128 * p + 128)
        far_middle[:, columns] = far_middle[:, columns] + natural(raised, p)

    def one_middle(i, _):
        pair = far_middle[:, pl.ds(pl.multiple_of(i * 128, 128), 128)]
        for half in range(2):
            at = 16 * i + 8 * half
            raised = lifted(swap(pair) if half else pair, leaf_rows[pl.ds(at, 8)].reshape(256, 128))
            for p in range(4):
                columns = pl.ds(pl.multiple_of(i * 1024 + half * 512 + 128 * p, 128), 128)
                leaf = far[:, columns] + natural(raised, p)
                a = lifted(leaf, basis_rows[at + 2 * p])
                b = lifted(swap(leaf), basis_rows[at + 2 * p + 1])
                tree[:, columns] = near[:, columns] + jnp.concatenate([a[:16], a[16:], b[:16], b[16:]], axis=1)
        return 0

    lax.fori_loop(0, 4, one_middle, 0, unroll=2)
    permute_columns(tree, inverse, out, False)


def from_behind(block, distance):
    devices = range(lax.axis_size(both))
    return lax.ppermute(block, both, [(i - distance, i) for i in devices if i - distance in devices])


def exchange(x):
    return lax.all_to_all(x, both, split_axis=0, concat_axis=0, tiled=True)


def shards(
    values,
    coords,
    order,
    leaf_basis,
    leaf_transfer,
    middle_transfer,
    root_transfer,
    leaf_skeleton,
    middle_skeleton,
    root_skeleton,
    top_skeleton,
    leaf_far,
    middle_far,
    root_far,
    leaf_near,
    leaf_sends,
    middle_sends,
):
    order_rows = order.reshape(32, 128)
    tree, first_leaves, last_leaves, basis_rows, leaf_rows, middle_rows, root_rows = call(
        tree_order,
        "tree_order",
        (
            shape(16, 4096), shape(24, 512), shape(24, 512),
            shape(64, 32, 128), shape(64, 32, 128), shape(8, 32, 128), shape(1, 32, 128),
        ),
        [VM, VM, VM, HBM, HBM, HBM, HBM],
        [pltpu.VMEM((8, 4096), f32), pltpu.SemaphoreType.DMA((4, 32))],
        flops=4 * 10**9,
    )(values, coords, order_rows, leaf_basis, leaf_transfer, middle_transfer, root_transfer)
    before = from_behind(last_leaves, 1)
    after = from_behind(first_leaves, -1)
    packed = call(
        pack_skeletons,
        "pack_skeletons",
        shape(128, 16, 128),
        [SM, SM, VM, VM],
        [
            pltpu.VMEM((3, 64, 128), f32),
            pltpu.VMEM((3, 8, 128), f32),
            pltpu.VMEM((64, 8, 128), f32),
            pltpu.VMEM((64, 8, 128), f32),
            pltpu.VMEM((8, 8, 128), f32),
            pltpu.VMEM((8, 8, 128), f32),
        ],
    )(leaf_sends, middle_sends, leaf_skeleton, middle_skeleton)
    skeletons = exchange(packed)

    outgoing, upper = call(
        up_pass,
        "up_pass",
        (shape(128, 64, 128), shape(128, 40, 128)),
        [SM, SM, VM, VM, VM, HBM, VM, VM],
        [
            pltpu.VMEM((128, 64, 128), f32),
            pltpu.VMEM((128, 40, 128), f32),
            pltpu.VMEM((16, 4096), f32),
            pltpu.VMEM((64, 8, 128), f32),
            pltpu.VMEM((8, 8, 128), f32),
            pltpu.VMEM((3, 1, 128), f32),
            pltpu.VMEM((64, 32, 128), f32),
            pltpu.SemaphoreType.DMA((6,)),
        ],
        flops=8 * 10**9,
        outs=(HBM, HBM),
    )(leaf_sends, middle_sends, tree, root_skeleton, basis_rows, leaf_rows, middle_rows, root_rows)
    outgoing, before, after = lax.optimization_barrier((outgoing, before, after))
    received = exchange(outgoing)

    kernels = [pltpu.VMEM((2, 1024, 256), bf16)] * 2
    near = call(
        near_field,
        "near_field",
        shape(16, 4096),
        [SM, VM, VM, VM, VM, VM],
        [
            pltpu.VMEM((24, 5120), f32),
            pltpu.VMEM((8, 4096), f32),
            pltpu.VMEM((88, 64, 128), bf16),
            pltpu.VMEM((81, 2, 16, 128), bf16),
            pltpu.VMEM((2, 448, 256), bf16),
            pltpu.VMEM((2, 448, 256), bf16),
        ],
        flops=22 * 10**9,
    )(leaf_near.T, before, tree, after, coords, order_rows)
    upper, near, skeletons = lax.optimization_barrier((upper, near, skeletons))
    upper_received = exchange(upper)
    leaf_table, middle_table = call(
        sources,
        "sources",
        (shape(1024, 64, 128, kind=bf16), shape(256, 64, 128, kind=bf16)),
        [VM],
        [
            pltpu.VMEM((1024, 64, 128), bf16),
            pltpu.VMEM((256, 64, 128), bf16),
            pltpu.SemaphoreType.DMA((10,)),
        ],
        flops=16 * 10**9,
        outs=(HBM, HBM),
    )(skeletons)
    far, inverse = call(
        far_leaves,
        "far_leaves",
        (shape(16, 4096), shape(4096, kind=jnp.int32)),
        [SM, SM, VM, HBM, HBM],
        [
            pltpu.VMEM((1024, 64, 128), bf16),
            pltpu.VMEM((128, 64, 128), f32),
            pltpu.VMEM((1024, 2, 16, 128), bf16),
            pltpu.VMEM((3, 64, 128), f32),
            *kernels,
            pltpu.SemaphoreType.DMA((5,)),
        ],
        flops=50 * 10**9,
        outs=(VM, SM),
    )(leaf_far, order, leaf_skeleton, received, leaf_table)
    inverse = inverse.reshape(32, 128)
    return call(
        finish,
        "finish",
        shape(16, 4096),
        [SM, SM, HBM, HBM, VM, VM, VM, VM, HBM, HBM, VM, VM, VM],
        [
            pltpu.VMEM((16, 512), f32),
            pltpu.VMEM((128, 16, 128), f32),
            pltpu.VMEM((256, 64, 128), bf16),
            pltpu.VMEM((128, 24, 128), f32),
            pltpu.VMEM((64, 32, 128), f32),
            pltpu.VMEM((64, 32, 128), f32),
            pltpu.VMEM((256, 2, 16, 128), bf16),
            pltpu.VMEM((144, 64, 128), bf16),
            *kernels,
            pltpu.VMEM((3, 8, 128), f32),
            pltpu.VMEM((3, 16, 128), f32),
            pltpu.VMEM((16, 4096), f32),
            pltpu.SemaphoreType.DMA((5,)),
        ],
        flops=10 * 10**9,
    )(
        middle_far, root_far, upper_received, middle_table, middle_skeleton, top_skeleton,
        near, far, basis_rows, leaf_rows, middle_rows, root_rows, inverse,
    )


def solution(mesh):
    split = P(both, None)
    placed = (
        P(None, both),
        P(None, both),
        P(both),
        split,
        split,
        split,
        split,
        split,
        split,
        split,
        P(),
        split,
        split,
        split,
        split,
        P(both),
        P(both),
    )
    return jax.shard_map(
        shards, mesh=mesh, in_specs=placed, out_specs=P(None, both), check_vma=False
    )
```

```python
import math

import jax
import jax.numpy as jnp
from jax import lax
from jax.experimental import pallas as pl
from jax.experimental.pallas import tpu as pltpu
from jax.sharding import PartitionSpec as P

LEAF = 64
RANK = 64
RHS = 16
FEATS = 32
COLS = 4

both = ("gx", "gy")
f32 = jnp.float32
bf16 = jnp.bfloat16
log2e = 1.0 / math.log(2.0)
scale = math.sqrt(3.0) / 0.3 * log2e

VM = pl.BlockSpec(memory_space=pltpu.VMEM)
SM = pl.BlockSpec(memory_space=pltpu.SMEM)


def lanes(shape):
    return lax.broadcasted_iota(jnp.int32, shape, len(shape) - 1)


def swap(x):
    return pltpu.roll(x, 64, axis=x.ndim - 1)


def halves(x):
    high = x.astype(bf16)
    return high, (x - high.astype(f32)).astype(bf16)


def thirds(x):
    first = x.astype(bf16).astype(f32)
    rest = x - first
    second = rest.astype(bf16).astype(f32)
    return first, second, (rest - second).astype(bf16).astype(f32)


NN = (((1,), (0,)), ((), ()))
NT = (((1,), (1,)), ((), ()))


def dot(a, b, dims=NN):
    return lax.dot_general(a, b, dims, preferred_element_type=f32)


def dot3(a, b, dims=NN):
    ah, al = halves(a)
    bh, bl = halves(b)
    rows = a.shape[0]
    first = dot(jnp.concatenate([ah, al], axis=0), bh, dims)
    return first[:rows] + first[rows:] + dot(ah, bl, dims)


def stacked(rows, norm_row, one_row, factor):
    x, y, z = [(jnp.broadcast_to(r, (8, 128)) - 0.5) * scale for r in rows]
    norm = x * x + y * y + z * z
    sub = lax.broadcasted_iota(jnp.int32, (8, 128), 0)
    out = jnp.where(sub < 2, x, jnp.where(sub < 4, y, z)) * factor
    out = jnp.where(sub == norm_row, norm, out)
    return jnp.where(sub == one_row, 1.0, out), sub


def target_features(rows):
    base, sub = stacked(rows, 6, 7, -2.0)
    first, second, third = thirds(base)
    even = sub % 2 == 0
    last = jnp.where(sub == 7, 1.0, jnp.where(even, third, second))
    return jnp.concatenate(
        [first, jnp.where(even, second, first), last, jnp.zeros_like(first)], axis=0
    ).astype(bf16)


def source_features(rows):
    base, sub = stacked(rows, 7, 6, 1.0)
    first, second, third = thirds(base)
    even = sub % 2 == 0
    norm = sub == 7
    return jnp.concatenate(
        [
            jnp.where(even | norm, first, second),
            jnp.where(even, first, jnp.where(norm, second, third)),
            jnp.where(even, first, jnp.where(norm, third, second)),
            jnp.zeros_like(first),
        ],
        axis=0,
    ).astype(bf16)


def source_row(v, column):
    return (v & -8) + ((v & 1) << 2) + ((column - (v >> 1)) & 3)


def source_eight(pairs, s_ref, at):
    tall = jnp.concatenate([source_features(rows) for rows in pairs], axis=0)
    eye = (lax.broadcasted_iota(jnp.int32, (128, 128), 0) == lanes((128, 128))).astype(f32).astype(bf16)
    turned = dot(eye, tall, NT)
    for k in range(COLS):
        moved = (turned if k == 0 else pltpu.roll(turned, FEATS * k, axis=1)).astype(bf16)
        s_ref[at + k] = moved[:64]
        s_ref[at + COLS + k] = moved[64:]


def put_values(x_ref, at, wide):
    high, low = halves(wide)
    x_ref[at, 0] = high
    x_ref[at, 1] = low


def values_from_tile(tile):
    left = lanes(tile.shape) < 64
    other = swap(tile)
    return jnp.concatenate([jnp.where(left, tile, other), jnp.where(left, other, tile)], axis=0)


def twice(rows, upper):
    left = lanes(rows.shape) < 64
    return jnp.where(left, swap(rows), rows) if upper else jnp.where(left, rows, swap(rows))


def make_kernel(ids, start, s_ref, spread, k_ref):
    stop = min(start + 4, len(ids) // COLS)
    group = lanes((64, 128)) // FEATS
    stack = []
    for g in range(start, stop):
        quad = ids[4 * g : 4 * g + 4]
        s = s_ref[source_row(quad[3], 3)]
        for c in (2, 1, 0):
            s = jnp.where(group <= c, s_ref[source_row(quad[c], c)], s)
        stack.append(s)
    square = jnp.maximum(dot(jnp.concatenate(stack, axis=0), spread), 1e-30)
    u = square * lax.rsqrt(square)
    high, low = halves((u + log2e) * jnp.exp2(-u))
    k_ref[0, 64 * start : 64 * stop] = high
    k_ref[1, 64 * start : 64 * stop] = low


def apply_kernel(ids, start, x_ref, k_ref, total):
    count = len(ids) // COLS
    stop = min(start + 4, count)
    near = lanes((16, 128)) < 64

    def joined(part):
        out = []
        for c in range(COLS):
            pieces = []
            for g in range(start, stop, 2):
                first = x_ref[ids[4 * g + c], part]
                if g + 1 < count:
                    pieces.append(jnp.where(near, first, x_ref[ids[4 * g + 4 + c], part]))
                else:
                    pieces.append(first[:, :64])
            out.append(jnp.concatenate(pieces, axis=1))
        return jnp.concatenate(out, axis=0)

    x_high, x_low = joined(0), joined(1)
    rows = slice(64 * start, 64 * stop)
    first = dot(jnp.concatenate([x_high, x_low], axis=0), k_ref[0, rows])
    second = dot(x_high, k_ref[1, rows])
    return (first, second) if total is None else (total[0] + first, total[1] + second)


def summed(total):
    rows = 16 * COLS
    whole = total[0][:rows] + total[0][rows:] + total[1]
    return whole[:16, :128] + whole[32:48, 128:], whole[16:32, :128] + whole[48:, 128:]


def spread_target(target):
    zero = jnp.zeros_like(target)
    left = lanes(target.shape) < 64
    lower = jnp.where(left, target, zero)
    upper = jnp.where(left, zero, target)
    return jnp.concatenate(
        [
            jnp.concatenate([lower, upper, zero, zero], axis=0),
            jnp.concatenate([zero, zero, lower, upper], axis=0),
        ],
        axis=1,
    )


def couple(parts, s_ref, x_ref, k_refs):
    for (ids, target), k_ref in zip(parts, k_refs):
        spread = spread_target(target)
        for q in range(0, len(ids) // COLS, 4):
            make_kernel(ids, q, s_ref, spread, k_ref)
    sums = []
    for (ids, _), k_ref in zip(parts, k_refs):
        total = None
        for q in range(0, len(ids) // COLS, 4):
            total = apply_kernel(ids, q, x_ref, k_ref, total)
        sums.append(one_target(summed(total)))
    return sums


def couple_all(count, ids, target, s_ref, x_ref, out, ka, kb, unroll=1, beside=None):
    def advance(new, k_new, old, k_old):
        made, used = ids(new), ids(old)
        spread = spread_target(target(new))
        total = None
        for q in range(0, len(made) // COLS, 4):
            make_kernel(made, q, s_ref, spread, k_new)
            total = apply_kernel(used, q, x_ref, k_old, total)
        return summed(total)

    first = ids(0)
    spread = spread_target(target(0))
    for q in range(0, len(first) // COLS, 4):
        make_kernel(first, q, s_ref, spread, ka)

    def pair(i, _):
        if beside is not None:
            beside(i)
        lower = advance(2 * i + 1, kb, 2 * i, ka)
        upper = advance(jnp.minimum(2 * i + 2, count - 1), ka, 2 * i + 1, kb)
        out[:, pl.ds(pl.multiple_of(i * 128, 128), 128)] = two_targets(lower, upper)
        return 0

    lax.fori_loop(0, count // 2, pair, 0, unroll=unroll)


def two_targets(first, second):
    left = lanes(first[0].shape) < 64
    return (
        jnp.where(left, first[0], second[1]) + swap(jnp.where(left, second[0], first[1]))
    ) * (1.0 / log2e)


def one_target(pair):
    return (pair[0] + swap(pair[1])) * (1.0 / log2e)


HBM = pl.BlockSpec(memory_space=pl.ANY)


def call(kernel, name, out, in_specs, scratch=(), flops=0, data=0, limit=60, outs=None):
    return pl.pallas_call(
        kernel,
        name=name,
        out_shape=out,
        in_specs=in_specs,
        out_specs=jax.tree.map(lambda _: VM, out) if outs is None else outs,
        scratch_shapes=list(scratch),
        cost_estimate=pl.CostEstimate(flops=flops, bytes_accessed=data, transcendentals=0),
        compiler_params=pltpu.CompilerParams(vmem_limit_bytes=limit * 2**20),
    )


def shape(*dims, kind=f32):
    return jax.ShapeDtypeStruct(dims, kind)


def put_rows(skeleton, table):
    first = skeleton[:, :128]
    table[0] = twice(first, False)
    table[1] = twice(first, True)
    last = skeleton[:, 128:]
    table[2] = jnp.concatenate([last, last], axis=1)


def rows_of(table, at):
    return [table[j, pl.ds(at, 1), :] for j in range(3)]


def pair_rows(table, a, b):
    left = lanes((1, 128)) < 64
    return [jnp.where(left, x, y) for x, y in zip(rows_of(table, a), rows_of(table, b))]


PAIR_ROWS = (0, 3, 8, 11)
MIDDLE_ROWS = (6, 7, 14)


def pack_skeletons(
    sends, middle_sends, leaf_skeleton, middle_skeleton,
    out, leaf_table, middle_table, early, late, middles, lasts,
):
    put_rows(leaf_skeleton, leaf_table)
    put_rows(middle_skeleton, middle_table)

    def spot(l, _):
        tile = jnp.concatenate(rows_of(leaf_table, l) + [jnp.zeros((5, 128), f32)], axis=0)
        early[l] = tile
        late[l] = pltpu.roll(tile, 3, axis=0)
        return 0

    lax.fori_loop(0, 64, spot, 0, unroll=4)
    for m in range(8):
        x, y, z = rows_of(middle_table, m)
        middles[m] = jnp.concatenate([jnp.zeros((6, 128), f32), x, y], axis=0)
        lasts[m] = jnp.concatenate([jnp.zeros((6, 128), f32), z, jnp.zeros((1, 128), f32)], axis=0)
    left = lanes((8, 128)) < 64

    def body(b, _):
        slot = [sends[b * 8 + c] for c in range(8)]
        m, n = middle_sends[2 * b], middle_sends[2 * b + 1]
        for half, third in ((0, middles), (1, lasts)):
            c = 4 * half
            first = early[slot[c]] + late[slot[c + 2]] + third[m]
            second = early[slot[c + 1]] + late[slot[c + 3]] + third[n]
            out[b, 8 * half : 8 * half + 8] = jnp.where(left, first, second)
        return 0

    lax.fori_loop(0, 128, body, 0, unroll=4)


def take(x, index):
    pieces = [
        jnp.take_along_axis(x[r : r + 8], index, axis=1, mode="promise_in_bounds")
        for r in range(0, x.shape[0], 8)
    ]
    return pieces[0] if len(pieces) == 1 else jnp.concatenate(pieces, axis=0)


def even_first():
    i = lanes((8, 128))
    return (i & 64) + 2 * (i & 31) + ((i >> 5) & 1)


def evens_odds():
    i = lanes((8, 128))
    return ((i & 32) << 1) + 2 * (i & 31) + (i >> 6)


def evens_odds_back():
    i = lanes((8, 128))
    return ((i & 1) << 6) + ((i >> 6) << 5) + ((i & 63) >> 1)


def permute_columns(source, index, out, halved, tiles=(0, 32), shift=0):
    height = source.shape[0] // 8

    def body(j, _):
        where = jnp.broadcast_to(index[pl.ds(j, 1), :], (8, 128))
        if halved:
            where = take(where, even_first())
        inside = where & 127
        tile = where >> 7
        found = [jnp.zeros((8, 128), f32)] * height
        for i in range(32):
            match = tile == i
            for r in range(height):
                piece = source[8 * r : 8 * r + 8, 128 * i : 128 * i + 128]
                found[r] = jnp.where(match, take(piece, inside), found[r])
        for r in range(height):
            out[8 * r : 8 * r + 8, pl.ds(pl.multiple_of((j + shift) * 128, 128), 128)] = found[r]
        return 0

    lax.fori_loop(*tiles, body, 0, unroll=2)


def pair_halves(result):
    return result[:16] + swap(result[16:])


def as_tile(x):
    left = lanes((8, 128)) < 64
    return jnp.where(left, x[:8], swap(x[8:]))


def side_by_side(a, b):
    return jnp.where(lanes(a.shape) < 64, a, swap(b))


def even_odd_rows(blocks):
    left = lanes((16, 128)) < 64
    even, odd = [], []
    for v, w in zip(blocks[::2], blocks[1::2]):
        even.append(jnp.where(left, v, swap(w)))
        odd.append(jnp.where(left, swap(v), w))
    return jnp.concatenate([jnp.concatenate(even, axis=1), jnp.concatenate(odd, axis=1)], axis=0)


def pad_points(coords, source):
    source[0:3] = coords[...]
    source[3:8] = jnp.zeros((5, 4096), f32)


def row_copies(whole, rows, sems):
    return [
        pltpu.make_async_copy(whole.at[:, pl.ds(128 * t, 128)], rows.at[:, t, :], sems.at[t])
        for t in range(32)
    ]


def tree_order(
    values, coords, order, basis, tree, first_leaves, last_leaves, basis_rows, source, sems
):
    copies = row_copies(basis, basis_rows, sems)
    for copy in copies:
        copy.start()
    pad_points(coords, source)
    permute_columns(values, order, tree, True)
    permute_columns(source, order, first_leaves.at[16:24], True, (0, 4))
    permute_columns(source, order, last_leaves.at[16:24], True, (28, 32), -28)
    first_leaves[0:16] = tree[:, :512]
    last_leaves[0:16] = tree[:, 3584:]
    for copy in copies:
        copy.wait()


def up_pass(
    sends, middle_sends, tree, root_skeleton, basis_rows, leaf_maps, middle_maps, root_maps,
    out, upper_out, leaf_rows, middle_rows, root_rows,
    message, upper, split, tiles, middle_tiles, root_table, sems, row_sems,
):
    copies = (
        row_copies(leaf_maps, leaf_rows, row_sems.at[0])
        + row_copies(middle_maps, middle_rows, row_sems.at[1])
        + row_copies(root_maps, root_rows, row_sems.at[2])
    )
    for copy in copies:
        copy.start()

    def leaf_pair(i, _):
        columns = pl.ds(pl.multiple_of(i * 128, 128), 128)
        x = tree[:, columns]
        a = pair_halves(dot3(jnp.concatenate([x[:, :32], x[:, 32:64]], axis=0), basis_rows[2 * i]))
        b = pair_halves(dot3(jnp.concatenate([x[:, 64:96], x[:, 96:]], axis=0), basis_rows[2 * i + 1]))
        split[:, columns] = take(side_by_side(a, b), evens_odds())
        tiles[2 * i] = as_tile(a)
        tiles[2 * i + 1] = as_tile(b)
        return 0

    lax.fori_loop(0, 32, leaf_pair, 0, unroll=4)

    def slots(b, _):
        for c in range(8):
            message[b, 8 * c : 8 * c + 8] = tiles[sends[8 * b + c]]
        return 0

    sent = []
    for p in range(4):
        lax.fori_loop(32 * p, 32 * p + 32, slots, 0, unroll=2)
        part = pl.ds(32 * p, 32)
        sent.append(pltpu.make_async_copy(message.at[part], out.at[part], sems.at[p]))
        sent[-1].start()
    for copy in copies:
        copy.wait()
    middles = []
    for j in range(8):
        blocks = [split[:, 512 * j + 128 * p : 512 * j + 128 * p + 128] for p in range(4)]
        part = pair_halves(dot3(even_odd_rows(blocks), leaf_rows[8 * j : 8 * j + 8].reshape(256, 128)))
        middle_tiles[j] = as_tile(part)
        middles.append(part)
    blocks = [take(side_by_side(middles[2 * p], middles[2 * p + 1]), evens_odds()) for p in range(4)]
    root = pair_halves(dot3(even_odd_rows(blocks), middle_rows[...].reshape(256, 128)))
    turned = take(root, evens_odds())
    top = pair_halves(dot3(jnp.concatenate([turned[:, :32], turned[:, 64:96]], axis=0), root_rows[0]))
    put_rows(root_skeleton, root_table)
    block = jnp.concatenate(
        [as_tile(root), as_tile(top)] + rows_of(root_table, 0) + [jnp.zeros((5, 128), f32)], axis=0
    )

    def middle_slots(b, _):
        for c in range(2):
            upper[b, 8 * c : 8 * c + 8] = middle_tiles[middle_sends[2 * b + c]]
        upper[b, 16:40] = block
        return 0

    lax.fori_loop(0, 128, middle_slots, 0, unroll=4)
    sent.append(pltpu.make_async_copy(upper, upper_out, sems.at[4]))
    sent[-1].start()
    for copy in sent:
        copy.wait()


def near_field(
    index, before, tree, after, coords, order, out, window, source, s_ref, x_ref, ka, kb
):
    window[:, :512] = before[...]
    window[0:16, 512:4608] = tree[...]
    window[:, 4608:] = after[...]
    pad_points(coords, source)
    permute_columns(source, order, window.at[16:24], True, (0, 32), 4)
    for k in range(8):
        s_ref[80 + k] = jnp.zeros((64, 128), bf16)
    x_ref[80] = jnp.zeros((2, 16, 128), bf16)

    def prepare(i, _):
        pairs = []
        for p in range(4):
            block = window[:, pl.ds(pl.multiple_of(i * 512 + p * 128, 128), 128)]
            pairs.append([block[16:17], block[17:18], block[18:19]])
            put_values(x_ref, 8 * i + 2 * p, twice(block[:16], False))
            put_values(x_ref, 8 * i + 2 * p + 1, twice(block[:16], True))
        source_eight(pairs, s_ref, 8 * i)
        return 0

    lax.fori_loop(0, 10, prepare, 0, unroll=2)

    def ids(l):
        return [l + 8] + [index[f, l] for f in range(26)] + [80]

    def target(l):
        block = window[16:24, pl.ds(pl.multiple_of((l >> 1) * 128 + 512, 128), 128)]
        left = lanes(block.shape) < 64
        points = jnp.where(left == (l % 2 == 0), block, swap(block))
        return target_features([points[0:1], points[1:2], points[2:3]])

    couple_all(64, ids, target, s_ref, x_ref, out, ka, kb, unroll=2)


def sources(received, out, middle_out, s_ref, middle_ref, sems):
    def prepare(q, _):
        block = received[q]
        source_eight([[block[r + j : r + j + 1] for j in range(3)] for r in PAIR_ROWS], s_ref, q * 8)
        return 0

    def middle(q, _):
        source_eight(
            [[received[4 * q + p, r : r + 1] for r in MIDDLE_ROWS] for p in range(4)], middle_ref, q * 8
        )
        return 0

    sent = []
    for table, whole, body, count in ((s_ref, out, prepare, 8), (middle_ref, middle_out, middle, 2)):
        for p in range(count):
            lax.fori_loop(16 * p, 16 * p + 16, body, 0, unroll=4)
            part = pl.ds(128 * p, 128)
            sent.append(pltpu.make_async_copy(table.at[part], whole.at[part], sems.at[len(sent)]))
            sent[-1].start()
    for copy in sent:
        copy.wait()


def far_ids(index):
    return lambda l: [index[l, f] for f in range(64)]


def far_leaves(
    index, order_list, skeleton, received, table, out, inverse, s_ref, tiles, x_ref, rows, ka, kb, sems
):
    parts = [
        pltpu.make_async_copy(
            received.at[pl.ds(32 * p, 32)], tiles.at[pl.ds(32 * p, 32)], sems.at[p]
        )
        for p in range(4)
    ]
    for part in parts:
        part.start()
    loaded = pltpu.make_async_copy(table, s_ref, sems.at[4])
    loaded.start()
    put_rows(skeleton, rows)
    for p in range(4):
        parts[p].wait()

        def prepare(q, _):
            for c in range(8):
                put_values(x_ref, 8 * q + c, values_from_tile(tiles[q, 8 * c : 8 * c + 8]))
            return 0

        lax.fori_loop(32 * p, 32 * p + 32, prepare, 0, unroll=2)
    loaded.wait()

    def invert(i):
        for l in (2 * i, 2 * i + 1):
            for p in range(64):
                inverse[order_list[l * 64 + p]] = l * 64 + (p % 2) * 32 + p // 2

    couple_all(
        64, far_ids(index), lambda l: target_features(rows_of(rows, l)), s_ref, x_ref, out, ka, kb, 2, invert
    )


def lifted(x, rows):
    left = lanes(x.shape) < 64
    zero = jnp.zeros_like(x)
    wide = jnp.concatenate([jnp.where(left, x, zero), jnp.where(left, zero, swap(x))], axis=0)
    return dot3(wide, rows, NT)


def natural(result, p):
    part = slice(64 * p, 64 * p + 64)
    return take(jnp.concatenate([result[:16, part], result[16:, part]], axis=1), evens_odds_back())


def finish(
    middle_index, root_index, received, middle_table_far, middle_skeleton, top_skeleton,
    near, far, basis_far, leaf_far, middle_rows, root_rows, inverse,
    out, far_middle, values, middle_table, roots, basis_rows, leaf_rows,
    x_ref, s_ref, ka, kb, middle_points, top_points, tree, sems,
):
    loads = [
        pltpu.make_async_copy(source, target, sems.at[i])
        for i, (source, target) in enumerate(
            (
                (received.at[pl.ds(0, 128), pl.ds(0, 16)], values),
                (middle_table_far, middle_table),
                (received.at[pl.ds(0, 128), pl.ds(16, 24)], roots),
                (leaf_far, leaf_rows),
                (basis_far, basis_rows),
            )
        )
    ]
    for load in loads:
        load.start()
    left = lanes((1, 128)) < 64
    put_rows(middle_skeleton, middle_points)
    put_rows(top_skeleton, top_points)
    group = lax.axis_index("gx")
    loads[0].wait()

    def middle_values(q, _):
        for c in range(2):
            put_values(x_ref, 2 * q + c, values_from_tile(values[q, 8 * c : 8 * c + 8]))
        return 0

    lax.fori_loop(0, 128, middle_values, 0, unroll=4)
    loads[1].wait()
    couple_all(
        8, far_ids(middle_index), lambda l: target_features(rows_of(middle_points, l)),
        middle_table, x_ref, far_middle, ka, kb,
    )
    loads[2].wait()

    def root_sources(q, _):
        pairs = []
        for p in range(4):
            a, b = roots[8 * q + 2 * p], roots[8 * q + 2 * p + 1]
            pairs.append([jnp.where(left, a[16 + j : 17 + j], b[16 + j : 17 + j]) for j in range(3)])
            put_values(x_ref, 8 * q + 2 * p, values_from_tile(a[:8]))
            put_values(x_ref, 8 * q + 2 * p + 1, values_from_tile(b[:8]))
        source_eight(pairs, s_ref, 8 * q)
        return 0

    lax.fori_loop(0, 16, root_sources, 0, unroll=4)
    for q in range(2):
        source_eight(
            [pair_rows(top_points, 8 * q + 2 * p, 8 * q + 2 * p + 1) for p in range(4)], s_ref, 128 + 8 * q
        )

    def parent(h, _):
        total = roots[8 * h][8:16]
        for n in range(1, 8):
            total = total + roots[8 * h + n][8:16]
        total = jnp.where(h == group, jnp.zeros_like(total), total)
        put_values(x_ref, 128 + h, values_from_tile(total))
        return 0

    lax.fori_loop(0, 16, parent, 0, unroll=4)
    own = roots[lax.axis_index(both)]
    far_root, top_far = couple(
        [
            (far_ids(root_index)(0), target_features([own[16:17], own[17:18], own[18:19]])),
            (list(range(128, 144)), target_features(rows_of(top_points, group))),
        ],
        s_ref,
        x_ref,
        (ka, kb),
    )
    loads[3].wait()
    loads[4].wait()

    raised = lifted(top_far, root_rows[0])
    gap = jnp.zeros((16, 32), f32)
    root = far_root + take(
        jnp.concatenate([raised[:16], gap, raised[16:], gap], axis=1), evens_odds_back()
    )
    raised = lifted(root, middle_rows[...].reshape(256, 128))
    for p in range(4):
        columns = slice(128 * p, 128 * p + 128)
        far_middle[:, columns] = far_middle[:, columns] + natural(raised, p)

    def one_middle(i, _):
        pair = far_middle[:, pl.ds(pl.multiple_of(i * 128, 128), 128)]
        for half in range(2):
            at = 16 * i + 8 * half
            raised = lifted(swap(pair) if half else pair, leaf_rows[pl.ds(at, 8)].reshape(256, 128))
            for p in range(4):
                columns = pl.ds(pl.multiple_of(i * 1024 + half * 512 + 128 * p, 128), 128)
                leaf = far[:, columns] + natural(raised, p)
                a = lifted(leaf, basis_rows[at + 2 * p])
                b = lifted(swap(leaf), basis_rows[at + 2 * p + 1])
                tree[:, columns] = near[:, columns] + jnp.concatenate([a[:16], a[16:], b[:16], b[16:]], axis=1)
        return 0

    lax.fori_loop(0, 4, one_middle, 0, unroll=2)
    permute_columns(tree, inverse, out, False)


def from_behind(block, distance):
    devices = range(lax.axis_size(both))
    return lax.ppermute(block, both, [(i - distance, i) for i in devices if i - distance in devices])


def exchange(x):
    return lax.all_to_all(x, both, split_axis=0, concat_axis=0, tiled=True)


def shards(
    values,
    coords,
    order,
    leaf_basis,
    leaf_transfer,
    middle_transfer,
    root_transfer,
    leaf_skeleton,
    middle_skeleton,
    root_skeleton,
    top_skeleton,
    leaf_far,
    middle_far,
    root_far,
    leaf_near,
    leaf_sends,
    middle_sends,
):
    order_rows = order.reshape(32, 128)
    tree, first_leaves, last_leaves, basis_rows = call(
        tree_order,
        "tree_order",
        (shape(16, 4096), shape(24, 512), shape(24, 512), shape(64, 32, 128)),
        [VM, VM, VM, HBM],
        [pltpu.VMEM((8, 4096), f32), pltpu.SemaphoreType.DMA((32,))],
        flops=4 * 10**9,
    )(values, coords, order_rows, leaf_basis)
    before = from_behind(last_leaves, 1)
    after = from_behind(first_leaves, -1)
    packed = call(
        pack_skeletons,
        "pack_skeletons",
        shape(128, 16, 128),
        [SM, SM, VM, VM],
        [
            pltpu.VMEM((3, 64, 128), f32),
            pltpu.VMEM((3, 8, 128), f32),
            pltpu.VMEM((64, 8, 128), f32),
            pltpu.VMEM((64, 8, 128), f32),
            pltpu.VMEM((8, 8, 128), f32),
            pltpu.VMEM((8, 8, 128), f32),
        ],
    )(leaf_sends, middle_sends, leaf_skeleton, middle_skeleton)
    skeletons = exchange(packed)

    outgoing, upper, leaf_rows, middle_rows, root_rows = call(
        up_pass,
        "up_pass",
        (
            shape(128, 64, 128), shape(128, 40, 128),
            shape(64, 32, 128), shape(8, 32, 128), shape(1, 32, 128),
        ),
        [SM, SM, VM, VM, VM, HBM, HBM, HBM],
        [
            pltpu.VMEM((128, 64, 128), f32),
            pltpu.VMEM((128, 40, 128), f32),
            pltpu.VMEM((16, 4096), f32),
            pltpu.VMEM((64, 8, 128), f32),
            pltpu.VMEM((8, 8, 128), f32),
            pltpu.VMEM((3, 1, 128), f32),
            pltpu.SemaphoreType.DMA((5,)),
            pltpu.SemaphoreType.DMA((3, 32)),
        ],
        flops=8 * 10**9,
        outs=(HBM, HBM, VM, VM, VM),
    )(
        leaf_sends, middle_sends, tree, root_skeleton, basis_rows,
        leaf_transfer, middle_transfer, root_transfer,
    )
    outgoing, before, after = lax.optimization_barrier((outgoing, before, after))
    received = exchange(outgoing)

    kernels = [pltpu.VMEM((2, 1024, 256), bf16)] * 2
    near = call(
        near_field,
        "near_field",
        shape(16, 4096),
        [SM, VM, VM, VM, VM, VM],
        [
            pltpu.VMEM((24, 5120), f32),
            pltpu.VMEM((8, 4096), f32),
            pltpu.VMEM((88, 64, 128), bf16),
            pltpu.VMEM((81, 2, 16, 128), bf16),
            pltpu.VMEM((2, 448, 256), bf16),
            pltpu.VMEM((2, 448, 256), bf16),
        ],
        flops=22 * 10**9,
    )(leaf_near.T, before, tree, after, coords, order_rows)
    upper, near = lax.optimization_barrier((upper, near))
    upper_received = exchange(upper)
    leaf_table, middle_table = call(
        sources,
        "sources",
        (shape(1024, 64, 128, kind=bf16), shape(256, 64, 128, kind=bf16)),
        [VM],
        [
            pltpu.VMEM((1024, 64, 128), bf16),
            pltpu.VMEM((256, 64, 128), bf16),
            pltpu.SemaphoreType.DMA((10,)),
        ],
        flops=16 * 10**9,
        outs=(HBM, HBM),
    )(skeletons)
    far, inverse = call(
        far_leaves,
        "far_leaves",
        (shape(16, 4096), shape(4096, kind=jnp.int32)),
        [SM, SM, VM, HBM, HBM],
        [
            pltpu.VMEM((1024, 64, 128), bf16),
            pltpu.VMEM((128, 64, 128), f32),
            pltpu.VMEM((1024, 2, 16, 128), bf16),
            pltpu.VMEM((3, 64, 128), f32),
            *kernels,
            pltpu.SemaphoreType.DMA((5,)),
        ],
        flops=50 * 10**9,
        outs=(VM, SM),
    )(leaf_far, order, leaf_skeleton, received, leaf_table)
    inverse = inverse.reshape(32, 128)
    return call(
        finish,
        "finish",
        shape(16, 4096),
        [SM, SM, HBM, HBM, VM, VM, VM, VM, HBM, HBM, VM, VM, VM],
        [
            pltpu.VMEM((16, 512), f32),
            pltpu.VMEM((128, 16, 128), f32),
            pltpu.VMEM((256, 64, 128), bf16),
            pltpu.VMEM((128, 24, 128), f32),
            pltpu.VMEM((64, 32, 128), f32),
            pltpu.VMEM((64, 32, 128), f32),
            pltpu.VMEM((256, 2, 16, 128), bf16),
            pltpu.VMEM((144, 64, 128), bf16),
            *kernels,
            pltpu.VMEM((3, 8, 128), f32),
            pltpu.VMEM((3, 16, 128), f32),
            pltpu.VMEM((16, 4096), f32),
            pltpu.SemaphoreType.DMA((5,)),
        ],
        flops=10 * 10**9,
        limit=36,
    )(
        middle_far, root_far, upper_received, middle_table, middle_skeleton, top_skeleton,
        near, far, basis_rows, leaf_rows, middle_rows, root_rows, inverse,
    )


def solution(mesh):
    split = P(both, None)
    placed = (
        P(None, both),
        P(None, both),
        P(both),
        split,
        split,
        split,
        split,
        split,
        split,
        split,
        P(),
        split,
        split,
        split,
        split,
        P(both),
        P(both),
    )
    return jax.shard_map(
        shards, mesh=mesh, in_specs=placed, out_specs=P(None, both), check_vma=False
    )
```

```python
import math

import jax
import jax.numpy as jnp
from jax import lax
from jax.experimental import pallas as pl
from jax.experimental.pallas import tpu as pltpu
from jax.sharding import PartitionSpec as P

LEAF = 64
RANK = 64
RHS = 16
FEATS = 32
COLS = 4

both = ("gx", "gy")
f32 = jnp.float32
bf16 = jnp.bfloat16
log2e = 1.0 / math.log(2.0)
scale = math.sqrt(3.0) / 0.3 * log2e

VM = pl.BlockSpec(memory_space=pltpu.VMEM)
SM = pl.BlockSpec(memory_space=pltpu.SMEM)


def lanes(shape):
    return lax.broadcasted_iota(jnp.int32, shape, len(shape) - 1)


def swap(x):
    return pltpu.roll(x, 64, axis=x.ndim - 1)


def halves(x):
    high = x.astype(bf16)
    return high, (x - high.astype(f32)).astype(bf16)


def thirds(x):
    first = x.astype(bf16).astype(f32)
    rest = x - first
    second = rest.astype(bf16).astype(f32)
    return first, second, (rest - second).astype(bf16).astype(f32)


NN = (((1,), (0,)), ((), ()))
NT = (((1,), (1,)), ((), ()))


def dot(a, b, dims=NN):
    return lax.dot_general(a, b, dims, preferred_element_type=f32)


def dot3(a, b, dims=NN):
    ah, al = halves(a)
    bh, bl = halves(b)
    rows = a.shape[0]
    first = dot(jnp.concatenate([ah, al], axis=0), bh, dims)
    return first[:rows] + first[rows:] + dot(ah, bl, dims)


def stacked(rows, norm_row, one_row, factor):
    x, y, z = [(jnp.broadcast_to(r, (8, 128)) - 0.5) * scale for r in rows]
    norm = x * x + y * y + z * z
    sub = lax.broadcasted_iota(jnp.int32, (8, 128), 0)
    out = jnp.where(sub < 2, x, jnp.where(sub < 4, y, z)) * factor
    out = jnp.where(sub == norm_row, norm, out)
    return jnp.where(sub == one_row, 1.0, out), sub


def target_features(rows):
    base, sub = stacked(rows, 6, 7, -2.0)
    first, second, third = thirds(base)
    even = sub % 2 == 0
    last = jnp.where(sub == 7, 1.0, jnp.where(even, third, second))
    return jnp.concatenate(
        [first, jnp.where(even, second, first), last, jnp.zeros_like(first)], axis=0
    ).astype(bf16)


def source_features(rows):
    base, sub = stacked(rows, 7, 6, 1.0)
    first, second, third = thirds(base)
    even = sub % 2 == 0
    norm = sub == 7
    return jnp.concatenate(
        [
            jnp.where(even | norm, first, second),
            jnp.where(even, first, jnp.where(norm, second, third)),
            jnp.where(even, first, jnp.where(norm, third, second)),
            jnp.zeros_like(first),
        ],
        axis=0,
    ).astype(bf16)


def source_row(v, column):
    return (v & -8) + ((v & 1) << 2) + ((column - (v >> 1)) & 3)


def source_eight(pairs, s_ref, at):
    tall = jnp.concatenate([source_features(rows) for rows in pairs], axis=0)
    eye = (lax.broadcasted_iota(jnp.int32, (128, 128), 0) == lanes((128, 128))).astype(f32).astype(bf16)
    turned = dot(eye, tall, NT)
    for k in range(COLS):
        moved = (turned if k == 0 else pltpu.roll(turned, FEATS * k, axis=1)).astype(bf16)
        s_ref[at + k] = moved[:64]
        s_ref[at + COLS + k] = moved[64:]


def put_values(x_ref, at, wide):
    high, low = halves(wide)
    x_ref[at, 0] = high
    x_ref[at, 1] = low


def values_from_tile(tile):
    left = lanes(tile.shape) < 64
    other = swap(tile)
    return jnp.concatenate([jnp.where(left, tile, other), jnp.where(left, other, tile)], axis=0)


def twice(rows, upper):
    left = lanes(rows.shape) < 64
    return jnp.where(left, swap(rows), rows) if upper else jnp.where(left, rows, swap(rows))


def make_kernel(ids, start, s_ref, spread, k_ref):
    stop = min(start + 4, len(ids) // COLS)
    group = lanes((64, 128)) // FEATS
    stack = []
    for g in range(start, stop):
        quad = ids[4 * g : 4 * g + 4]
        s = s_ref[source_row(quad[3], 3)]
        for c in (2, 1, 0):
            s = jnp.where(group <= c, s_ref[source_row(quad[c], c)], s)
        stack.append(s)
    square = jnp.maximum(dot(jnp.concatenate(stack, axis=0), spread), 1e-30)
    u = square * lax.rsqrt(square)
    high, low = halves((u + log2e) * jnp.exp2(-u))
    k_ref[0, 64 * start : 64 * stop] = high
    k_ref[1, 64 * start : 64 * stop] = low


def apply_kernel(ids, start, x_ref, k_ref, total):
    count = len(ids) // COLS
    stop = min(start + 4, count)
    near = lanes((16, 128)) < 64

    def joined(part):
        out = []
        for c in range(COLS):
            pieces = []
            for g in range(start, stop, 2):
                first = x_ref[ids[4 * g + c], part]
                if g + 1 < count:
                    pieces.append(jnp.where(near, first, x_ref[ids[4 * g + 4 + c], part]))
                else:
                    pieces.append(first[:, :64])
            out.append(jnp.concatenate(pieces, axis=1))
        return jnp.concatenate(out, axis=0)

    x_high, x_low = joined(0), joined(1)
    rows = slice(64 * start, 64 * stop)
    first = dot(jnp.concatenate([x_high, x_low], axis=0), k_ref[0, rows])
    second = dot(x_high, k_ref[1, rows])
    return (first, second) if total is None else (total[0] + first, total[1] + second)


def summed(total):
    rows = 16 * COLS
    whole = total[0][:rows] + total[0][rows:] + total[1]
    return whole[:16, :128] + whole[32:48, 128:], whole[16:32, :128] + whole[48:, 128:]


def spread_target(target):
    zero = jnp.zeros_like(target)
    left = lanes(target.shape) < 64
    lower = jnp.where(left, target, zero)
    upper = jnp.where(left, zero, target)
    return jnp.concatenate(
        [
            jnp.concatenate([lower, upper, zero, zero], axis=0),
            jnp.concatenate([zero, zero, lower, upper], axis=0),
        ],
        axis=1,
    )


def couple(parts, s_ref, x_ref, k_refs):
    for (ids, target), k_ref in zip(parts, k_refs):
        spread = spread_target(target)
        for q in range(0, len(ids) // COLS, 4):
            make_kernel(ids, q, s_ref, spread, k_ref)
    sums = []
    for (ids, _), k_ref in zip(parts, k_refs):
        total = None
        for q in range(0, len(ids) // COLS, 4):
            total = apply_kernel(ids, q, x_ref, k_ref, total)
        sums.append(one_target(summed(total)))
    return sums


def couple_all(count, ids, target, s_ref, x_ref, out, ka, kb, unroll=1, beside=None):
    def advance(new, k_new, old, k_old):
        made, used = ids(new), ids(old)
        spread = spread_target(target(new))
        total = None
        for q in range(0, len(made) // COLS, 4):
            make_kernel(made, q, s_ref, spread, k_new)
            total = apply_kernel(used, q, x_ref, k_old, total)
        return summed(total)

    first = ids(0)
    spread = spread_target(target(0))
    for q in range(0, len(first) // COLS, 4):
        make_kernel(first, q, s_ref, spread, ka)

    def pair(i, _):
        if beside is not None:
            beside(i)
        lower = advance(2 * i + 1, kb, 2 * i, ka)
        upper = advance(jnp.minimum(2 * i + 2, count - 1), ka, 2 * i + 1, kb)
        out[:, pl.ds(pl.multiple_of(i * 128, 128), 128)] = two_targets(lower, upper)
        return 0

    lax.fori_loop(0, count // 2, pair, 0, unroll=unroll)


def two_targets(first, second):
    left = lanes(first[0].shape) < 64
    return (
        jnp.where(left, first[0], second[1]) + swap(jnp.where(left, second[0], first[1]))
    ) * (1.0 / log2e)


def one_target(pair):
    return (pair[0] + swap(pair[1])) * (1.0 / log2e)


HBM = pl.BlockSpec(memory_space=pl.ANY)


def call(kernel, name, out, in_specs, scratch=(), flops=0, data=0, limit=60, outs=None):
    return pl.pallas_call(
        kernel,
        name=name,
        out_shape=out,
        in_specs=in_specs,
        out_specs=jax.tree.map(lambda _: VM, out) if outs is None else outs,
        scratch_shapes=list(scratch),
        cost_estimate=pl.CostEstimate(flops=flops, bytes_accessed=data, transcendentals=0),
        compiler_params=pltpu.CompilerParams(vmem_limit_bytes=limit * 2**20),
    )


def shape(*dims, kind=f32):
    return jax.ShapeDtypeStruct(dims, kind)


def put_rows(skeleton, table):
    first = skeleton[:, :128]
    table[0] = twice(first, False)
    table[1] = twice(first, True)
    last = skeleton[:, 128:]
    table[2] = jnp.concatenate([last, last], axis=1)


def rows_of(table, at):
    return [table[j, pl.ds(at, 1), :] for j in range(3)]


def pair_rows(table, a, b):
    left = lanes((1, 128)) < 64
    return [jnp.where(left, x, y) for x, y in zip(rows_of(table, a), rows_of(table, b))]


PAIR_ROWS = (0, 3, 8, 11)
MIDDLE_ROWS = (6, 7, 14)


def pack_skeletons(
    sends, middle_sends, leaf_skeleton, middle_skeleton,
    out, leaf_table, middle_table, early, late, middles, lasts,
):
    put_rows(leaf_skeleton, leaf_table)
    put_rows(middle_skeleton, middle_table)

    def spot(l, _):
        tile = jnp.concatenate(rows_of(leaf_table, l) + [jnp.zeros((5, 128), f32)], axis=0)
        early[l] = tile
        late[l] = pltpu.roll(tile, 3, axis=0)
        return 0

    lax.fori_loop(0, 64, spot, 0, unroll=4)
    for m in range(8):
        x, y, z = rows_of(middle_table, m)
        middles[m] = jnp.concatenate([jnp.zeros((6, 128), f32), x, y], axis=0)
        lasts[m] = jnp.concatenate([jnp.zeros((6, 128), f32), z, jnp.zeros((1, 128), f32)], axis=0)
    left = lanes((8, 128)) < 64

    def body(b, _):
        slot = [sends[b * 8 + c] for c in range(8)]
        m, n = middle_sends[2 * b], middle_sends[2 * b + 1]
        for half, third in ((0, middles), (1, lasts)):
            c = 4 * half
            first = early[slot[c]] + late[slot[c + 2]] + third[m]
            second = early[slot[c + 1]] + late[slot[c + 3]] + third[n]
            out[b, 8 * half : 8 * half + 8] = jnp.where(left, first, second)
        return 0

    lax.fori_loop(0, 128, body, 0, unroll=4)


def take(x, index):
    pieces = [
        jnp.take_along_axis(x[r : r + 8], index, axis=1, mode="promise_in_bounds")
        for r in range(0, x.shape[0], 8)
    ]
    return pieces[0] if len(pieces) == 1 else jnp.concatenate(pieces, axis=0)


def even_first():
    i = lanes((8, 128))
    return (i & 64) + 2 * (i & 31) + ((i >> 5) & 1)


def evens_odds():
    i = lanes((8, 128))
    return ((i & 32) << 1) + 2 * (i & 31) + (i >> 6)


def evens_odds_back():
    i = lanes((8, 128))
    return ((i & 1) << 6) + ((i >> 6) << 5) + ((i & 63) >> 1)


def permute_columns(source, index, out, halved, tiles=(0, 32), shift=0):
    height = source.shape[0] // 8

    def body(j, _):
        where = jnp.broadcast_to(index[pl.ds(j, 1), :], (8, 128))
        if halved:
            where = take(where, even_first())
        inside = where & 127
        tile = where >> 7
        found = [jnp.zeros((8, 128), f32)] * height
        for i in range(32):
            match = tile == i
            for r in range(height):
                piece = source[8 * r : 8 * r + 8, 128 * i : 128 * i + 128]
                found[r] = jnp.where(match, take(piece, inside), found[r])
        for r in range(height):
            out[8 * r : 8 * r + 8, pl.ds(pl.multiple_of((j + shift) * 128, 128), 128)] = found[r]
        return 0

    lax.fori_loop(*tiles, body, 0, unroll=2)


def pair_halves(result):
    return result[:16] + swap(result[16:])


def as_tile(x):
    left = lanes((8, 128)) < 64
    return jnp.where(left, x[:8], swap(x[8:]))


def side_by_side(a, b):
    return jnp.where(lanes(a.shape) < 64, a, swap(b))


def even_odd_rows(blocks):
    left = lanes((16, 128)) < 64
    even, odd = [], []
    for v, w in zip(blocks[::2], blocks[1::2]):
        even.append(jnp.where(left, v, swap(w)))
        odd.append(jnp.where(left, swap(v), w))
    return jnp.concatenate([jnp.concatenate(even, axis=1), jnp.concatenate(odd, axis=1)], axis=0)


def pad_points(coords, source):
    source[0:3] = coords[...]
    source[3:8] = jnp.zeros((5, 4096), f32)


def tree_order(
    values, coords, order, basis, leaf_maps, middle_maps, root_maps,
    tree, first_leaves, last_leaves, basis_rows, leaf_rows, middle_rows, root_rows, source, sems,
):
    copies = []
    for m, (whole, rows) in enumerate(
        ((basis, basis_rows), (leaf_maps, leaf_rows), (middle_maps, middle_rows), (root_maps, root_rows))
    ):
        copies += [
            pltpu.make_async_copy(whole.at[:, pl.ds(128 * t, 128)], rows.at[:, t, :], sems.at[m, t])
            for t in range(32)
        ]
    for copy in copies:
        copy.start()
    pad_points(coords, source)
    permute_columns(values, order, tree, True)
    permute_columns(source, order, first_leaves.at[16:24], True, (0, 4))
    permute_columns(source, order, last_leaves.at[16:24], True, (28, 32), -28)
    first_leaves[0:16] = tree[:, :512]
    last_leaves[0:16] = tree[:, 3584:]
    for copy in copies:
        copy.wait()


def up_pass(
    sends, middle_sends, tree, root_skeleton, basis_rows, leaf_far, middle_rows, root_rows,
    out, upper_out, message, upper, split, tiles, middle_tiles, root_table, leaf_rows, sems,
):
    load = pltpu.make_async_copy(leaf_far, leaf_rows, sems.at[4])
    load.start()

    def leaf_pair(i, _):
        columns = pl.ds(pl.multiple_of(i * 128, 128), 128)
        x = tree[:, columns]
        a = pair_halves(dot3(jnp.concatenate([x[:, :32], x[:, 32:64]], axis=0), basis_rows[2 * i]))
        b = pair_halves(dot3(jnp.concatenate([x[:, 64:96], x[:, 96:]], axis=0), basis_rows[2 * i + 1]))
        split[:, columns] = take(side_by_side(a, b), evens_odds())
        tiles[2 * i] = as_tile(a)
        tiles[2 * i + 1] = as_tile(b)
        return 0

    lax.fori_loop(0, 32, leaf_pair, 0, unroll=4)

    def slots(b, _):
        for c in range(8):
            message[b, 8 * c : 8 * c + 8] = tiles[sends[8 * b + c]]
        return 0

    sent = []
    for p in range(4):
        lax.fori_loop(32 * p, 32 * p + 32, slots, 0, unroll=2)
        part = pl.ds(32 * p, 32)
        sent.append(pltpu.make_async_copy(message.at[part], out.at[part], sems.at[p]))
        sent[-1].start()
    load.wait()
    middles = []
    for j in range(8):
        blocks = [split[:, 512 * j + 128 * p : 512 * j + 128 * p + 128] for p in range(4)]
        part = pair_halves(dot3(even_odd_rows(blocks), leaf_rows[8 * j : 8 * j + 8].reshape(256, 128)))
        middle_tiles[j] = as_tile(part)
        middles.append(part)
    blocks = [take(side_by_side(middles[2 * p], middles[2 * p + 1]), evens_odds()) for p in range(4)]
    root = pair_halves(dot3(even_odd_rows(blocks), middle_rows[...].reshape(256, 128)))
    turned = take(root, evens_odds())
    top = pair_halves(dot3(jnp.concatenate([turned[:, :32], turned[:, 64:96]], axis=0), root_rows[0]))
    put_rows(root_skeleton, root_table)
    block = jnp.concatenate(
        [as_tile(root), as_tile(top)] + rows_of(root_table, 0) + [jnp.zeros((5, 128), f32)], axis=0
    )

    def middle_slots(b, _):
        for c in range(2):
            upper[b, 8 * c : 8 * c + 8] = middle_tiles[middle_sends[2 * b + c]]
        upper[b, 16:40] = block
        return 0

    lax.fori_loop(0, 128, middle_slots, 0, unroll=4)
    sent.append(pltpu.make_async_copy(upper, upper_out, sems.at[5]))
    sent[-1].start()
    for copy in sent:
        copy.wait()


def near_field(
    index, before, tree, after, coords, order, out, window, source, s_ref, x_ref, ka, kb
):
    window[:, :512] = before[...]
    window[0:16, 512:4608] = tree[...]
    window[:, 4608:] = after[...]
    pad_points(coords, source)
    permute_columns(source, order, window.at[16:24], True, (0, 32), 4)
    for k in range(8):
        s_ref[80 + k] = jnp.zeros((64, 128), bf16)
    x_ref[80] = jnp.zeros((2, 16, 128), bf16)

    def prepare(i, _):
        pairs = []
        for p in range(4):
            block = window[:, pl.ds(pl.multiple_of(i * 512 + p * 128, 128), 128)]
            pairs.append([block[16:17], block[17:18], block[18:19]])
            put_values(x_ref, 8 * i + 2 * p, twice(block[:16], False))
            put_values(x_ref, 8 * i + 2 * p + 1, twice(block[:16], True))
        source_eight(pairs, s_ref, 8 * i)
        return 0

    lax.fori_loop(0, 10, prepare, 0, unroll=2)

    def ids(l):
        return [l + 8] + [index[f, l] for f in range(26)] + [80]

    def target(l):
        block = window[16:24, pl.ds(pl.multiple_of((l >> 1) * 128 + 512, 128), 128)]
        left = lanes(block.shape) < 64
        points = jnp.where(left == (l % 2 == 0), block, swap(block))
        return target_features([points[0:1], points[1:2], points[2:3]])

    couple_all(64, ids, target, s_ref, x_ref, out, ka, kb, unroll=2)


def sources(received, out, middle_out, s_ref, middle_ref, sems):
    def prepare(q, _):
        block = received[q]
        source_eight([[block[r + j : r + j + 1] for j in range(3)] for r in PAIR_ROWS], s_ref, q * 8)
        return 0

    def middle(q, _):
        source_eight(
            [[received[4 * q + p, r : r + 1] for r in MIDDLE_ROWS] for p in range(4)], middle_ref, q * 8
        )
        return 0

    sent = []
    for table, whole, body, count in ((s_ref, out, prepare, 8), (middle_ref, middle_out, middle, 2)):
        for p in range(count):
            lax.fori_loop(16 * p, 16 * p + 16, body, 0, unroll=4)
            part = pl.ds(128 * p, 128)
            sent.append(pltpu.make_async_copy(table.at[part], whole.at[part], sems.at[len(sent)]))
            sent[-1].start()
    for copy in sent:
        copy.wait()


def far_ids(index):
    return lambda l: [index[l, f] for f in range(64)]


def far_leaves(
    index, order_list, skeleton, received, table, out, inverse, s_ref, tiles, x_ref, rows, ka, kb, sems
):
    parts = [
        pltpu.make_async_copy(
            received.at[pl.ds(32 * p, 32)], tiles.at[pl.ds(32 * p, 32)], sems.at[p]
        )
        for p in range(4)
    ]
    for part in parts:
        part.start()
    loaded = pltpu.make_async_copy(table, s_ref, sems.at[4])
    loaded.start()
    put_rows(skeleton, rows)
    for p in range(4):
        parts[p].wait()

        def prepare(q, _):
            for c in range(8):
                put_values(x_ref, 8 * q + c, values_from_tile(tiles[q, 8 * c : 8 * c + 8]))
            return 0

        lax.fori_loop(32 * p, 32 * p + 32, prepare, 0, unroll=2)
    loaded.wait()

    def invert(i):
        for l in (2 * i, 2 * i + 1):
            for p in range(64):
                inverse[order_list[l * 64 + p]] = l * 64 + (p % 2) * 32 + p // 2

    couple_all(
        64, far_ids(index), lambda l: target_features(rows_of(rows, l)), s_ref, x_ref, out, ka, kb, 2, invert
    )


def lifted(x, rows):
    left = lanes(x.shape) < 64
    zero = jnp.zeros_like(x)
    wide = jnp.concatenate([jnp.where(left, x, zero), jnp.where(left, zero, swap(x))], axis=0)
    return dot3(wide, rows, NT)


def natural(result, p):
    part = slice(64 * p, 64 * p + 64)
    return take(jnp.concatenate([result[:16, part], result[16:, part]], axis=1), evens_odds_back())


def finish(
    middle_index, root_index, received, middle_table_far, middle_skeleton, top_skeleton,
    near, far, basis_far, leaf_far, middle_rows, root_rows, inverse,
    out, far_middle, values, middle_table, roots, basis_rows, leaf_rows,
    x_ref, s_ref, ka, kb, middle_points, top_points, tree, sems,
):
    loads = [
        pltpu.make_async_copy(source, target, sems.at[i])
        for i, (source, target) in enumerate(
            (
                (received.at[pl.ds(0, 128), pl.ds(0, 16)], values),
                (middle_table_far, middle_table),
                (received.at[pl.ds(0, 128), pl.ds(16, 24)], roots),
                (leaf_far, leaf_rows),
                (basis_far, basis_rows),
            )
        )
    ]
    for load in loads:
        load.start()
    left = lanes((1, 128)) < 64
    put_rows(middle_skeleton, middle_points)
    put_rows(top_skeleton, top_points)
    group = lax.axis_index("gx")
    loads[0].wait()

    def middle_values(q, _):
        for c in range(2):
            put_values(x_ref, 2 * q + c, values_from_tile(values[q, 8 * c : 8 * c + 8]))
        return 0

    lax.fori_loop(0, 128, middle_values, 0, unroll=4)
    loads[1].wait()
    couple_all(
        8, far_ids(middle_index), lambda l: target_features(rows_of(middle_points, l)),
        middle_table, x_ref, far_middle, ka, kb,
    )
    loads[2].wait()

    def root_sources(q, _):
        pairs = []
        for p in range(4):
            a, b = roots[8 * q + 2 * p], roots[8 * q + 2 * p + 1]
            pairs.append([jnp.where(left, a[16 + j : 17 + j], b[16 + j : 17 + j]) for j in range(3)])
            put_values(x_ref, 8 * q + 2 * p, values_from_tile(a[:8]))
            put_values(x_ref, 8 * q + 2 * p + 1, values_from_tile(b[:8]))
        source_eight(pairs, s_ref, 8 * q)
        return 0

    lax.fori_loop(0, 16, root_sources, 0, unroll=4)
    for q in range(2):
        source_eight(
            [pair_rows(top_points, 8 * q + 2 * p, 8 * q + 2 * p + 1) for p in range(4)], s_ref, 128 + 8 * q
        )

    def parent(h, _):
        total = roots[8 * h][8:16]
        for n in range(1, 8):
            total = total + roots[8 * h + n][8:16]
        total = jnp.where(h == group, jnp.zeros_like(total), total)
        put_values(x_ref, 128 + h, values_from_tile(total))
        return 0

    lax.fori_loop(0, 16, parent, 0, unroll=4)
    own = roots[lax.axis_index(both)]
    far_root, top_far = couple(
        [
            (far_ids(root_index)(0), target_features([own[16:17], own[17:18], own[18:19]])),
            (list(range(128, 144)), target_features(rows_of(top_points, group))),
        ],
        s_ref,
        x_ref,
        (ka, kb),
    )
    loads[3].wait()
    loads[4].wait()

    raised = lifted(top_far, root_rows[0])
    gap = jnp.zeros((16, 32), f32)
    root = far_root + take(
        jnp.concatenate([raised[:16], gap, raised[16:], gap], axis=1), evens_odds_back()
    )
    raised = lifted(root, middle_rows[...].reshape(256, 128))
    for p in range(4):
        columns = slice(128 * p, 128 * p + 128)
        far_middle[:, columns] = far_middle[:, columns] + natural(raised, p)

    def one_middle(i, _):
        pair = far_middle[:, pl.ds(pl.multiple_of(i * 128, 128), 128)]
        for half in range(2):
            at = 16 * i + 8 * half
            raised = lifted(swap(pair) if half else pair, leaf_rows[pl.ds(at, 8)].reshape(256, 128))
            for p in range(4):
                columns = pl.ds(pl.multiple_of(i * 1024 + half * 512 + 128 * p, 128), 128)
                leaf = far[:, columns] + natural(raised, p)
                a = lifted(leaf, basis_rows[at + 2 * p])
                b = lifted(swap(leaf), basis_rows[at + 2 * p + 1])
                tree[:, columns] = near[:, columns] + jnp.concatenate([a[:16], a[16:], b[:16], b[16:]], axis=1)
        return 0

    lax.fori_loop(0, 4, one_middle, 0, unroll=2)
    permute_columns(tree, inverse, out, False)


def from_behind(block, distance):
    devices = range(lax.axis_size(both))
    return lax.ppermute(block, both, [(i - distance, i) for i in devices if i - distance in devices])


def exchange(x):
    return lax.all_to_all(x, both, split_axis=0, concat_axis=0, tiled=True)


def shards(
    values,
    coords,
    order,
    leaf_basis,
    leaf_transfer,
    middle_transfer,
    root_transfer,
    leaf_skeleton,
    middle_skeleton,
    root_skeleton,
    top_skeleton,
    leaf_far,
    middle_far,
    root_far,
    leaf_near,
    leaf_sends,
    middle_sends,
):
    order_rows = order.reshape(32, 128)
    tree, first_leaves, last_leaves, basis_rows, leaf_rows, middle_rows, root_rows = call(
        tree_order,
        "tree_order",
        (
            shape(16, 4096), shape(24, 512), shape(24, 512),
            shape(64, 32, 128), shape(64, 32, 128), shape(8, 32, 128), shape(1, 32, 128),
        ),
        [VM, VM, VM, HBM, HBM, HBM, HBM],
        [pltpu.VMEM((8, 4096), f32), pltpu.SemaphoreType.DMA((4, 32))],
        flops=4 * 10**9,
    )(values, coords, order_rows, leaf_basis, leaf_transfer, middle_transfer, root_transfer)
    before = from_behind(last_leaves, 1)
    after = from_behind(first_leaves, -1)
    packed = call(
        pack_skeletons,
        "pack_skeletons",
        shape(128, 16, 128),
        [SM, SM, VM, VM],
        [
            pltpu.VMEM((3, 64, 128), f32),
            pltpu.VMEM((3, 8, 128), f32),
            pltpu.VMEM((64, 8, 128), f32),
            pltpu.VMEM((64, 8, 128), f32),
            pltpu.VMEM((8, 8, 128), f32),
            pltpu.VMEM((8, 8, 128), f32),
        ],
    )(leaf_sends, middle_sends, leaf_skeleton, middle_skeleton)
    skeletons = exchange(packed)

    outgoing, upper = call(
        up_pass,
        "up_pass",
        (shape(128, 64, 128), shape(128, 40, 128)),
        [SM, SM, VM, VM, VM, HBM, VM, VM],
        [
            pltpu.VMEM((128, 64, 128), f32),
            pltpu.VMEM((128, 40, 128), f32),
            pltpu.VMEM((16, 4096), f32),
            pltpu.VMEM((64, 8, 128), f32),
            pltpu.VMEM((8, 8, 128), f32),
            pltpu.VMEM((3, 1, 128), f32),
            pltpu.VMEM((64, 32, 128), f32),
            pltpu.SemaphoreType.DMA((6,)),
        ],
        flops=8 * 10**9,
        outs=(HBM, HBM),
    )(leaf_sends, middle_sends, tree, root_skeleton, basis_rows, leaf_rows, middle_rows, root_rows)
    outgoing, before, after = lax.optimization_barrier((outgoing, before, after))
    received = exchange(outgoing)

    kernels = [pltpu.VMEM((2, 1024, 256), bf16)] * 2
    near = call(
        near_field,
        "near_field",
        shape(16, 4096),
        [SM, VM, VM, VM, VM, VM],
        [
            pltpu.VMEM((24, 5120), f32),
            pltpu.VMEM((8, 4096), f32),
            pltpu.VMEM((88, 64, 128), bf16),
            pltpu.VMEM((81, 2, 16, 128), bf16),
            pltpu.VMEM((2, 448, 256), bf16),
            pltpu.VMEM((2, 448, 256), bf16),
        ],
        flops=22 * 10**9,
    )(leaf_near.T, before, tree, after, coords, order_rows)
    near, skeletons = lax.optimization_barrier((near, skeletons))
    leaf_table, middle_table = call(
        sources,
        "sources",
        (shape(1024, 64, 128, kind=bf16), shape(256, 64, 128, kind=bf16)),
        [VM],
        [
            pltpu.VMEM((1024, 64, 128), bf16),
            pltpu.VMEM((256, 64, 128), bf16),
            pltpu.SemaphoreType.DMA((10,)),
        ],
        flops=16 * 10**9,
        outs=(HBM, HBM),
    )(skeletons)
    upper, leaf_table = lax.optimization_barrier((upper, leaf_table))
    upper_received = exchange(upper)
    far, inverse = call(
        far_leaves,
        "far_leaves",
        (shape(16, 4096), shape(4096, kind=jnp.int32)),
        [SM, SM, VM, HBM, HBM],
        [
            pltpu.VMEM((1024, 64, 128), bf16),
            pltpu.VMEM((128, 64, 128), f32),
            pltpu.VMEM((1024, 2, 16, 128), bf16),
            pltpu.VMEM((3, 64, 128), f32),
            *kernels,
            pltpu.SemaphoreType.DMA((5,)),
        ],
        flops=10**9,
        outs=(VM, SM),
    )(leaf_far, order, leaf_skeleton, received, leaf_table)
    inverse = inverse.reshape(32, 128)
    return call(
        finish,
        "finish",
        shape(16, 4096),
        [SM, SM, HBM, HBM, VM, VM, VM, VM, HBM, HBM, VM, VM, VM],
        [
            pltpu.VMEM((16, 512), f32),
            pltpu.VMEM((128, 16, 128), f32),
            pltpu.VMEM((256, 64, 128), bf16),
            pltpu.VMEM((128, 24, 128), f32),
            pltpu.VMEM((64, 32, 128), f32),
            pltpu.VMEM((64, 32, 128), f32),
            pltpu.VMEM((256, 2, 16, 128), bf16),
            pltpu.VMEM((144, 64, 128), bf16),
            *kernels,
            pltpu.VMEM((3, 8, 128), f32),
            pltpu.VMEM((3, 16, 128), f32),
            pltpu.VMEM((16, 4096), f32),
            pltpu.SemaphoreType.DMA((5,)),
        ],
        flops=10 * 10**9,
    )(
        middle_far, root_far, upper_received, middle_table, middle_skeleton, top_skeleton,
        near, far, basis_rows, leaf_rows, middle_rows, root_rows, inverse,
    )


def solution(mesh):
    split = P(both, None)
    placed = (
        P(None, both),
        P(None, both),
        P(both),
        split,
        split,
        split,
        split,
        split,
        split,
        split,
        P(),
        split,
        split,
        split,
        split,
        P(both),
        P(both),
    )
    return jax.shard_map(
        shards, mesh=mesh, in_specs=placed, out_specs=P(None, both), check_vma=False
    )
```
